32 devices in a mesh: dp: 4 (over x, core), fsdp: 8 (over z, y).
Axes of the slice: x: 2, y: 2, z: 4, core: 2. Of those that a mesh axis runs over, the one named last changes fastest.
Arguments:
- hidden_in: bfloat16 [32, 544, 768], P(('dp', 'fsdp')), may hold values from -6 to 6
- out_grad: bfloat16 [32, 544, 768], P(('dp', 'fsdp')), may hold values from -6 to 6
- passage_len: int32 [32], P(('dp', 'fsdp')), may hold values from 128 to 512
- query_len: int32 [32], P(('dp', 'fsdp')), may hold values from 8 to 32
- prefix_units: int32 [32, 2], P(('dp', 'fsdp')), may hold values from 1 to 12
- qkv_weight: bfloat16 [2, 2304, 768], P(None, ('dp', 'fsdp')), may hold values from -0.21875 to 0.21875
- attn_weight: bfloat16 [2, 768, 768], P(None, ('dp', 'fsdp')), may hold values from -0.875 to 0.875
- in_weight: bfloat16 [2, 3072, 768], P(None, ('dp', 'fsdp')), may hold values from -0.21875 to 0.21875
- down_weight: bfloat16 [2, 768, 3072], P(None, ('dp', 'fsdp')), may hold values from -0.109375 to 0.109375
- norm_gains: bfloat16 [2, 2, 768], P(None, None, ('dp', 'fsdp')), may hold values from 0.5 to 1.5
- bias_rows: bfloat16 [2, 6, 768], P(None, None, ('dp', 'fsdp')), may hold values from -1 to 1
- in_bias: bfloat16 [2, 3072], P(None, ('dp', 'fsdp')), may hold values from -1 to 1
Outputs:
- activations: bfloat16 [32, 544, 768], P(('dp', 'fsdp'))
- pooled: float32 [32, 2, 2, 768], P(('dp', 'fsdp'))
- input_grad: bfloat16 [32, 544, 768], P(('dp', 'fsdp'))
- grad_qkv: float32 [2, 2304, 768], P(None, ('dp', 'fsdp'))
- grad_attn: float32 [2, 768, 768], P(None, ('dp', 'fsdp'))
- grad_in: float32 [2, 3072, 768], P(None, ('dp', 'fsdp'))
- grad_down: float32 [2, 768, 3072], P(None, ('dp', 'fsdp'))
- grad_gains: float32 [2, 2, 768], P(None, None, ('dp', 'fsdp'))
- grad_biases: float32 [2, 6, 768], P(None, None, ('dp', 'fsdp'))
- grad_in_bias: float32 [2, 3072], P(None, ('dp', 'fsdp'))
The draws below stay inside these ranges and needn't reach their ends.
All inputs are finite; a program needn't handle non-finite values.
Results may differ from the reference program's by a relative error of at most 0.024.
Values may be sent and summed in bfloat16 or wider, within the bound.
A program may use at most 256 MiB of HBM per device.

```python
import jax
import jax.numpy as jnp
from jax import lax

D = 768
HEADS = 12
HEAD_DIM = 64
FF = 3072
LP = 512
LQ = 32
S = 544
PAIRS = 32


def place_ends(entries, own_key, least, top_value):
    longest = entries.shape.index(max(entries.shape))
    spots = []
    for shift in (0, 1):
        where = [jax.random.randint(jax.random.fold_in(own_key, axis), (), 0, length) for axis, length in enumerate(entries.shape)]
        where[longest] = (where[longest] + shift) % entries.shape[longest]
        spots.append(tuple(where))
    return entries.at[spots[0]].set(least).at[spots[1]].set(top_value)


def with_spikes(values, key, source, target, parts, factor):
    def block_of(dim):
        return (jnp.arange(values.shape[dim]) // (values.shape[dim] // parts)).reshape((-1,) + (1,) * (values.ndim - 1 - dim))

    one_side = jax.random.permutation(key, parts)[block_of(target)]
    far = (block_of(target) + parts // 2) % parts
    return jnp.where((block_of(source) == one_side) | (block_of(source) == far), factor * values, values)


def steps_of(own_key, shape, pieces, low, largest):
    factor_of, own = 1.0, jax.random.fold_in(own_key, 6)
    for axis_at, blocks in pieces:
        draws = jnp.exp(jax.random.uniform(jax.random.fold_in(own, axis_at), (blocks,), jnp.float32, low / len(pieces), largest / len(pieces)))
        factor_of = factor_of * jnp.repeat(draws, shape[axis_at] // blocks).reshape([-1 if axis == axis_at else 1 for axis in range(len(shape))])
    return factor_of


def centred(key, extent, scale, bound, shards=(), kind=jnp.bfloat16):
    values = jax.random.normal(key, extent, jnp.float32) * scale
    if len(shards) > 0:
        values = steps_of(key, extent, shards, -0.22, 0.18) * values
    return jnp.clip(values, min=-bound, max=bound).astype(kind)


def heavy_noise(key, dims, scale, most, pieces, heavy, dtype=jnp.bfloat16):
    drawn = scale * jax.random.normal(key, dims, jnp.float32)
    if pieces:
        drawn = drawn * steps_of(key, dims, pieces, -0.22, 0.18)
    return jnp.clip(with_spikes(drawn, jax.random.fold_in(key, 3), *heavy), -most, most).astype(dtype)


def setup_inputs(seed: int = 0) -> dict:
    seeds = jax.random.split(jax.random.key(seed), 13)
    return {
        "hidden_in": centred(seeds[0], (PAIRS, S, D), 1.0, 6.0, ((0, 32),)),
        "out_grad": heavy_noise(seeds[1], (PAIRS, S, D), 1.0, 6.0, ((0, 32),), (0, 2, 32, 2.75)),
        "passage_len": place_ends(jax.random.randint(seeds[2], (PAIRS,), LP // 4, LP + 1), jax.random.fold_in(seeds[2], 1), LP // 4, LP).astype(jnp.int32),
        "query_len": place_ends(jax.random.randint(seeds[3], (PAIRS,), LQ // 4, LQ + 1), jax.random.fold_in(seeds[3], 1), LQ // 4, LQ).astype(jnp.int32),
        "prefix_units": place_ends(jax.random.randint(seeds[4], (PAIRS, 2), 1, D // 64 + 1), jax.random.fold_in(seeds[4], 1), 1, (D // 64 + 1) - 1).astype(jnp.int32),
        "qkv_weight": centred(seeds[5], (2, 3 * D, D), D ** -0.5, 0.21875, ((1, 32),)),
        "attn_weight": centred(seeds[6], (2, D, D), (D // 16) ** -0.5, 0.875, ((1, 32),)),
        "in_weight": centred(seeds[7], (2, FF, D), D ** -0.5, 0.21875, ((1, 32),)),
        "down_weight": centred(seeds[8], (2, D, FF), FF ** -0.5, 0.109375, ((1, 32),)),
        "norm_gains": jnp.clip(1.0 + 0.1 * jax.random.normal(seeds[9], (2, 2, D), jnp.float32), 0.5, 1.5).astype(jnp.bfloat16),
        "bias_rows": centred(seeds[10], (2, 6, D), 0.2, 1.0, ((2, 32),)),
        "in_bias": centred(seeds[11], (2, FF), 0.2, 1.0, ((1, 32),)),
    }


ln_eps = 1e-12
neg_big = -1e+30
prefix_step = 64

@jax.custom_vjp
def low(v):
    return lax.optimization_barrier(v.astype(jnp.bfloat16)).astype(jnp.float32)

@jax.custom_vjp
def low_back(v):
    return v

def low_keep(v):
    return (low(v), None)

def low_pass(kept, grad):
    return (grad,)

def back_keep(v):
    return (v, None)

def back_low(kept, grad):
    return (low(grad),)
low.defvjp(low_keep, low_pass)
low_back.defvjp(back_keep, back_low)

def matmul_t(left, right):
    return jnp.dot(left, right.T, precision=lax.Precision.HIGHEST, preferred_element_type=jnp.float32)

def layer_norm(values, gain_row, shift_row):
    center = values - lax.optimization_barrier(jnp.mean(values, -1, keepdims=True))
    return center * lax.rsqrt(lax.optimization_barrier(jnp.mean(center * center, -1, keepdims=True)) + ln_eps) * gain_row + shift_row

def encoder_layer(x_rows, w_qkv, w_attn, w_in, w_down, gain_rows, shift_rows, hidden_bias, allowed):
    slot_count = x_rows.shape[0]
    low_in = low(x_rows)
    zero_row = jnp.zeros_like(shift_rows[0])
    qkv_bias = jnp.concatenate([shift_rows[0], zero_row, shift_rows[1]])
    qkv_all = low(low_back(matmul_t(low_in, w_qkv) + qkv_bias))
    head_stack = qkv_all.reshape(slot_count, 3, HEADS, HEAD_DIM)
    scores = jnp.einsum('qhd,khd->hqk', head_stack[:, 0], head_stack[:, 1], precision=lax.Precision.HIGHEST) * HEAD_DIM ** (-0.5)
    scores = low_back(jnp.where(allowed[None], scores, neg_big))
    attention_weights_norm = low(jax.nn.softmax(scores, axis=-1))
    context = jnp.einsum('hqk,khd->qhd', attention_weights_norm, head_stack[:, 2], precision=lax.Precision.HIGHEST).reshape(slot_count, D)
    context = low(low_back(context))
    attn_out = low_back(matmul_t(context, w_attn) + shift_rows[2])
    depth_mid = layer_norm(x_rows + attn_out, gain_rows[0], shift_rows[3])
    hidden_pre = low_back(matmul_t(low(depth_mid), w_in) + hidden_bias)
    hidden_act = low(jax.nn.gelu(hidden_pre, approximate=False))
    down_out = low_back(matmul_t(hidden_act, w_down) + shift_rows[4])
    return layer_norm(depth_mid + down_out, gain_rows[1], shift_rows[5])

def reference(hidden_in, out_grad, passage_len, query_len, prefix_units, qkv_weight, attn_weight, in_weight, down_weight, norm_gains, bias_rows, in_bias):
    weights_f32 = tuple((member.astype(jnp.float32) for member in (qkv_weight, attn_weight, in_weight, down_weight, norm_gains, bias_rows, in_bias)))
    slot_count = LP + LQ
    position = jnp.arange(slot_count)
    in_query = position >= LP
    feature = jnp.arange(D)

    def one_pair(totals, inputs):
        pair_rows, pair_grad, pass_len, ques_len, unit_pair = inputs
        valid_slot = jnp.where(in_query, position - LP < ques_len, position < pass_len)
        allowed = (in_query[:, None] == in_query[None, :]) & valid_slot[None, :]
        pass_w = jnp.where(~in_query & valid_slot, 1.0, 0.0) / pass_len.astype(jnp.float32)
        ques_w = jnp.where(in_query & valid_slot, 1.0, 0.0) / ques_len.astype(jnp.float32)
        pool_weights = jnp.stack([pass_w, ques_w])
        keep_rows = jnp.stack([(feature < prefix_step * unit_pair[0]).astype(jnp.float32), (feature < prefix_step * unit_pair[1]).astype(jnp.float32)])

        def forward(x_rows, w_qkv, w_attn, w_in, w_down, gains_all, shifts_all, biases_in):
            depth_one = encoder_layer(x_rows, w_qkv[0], w_attn[0], w_in[0], w_down[0], gains_all[0], shifts_all[0], biases_in[0], allowed)
            depth_two = encoder_layer(depth_one, w_qkv[1], w_attn[1], w_in[1], w_down[1], gains_all[1], shifts_all[1], biases_in[1], allowed)
            pooled_list = []
            for depth_index, depth_vals in enumerate((depth_one, depth_two)):
                pooled_sums = jnp.einsum('ct,td->cd', pool_weights, depth_vals, precision=lax.Precision.HIGHEST)
                pooled_list.append(pooled_sums * keep_rows[depth_index][None, :])
            return (depth_two, jnp.stack(pooled_list))
        (depth_two, pooled_pair), pullback = jax.vjp(forward, pair_rows.astype(jnp.float32), *weights_f32)
        gradients = pullback((pair_grad.astype(jnp.float32), jnp.zeros_like(pooled_pair)))
        new_totals = tuple((total_now + grad_now for total_now, grad_now in zip(totals, gradients[1:])))
        return (new_totals, (depth_two.astype(jnp.bfloat16), pooled_pair, gradients[0].astype(jnp.bfloat16)))
    zero_totals = tuple((jnp.zeros_like(member) for member in weights_f32))
    totals, (activations, pooled, input_grad) = lax.scan(one_pair, zero_totals, (hidden_in, out_grad, passage_len, query_len, prefix_units))
    return (activations, pooled, input_grad, totals[0], totals[1], totals[2], totals[3], totals[4], totals[5], totals[6])
```

```python
import functools
import math
from functools import partial

import jax
import jax.numpy as jnp
import numpy as np
from jax import lax
from jax.experimental import pallas as pl
from jax.experimental.pallas import tpu as pltpu
from jax.sharding import PartitionSpec as P

AX = ("dp", "fsdp")

HEADS = 12
HEAD_DIM = 64
LP = 512


ln_eps = 1e-12
neg_big = -1e30
prefix_step = 64


def product_t(left, right):
    return lax.dot_general(
        left, right, (((1,), (1,)), ((), ())), preferred_element_type=jnp.float32
    )


def product_n(left, right):
    return jnp.dot(left, right, preferred_element_type=jnp.float32)


def product_tn(left, right):
    return lax.dot_general(
        left, right, (((0,), (0,)), ((), ())), preferred_element_type=jnp.float32
    )


def norm_forward(values, gain_row, shift_row):
    center = values - jnp.mean(values, -1, keepdims=True)
    inverse = lax.rsqrt(jnp.mean(center * center, -1, keepdims=True) + ln_eps)
    normed = center * inverse
    return (normed * gain_row + shift_row, normed, inverse)


def norm_backward(output_gradient, normed, inverse, gain_row):
    scaled = output_gradient * gain_row
    grad_input = inverse * (
        scaled
        - jnp.mean(scaled, -1, keepdims=True)
        - normed * jnp.mean(scaled * normed, -1, keepdims=True)
    )
    return (grad_input, jnp.sum(output_gradient * normed, 0), jnp.sum(output_gradient, 0))


def column_sum(values):
    return jnp.sum(values.astype(jnp.float32), 0)


def fetch_forward(shards, depth_index):
    return (
        lax.all_gather(shards[0][depth_index], AX, axis=0, tiled=True),
        lax.all_gather(shards[1][depth_index], AX, axis=0, tiled=True),
        lax.all_gather(shards[2][depth_index], AX, axis=0, tiled=True),
        lax.all_gather(shards[3][depth_index], AX, axis=0, tiled=True),
        lax.all_gather(shards[4][depth_index], AX, axis=1, tiled=True),
        lax.all_gather(shards[5][depth_index], AX, axis=1, tiled=True),
        lax.all_gather(shards[6][depth_index], AX, axis=0, tiled=True),
    )


def fetch_backward(shards, depth_index):
    return (
        lax.all_gather(shards[0][depth_index], AX, axis=0, tiled=True),
        lax.all_gather(shards[1][depth_index], AX, axis=0, tiled=True),
        lax.all_gather(shards[2][depth_index], AX, axis=0, tiled=True),
        lax.all_gather(shards[3][depth_index], AX, axis=0, tiled=True),
        lax.all_gather(shards[4][depth_index], AX, axis=1, tiled=True),
        lax.all_gather(shards[5][depth_index], AX, axis=1, tiled=True),
        lax.all_gather(shards[6][depth_index], AX, axis=0, tiled=True),
    )


def owner_term(operands, dev_count, dev_total):
    (
        grad_qkv_low,
        inputs_low,
        grad_attn_low,
        context_low,
        grad_pre_low,
        mid_low,
        grad_down_low,
        hidden_low,
    ) = operands
    rows_here = inputs_low.shape[0]
    width = inputs_low.shape[1]

    def select_cols(values):
        per_device = values.shape[1] // dev_total
        chosen = values.reshape(rows_here, dev_total, per_device)
        return chosen.reshape(rows_here, dev_count * per_device)

    pieces = [
        product_tn(select_cols(grad_qkv_low), inputs_low),
        product_tn(select_cols(grad_attn_low), context_low),
        product_tn(select_cols(grad_pre_low), mid_low),
        product_tn(select_cols(grad_down_low), hidden_low),
    ]
    return jnp.concatenate([piece.astype(jnp.bfloat16).reshape(dev_count, -1, width) for piece in pieces], axis=1)


def split_owned(owned_rows, dev_total, model_width, hidden_width):
    qkv_rows = 3 * model_width // dev_total
    attn_rows = model_width // dev_total
    in_rows = hidden_width // dev_total
    grad_w_qkv = owned_rows[:qkv_rows]
    grad_w_attn = owned_rows[qkv_rows : qkv_rows + attn_rows]
    grad_w_in = owned_rows[qkv_rows + attn_rows : qkv_rows + attn_rows + in_rows]
    grad_w_down = owned_rows[qkv_rows + attn_rows + in_rows :].reshape(
        model_width // dev_total, hidden_width
    )
    return (grad_w_qkv, grad_w_attn, grad_w_in, grad_w_down)


def body(
    hidden_in,
    out_grad,
    passage_len,
    query_len,
    prefix_units,
    qkv_weight,
    attn_weight,
    in_weight,
    down_weight,
    norm_gains,
    bias_rows,
    in_bias,
):
    pair_count = hidden_in.shape[0]
    slot_count = hidden_in.shape[1]
    model_width = hidden_in.shape[2]
    hidden_width = in_bias.shape[1] * lax.axis_size(AX)
    dev_total = lax.axis_size(AX)
    row_count = pair_count * slot_count
    head_scale = HEAD_DIM ** (-0.5)
    position = jnp.arange(slot_count)
    in_query = position >= LP
    valid_slot = jnp.where(
        in_query[None, :],
        (position - LP)[None, :] < query_len[:, None],
        position[None, :] < passage_len[:, None],
    )
    allowed = (in_query[:, None] == in_query[None, :])[None] & valid_slot[:, None, :]

    def masked_scores(query_matrix, key_matrix):
        scores = (
            jnp.einsum("ifm,igm->ifg", query_matrix, key_matrix, preferred_element_type=jnp.float32)
            * head_scale
        )
        return jnp.where(allowed, scores, neg_big)

    def attend_head(operands):
        query_matrix, key_matrix, value_matrix = operands
        scores = masked_scores(query_matrix, key_matrix)
        row_max = jnp.max(scores, -1, keepdims=True)
        exp_terms = jnp.exp(scores - row_max)
        row_total = jnp.sum(exp_terms, -1, keepdims=True)
        attention_weights_norm = (exp_terms / row_total).astype(jnp.bfloat16)
        context = jnp.einsum(
            "exr,erl->exl", attention_weights_norm, value_matrix, preferred_element_type=jnp.float32
        )
        return (context.astype(jnp.bfloat16), (row_max + jnp.log(row_total))[..., 0])

    def attend_back(operands):
        query_matrix, key_matrix, value_matrix, context_gradient, log_totals = operands
        scores = masked_scores(query_matrix, key_matrix)
        attention_weights_norm = jnp.exp(scores - log_totals[..., None])
        grad_values = jnp.einsum(
            "cza,czj->caj",
            attention_weights_norm.astype(jnp.bfloat16),
            context_gradient,
            preferred_element_type=jnp.float32,
        )
        grad_probs = jnp.einsum(
            "ifm,igm->ifg", context_gradient, value_matrix, preferred_element_type=jnp.float32
        )
        inner_sum = jnp.sum(attention_weights_norm * grad_probs, -1, keepdims=True)
        score_gradient = (attention_weights_norm * (grad_probs - inner_sum)).astype(jnp.bfloat16)
        grad_query = (
            jnp.einsum(
                "exr,erl->exl", score_gradient, key_matrix, preferred_element_type=jnp.float32
            )
            * head_scale
        )
        grad_keys = (
            jnp.einsum(
                "cza,czj->caj", score_gradient, query_matrix, preferred_element_type=jnp.float32
            )
            * head_scale
        )
        return (
            grad_query.astype(jnp.bfloat16),
            grad_keys.astype(jnp.bfloat16),
            grad_values.astype(jnp.bfloat16),
        )

    def layer_backward(output_gradient, saved, params):
        w_qkv, w_attn, w_in, w_down, gain_rows, shift_rows, hidden_bias = params
        (
            inputs_low,
            head_stack,
            log_totals,
            context_low,
            normed_a,
            inverse_a,
            mid_low,
            hidden_pre,
            hidden_low,
            normed_b,
            inverse_b,
        ) = saved
        gain_f = gain_rows.astype(jnp.float32)
        grad_second, grad_gain_b, grad_shift_b = norm_backward(
            output_gradient, normed_b, inverse_b, gain_f[1]
        )
        grad_down_low = grad_second.astype(jnp.bfloat16)
        grad_hidden = product_n(grad_down_low, w_down)
        unused_value, gelu_back = jax.vjp(partial(jax.nn.gelu, approximate=False), hidden_pre)
        grad_pre_low = gelu_back(grad_hidden)[0].astype(jnp.bfloat16)
        middle_gradient = grad_second + product_n(grad_pre_low, w_in)
        grad_attn_sum, grad_gain_a, grad_shift_a = norm_backward(
            middle_gradient, normed_a, inverse_a, gain_f[0]
        )
        grad_attn_low = grad_attn_sum.astype(jnp.bfloat16)
        context_gradient = product_n(grad_attn_low, w_attn).astype(jnp.bfloat16)
        context_heads = context_gradient.reshape(pair_count, slot_count, HEADS, HEAD_DIM).transpose(
            2, 0, 1, 3
        )
        grads_query, grads_keys, grads_values = lax.map(
            attend_back, (head_stack[0], head_stack[1], head_stack[2], context_heads, log_totals)
        )
        grad_qkv_low = (
            jnp.stack([grads_query, grads_keys, grads_values])
            .transpose(2, 3, 0, 1, 4)
            .reshape(row_count, 3 * model_width)
        )
        grad_inputs = grad_attn_sum + product_n(grad_qkv_low, w_qkv)
        qkv_sums = column_sum(grad_qkv_low)
        grad_shift_rows = jnp.stack(
            [
                qkv_sums[:model_width],
                qkv_sums[2 * model_width :],
                column_sum(grad_attn_low),
                grad_shift_a,
                column_sum(grad_down_low),
                grad_shift_b,
            ]
        )
        grad_gain_rows = jnp.stack([grad_gain_a, grad_gain_b])
        small_terms = (grad_gain_rows, grad_shift_rows, column_sum(grad_pre_low))
        operands = (
            grad_qkv_low,
            inputs_low,
            grad_attn_low,
            context_low,
            grad_pre_low,
            mid_low,
            grad_down_low,
            hidden_low,
        )
        return (grad_inputs, small_terms, operands)

    pass_w = (
        jnp.where((~in_query)[None, :] & valid_slot, 1.0, 0.0)
        / passage_len.astype(jnp.float32)[:, None]
    )
    ques_w = (
        jnp.where(in_query[None, :] & valid_slot, 1.0, 0.0) / query_len.astype(jnp.float32)[:, None]
    )
    pool_weights = jnp.stack([pass_w, ques_w], axis=1)
    feature = jnp.arange(model_width)
    shards = (qkv_weight, attn_weight, in_weight, down_weight, norm_gains, bias_rows, in_bias)
    current = hidden_in.reshape(row_count, model_width).astype(jnp.float32)
    current_low = hidden_in.reshape(row_count, model_width)
    saved_all = []
    params_all = []
    pooled_list = []
    for depth_index in range(2):
        params = fetch_forward(shards, depth_index)
        (
            layer_w_qkv,
            layer_w_attn,
            layer_w_in,
            layer_w_down,
            layer_gain_rows,
            layer_shift_rows,
            layer_hidden_bias,
        ) = params
        layer_gain_f = layer_gain_rows.astype(jnp.float32)
        shift_f = layer_shift_rows.astype(jnp.float32)
        qkv_bias = jnp.concatenate([shift_f[0], jnp.zeros_like(shift_f[0]), shift_f[1]])
        qkv_low = (product_t(current_low, layer_w_qkv) + qkv_bias).astype(jnp.bfloat16)
        layer_head_stack = qkv_low.reshape(pair_count, slot_count, 3, HEADS, HEAD_DIM).transpose(
            2, 3, 0, 1, 4
        )
        contexts, layer_log_totals = lax.map(
            attend_head, (layer_head_stack[0], layer_head_stack[1], layer_head_stack[2])
        )
        layer_context_low = contexts.transpose(1, 2, 0, 3).reshape(row_count, model_width)
        attn_out = product_t(layer_context_low, layer_w_attn) + shift_f[2]
        depth_mid, layer_normed_a, layer_inverse_a = norm_forward(
            current + attn_out, layer_gain_f[0], shift_f[3]
        )
        layer_mid_low = depth_mid.astype(jnp.bfloat16)
        layer_hidden_pre = product_t(layer_mid_low, layer_w_in) + layer_hidden_bias.astype(
            jnp.float32
        )
        layer_hidden_low = jax.nn.gelu(layer_hidden_pre, approximate=False).astype(jnp.bfloat16)
        down_out = product_t(layer_hidden_low, layer_w_down) + shift_f[4]
        layer_out, layer_normed_b, layer_inverse_b = norm_forward(
            depth_mid + down_out, layer_gain_f[1], shift_f[5]
        )
        layer_saved = (
            current_low,
            layer_head_stack,
            layer_log_totals,
            layer_context_low,
            layer_normed_a,
            layer_inverse_a,
            layer_mid_low,
            layer_hidden_pre,
            layer_hidden_low,
            layer_normed_b,
            layer_inverse_b,
        )
        current = layer_out
        saved = layer_saved
        current_low = current.astype(jnp.bfloat16)
        saved_all.append(saved)
        params_all.append(params)
        keep_cols = (feature[None, :] < prefix_step * prefix_units[:, depth_index][:, None]).astype(
            jnp.float32
        )
        pooled_sums = jnp.einsum(
            "bct,btd->bcd",
            pool_weights,
            current.reshape(pair_count, slot_count, model_width),
            precision=lax.Precision.HIGHEST,
        )
        pooled_list.append(pooled_sums * keep_cols[:, None, :])
    activations = current_low.reshape(pair_count, slot_count, model_width)
    pooled = jnp.stack(pooled_list, axis=1)
    layer_rows = (4 * model_width + 2 * hidden_width) // dev_total
    gradient = out_grad.reshape(row_count, model_width).astype(jnp.float32)
    small_by_depth = [None, None]
    operands_by_depth = [None, None]
    matrices_by_depth = [None, None]
    for depth_index in (1, 0):
        params = fetch_backward(shards, depth_index)
        gradient, small_terms, operands = layer_backward(gradient, saved_all[depth_index], params)
        small_by_depth[depth_index] = small_terms
        operands_by_depth[depth_index] = operands

        def layer_fn(row_start, row_number, operands=operands):
            return owner_term(operands, row_number // layer_rows, dev_total).reshape(
                row_number, model_width
            )

        owned_rows = lax.psum_scatter(
            layer_fn(jnp.int32(0), lax.axis_size(AX) * layer_rows),
            AX,
            scatter_dimension=0,
            tiled=True,
        ).astype(jnp.float32)
        matrices_by_depth[depth_index] = split_owned(
            owned_rows, dev_total, model_width, hidden_width
        )
    small_stacks = [
        jnp.stack([small_by_depth[0][slot_index], small_by_depth[1][slot_index]])
        for slot_index in range(3)
    ]
    grad_gains, grad_biases, grad_in_bias = (
        lax.psum_scatter(small_stacks[0], AX, scatter_dimension=2, tiled=True),
        lax.psum_scatter(small_stacks[1], AX, scatter_dimension=2, tiled=True),
        lax.psum_scatter(small_stacks[2], AX, scatter_dimension=1, tiled=True),
    )
    matrix_out = tuple(
        (
            jnp.stack([matrices_by_depth[0][slot_index], matrices_by_depth[1][slot_index]])
            for slot_index in range(4)
        )
    )
    input_grad = gradient.astype(jnp.bfloat16).reshape(pair_count, slot_count, model_width)
    return (
        activations,
        pooled,
        input_grad,
        matrix_out[0],
        matrix_out[1],
        matrix_out[2],
        matrix_out[3],
        grad_gains,
        grad_biases,
        grad_in_bias,
    )


MESH = pl.DeviceIdType.MESH

PIECES = ((0, 16), (16, 16), (32, 32), (64, 32))
LAYERS, CHUNKS, ROWS, WIDTH = 2, 3, 96, 768


class Place:
    def __init__(self, nz):
        dp, fs = lax.axis_index("dp"), lax.axis_index("fsdp")
        self.nz = nz
        self.x, self.c = dp // 2, lax.rem(dp, 2)
        self.z, self.y = fs // 2, lax.rem(fs, 2)

    def device(self, x=None, c=None, z=None, y=None):
        x = self.x if x is None else x
        c = self.c if c is None else c
        z = self.z if z is None else z
        y = self.y if y is None else y
        return (x * 2 + c, z * 2 + y)

    def over_x(self):
        return self.device(x=1 - self.x)

    def over_y(self):
        return self.device(y=1 - self.y)

    def over_c(self):
        return self.device(c=1 - self.c)

    def along_z(self, way):
        return self.device(z=self.z + (1 if way == 0 else -1))

    def has_z(self, way, steps):
        return self.z + steps < self.nz if way == 0 else self.z - steps >= 0


def entry_barrier(place):
    bar = pltpu.get_barrier_semaphore()
    for dev in (place.over_x(), place.over_y(), place.over_c()):
        pl.semaphore_signal(bar, inc=1, device_id=dev, device_id_type=MESH)
    for way in (0, 1):
        @pl.when(place.has_z(way, 1))
        def _():
            pl.semaphore_signal(bar, inc=1, device_id=place.along_z(way), device_id_type=MESH)
    pl.semaphore_wait(bar, 3 + place.has_z(0, 1).astype(jnp.int32) + place.has_z(1, 1).astype(jnp.int32))


class Gather:
    def __init__(self, place, shard, out, sz, rz, sb, rb):
        self.p, self.shard, self.out = place, shard, out
        self.sz, self.rz, self.sb, self.rb = sz, rz, sb, rb

    def slot(self, i, t, x, c, z, y):
        lo, n = PIECES[t]
        l, ch = i
        return self.out.at[l, ch, x, c, z, y, pl.ds(lo, n)]

    def copy(self, src, dst, s, r, dev):
        return pltpu.make_async_remote_copy(
            src_ref=src, dst_ref=dst, send_sem=s, recv_sem=r, device_id=dev, device_id_type=MESH)

    def zcopy(self, i, t, way, dist, zs):
        p = self.p
        x = slice(None) if t == 2 else p.x
        y = slice(None) if t == 3 else p.y
        ref = self.slot(i, t, x, p.c, zs, y)
        src = ref
        n = i[0] * CHUNKS + i[1]
        return self.copy(src, ref, self.sz.at[n, t, way, dist - 1], self.rz.at[n, t, way, dist - 1], p.along_z(way))

    def zsend(self, i, t, way, dist):
        p = self.p
        zs = p.z - (dist - 1) if way == 0 else p.z + (dist - 1)
        ok = p.has_z(way, 1)
        if dist > 1:
            ok = jnp.logical_and(ok, p.has_z(1 - way, dist - 1))
        return ok, lambda: self.zcopy(i, t, way, dist, zs)

    def zrecv(self, i, t, way, dist):
        p = self.p
        zs = p.z - dist if way == 0 else p.z + dist
        return p.has_z(1 - way, dist), lambda: self.zcopy(i, t, way, dist, zs)

    def zstep(self, i, t, dist):
        for way in (0, 1):
            ok, mk = self.zrecv(i, t, way, dist)

            @pl.when(ok)
            def _():
                mk().wait_recv()
            if dist + 1 < self.p.nz:
                ok2, mk2 = self.zsend(i, t, way, dist + 1)

                @pl.when(ok2)
                def _():
                    mk2().start()

    def zfirst(self, i, t):
        for way in (0, 1):
            ok, mk = self.zsend(i, t, way, 1)

            @pl.when(ok)
            def _():
                mk().start()

    def bulk(self, i, t, axis, mine):
        p = self.p
        al = slice(None)
        n = i[0] * CHUNKS + i[1]
        if axis == "c":
            c = p.c if mine else 1 - p.c
            ref, dev, k = self.slot(i, t, al, c, al, al), p.over_c(), 2
        elif axis == "x":
            x = p.x if mine else 1 - p.x
            z = p.z if t == 2 else al
            y = al if t in (1, 3) else p.y
            ref, dev, k = self.slot(i, t, x, p.c, z, y), p.over_x(), 0
        else:
            y = p.y if mine else 1 - p.y
            z = p.z if t == 3 else al
            x = al if t in (0, 2) else p.x
            ref, dev, k = self.slot(i, t, x, p.c, z, y), p.over_y(), 1
        return self.copy(ref, ref, self.sb.at[n, t, k], self.rb.at[n, t, k], dev)

    def step(self, grp, st, i):
        for t in {"AB": (0, 1), "CD": (2, 3), "S": (0,)}[grp]:
            first, second = ("x", "y") if t in (0, 2) else ("y", "x")
            if t < 2:
                if st == 0:
                    self.zfirst(i, t)
                elif st <= 3:
                    self.zstep(i, t, st)
                    if st == 3:
                        self.bulk(i, t, first, True).start()
                elif st == 4:
                    self.bulk(i, t, first, False).wait_recv()
                    self.bulk(i, t, second, True).start()
            else:
                if st == 0:
                    self.bulk(i, t, first, True).start()
                elif st == 1:
                    self.bulk(i, t, first, False).wait_recv()
                    self.zfirst(i, t)
                elif st <= 4:
                    self.zstep(i, t, st - 1)
                    if st == 4:
                        self.bulk(i, t, second, True).start()
            if st == 5:
                self.bulk(i, t, second, False).wait_recv()
                self.bulk(i, t, "c", True).start()
            elif st == 6:
                self.bulk(i, t, "c", False).wait_recv()

    def finish(self, i, types=(0, 1, 2, 3)):
        for t in types:
            for axis in ("x", "y", "c"):
                self.bulk(i, t, axis, True).wait_send()
            for way in (0, 1):
                for dist in range(1, self.p.nz):
                    ok, mk = self.zsend(i, t, way, dist)

                    @pl.when(ok)
                    def _():
                        mk().wait_send()


def gather_kernel(nz, shard, out, sz, rz, sb, rb, local):
    place = Place(nz)
    p = place
    own = pltpu.make_async_copy(shard, out.at[:, :, p.x, p.c, p.z, p.y], local)
    own.start()
    entry_barrier(place)
    own.wait()
    g = Gather(place, shard, out, sz, rz, sb, rb)
    chunks = [(l, ch) for l in range(LAYERS) for ch in range(CHUNKS)]
    for grp, st, c in ORDER:
        g.step(grp, st, chunks[c])
    for i in chunks:
        g.finish(i)


def gather_call(shard, nz, cid=0):
    n = LAYERS * CHUNKS
    return pl.pallas_call(
        functools.partial(gather_kernel, nz),
        out_shape=jax.ShapeDtypeStruct((LAYERS, CHUNKS, 2, 2, nz, 2, ROWS, WIDTH), jnp.bfloat16),
        in_specs=[pl.BlockSpec(memory_space=pl.ANY)],
        out_specs=pl.BlockSpec(memory_space=pl.ANY),
        scratch_shapes=[
            pltpu.SemaphoreType.DMA((n, 4, 2, nz - 1)), pltpu.SemaphoreType.DMA((n, 4, 2, nz - 1)),
            pltpu.SemaphoreType.DMA((n, 4, 3)), pltpu.SemaphoreType.DMA((n, 4, 3)),
            pltpu.SemaphoreType.DMA(()),
        ],
        compiler_params=pltpu.CompilerParams(collective_id=cid, has_side_effects=True),
        name="gather_weights",
    )(shard)


F32, BF16 = jnp.float32, jnp.bfloat16
HEAD = 64
EPS = 1e-12


def nt(a, b):
    return lax.dot_general(a, b, (((1,), (1,)), ((), ())), preferred_element_type=F32)


def nn(a, b):
    return jnp.dot(a, b, preferred_element_type=F32)


def lane_is(shape, half):
    lane = lax.broadcasted_iota(jnp.int32, shape, len(shape) - 1)
    return (lane < HEAD) if half == 0 else (lane >= HEAD)


def gelu_both(x):
    e = jnp.exp(x * x * -0.5)
    k = 1.0 / (1.0 + (0.3275911 / math.sqrt(2.0)) * jnp.abs(x))
    poly = k * (0.254829592 + k * (-0.284496736 + k * (1.421413741 + k * (-1.453152027 + k * 1.061405429))))
    tail = 0.5 * poly * e
    cdf = jnp.where(x >= 0, 1.0 - tail, tail)
    return x * cdf, cdf + x * (e * (1.0 / math.sqrt(2.0 * math.pi)))


def relay_first(pk, wq, wo, width):
    def body(i, _):
        blk = pk[pl.ds(2 * i, 2)].astype(F32)
        q = jnp.concatenate([blk[0, :72], blk[1, :72]], 0).astype(BF16)
        o = jnp.concatenate([blk[0, 72:], blk[1, 72:]], 0).astype(BF16)
        wq[pl.ds(pl.multiple_of(144 * i, 16), 144), :] = q
        wo[pl.ds(pl.multiple_of(48 * i, 16), 48), :] = o
        return 0
    lax.fori_loop(0, pk.shape[0] // 2, body, 0)


def relay_down(pk, wd, width):
    def body(i, _):
        blk = pk[pl.ds(2 * i, 2)].astype(F32)
        for q in range(4):
            part = jnp.concatenate([blk[0, 24 * q:24 * q + 24], blk[1, 24 * q:24 * q + 24]], 0).astype(BF16)
            wd[pl.ds(pl.multiple_of(48 * i, 16), 48), q * width:(q + 1) * width] = part
        return 0
    lax.fori_loop(0, pk.shape[0] // 2, body, 0)


def project_qkv(xb, wq, bias, out, j, cols):
    sl = slice(j * cols, (j + 1) * cols)
    out[:, sl] = (nt(xb[...], wq[sl, :]) + bias[:, sl]).astype(BF16)


def attend_pair(qkv, key_bias, ctx, lse, i, width):
    a = 128 * i
    q2 = qkv[0:LP, a:a + 128] * jnp.asarray(0.125, BF16)
    k2 = qkv[0:LP, width + a:width + a + 128]
    v2 = qkv[0:LP, 2 * width + a:2 * width + a + 128]
    v2t = v2.T
    parts = []
    for half in (0, 1):
        qm = jnp.where(lane_is(q2.shape, half), q2, jnp.zeros_like(q2))
        s = nt(k2, qm) + key_bias[...]
        m = jnp.max(s, 0, keepdims=True)
        p = jnp.exp(s - m)
        total = jnp.sum(p, 0, keepdims=True)
        pb = (p * (1.0 / total)).astype(BF16)
        lse[2 * i + half] = m + jnp.log(total)
        parts.append(nn(v2t[HEAD * half:HEAD * half + HEAD], pb))
    ctx[0:LP, a:a + 128] = jnp.concatenate(parts, 0).T.astype(BF16)


def query_probs(qkv, query_bias, heads, width):
    rows = qkv.shape[0] - LP
    q = qkv[LP:, 0:width] * jnp.asarray(0.125, BF16)
    lane = lax.broadcasted_iota(jnp.int32, (heads, rows, width), 2)
    head = lax.broadcasted_iota(jnp.int32, (heads, rows, width), 0)
    mine = jnp.logical_and(lane >= head * HEAD, lane < head * HEAD + HEAD)
    qx = jnp.where(mine, q[None].astype(F32), 0.0).astype(BF16).reshape(heads * rows, width)
    s = nt(qx, qkv[LP:, width:2 * width]) + query_bias[...]
    m = jnp.max(s, -1, keepdims=True)
    p = jnp.exp(s - m)
    return mine, p * (1.0 / jnp.sum(p, -1, keepdims=True)), qx


def attend_query(qkv, query_bias, ctx, heads, width):
    rows = qkv.shape[0] - LP
    mine, p, _ = query_probs(qkv, query_bias, heads, width)
    c = nn(p.astype(BF16), qkv[LP:, 2 * width:]).reshape(heads, rows, width)
    ctx[LP:, :] = jnp.sum(jnp.where(mine, c, 0.0), 0).astype(BF16)


def norm_rows(x, o, bias, gain, shift, n_out, r_out, y_out, yb_out, step=32):
    def body(i, _):
        rows = pl.ds(pl.multiple_of(i * step, step), step)
        v = x[rows, :] + o[rows, :] + bias
        c = v - jnp.mean(v, -1, keepdims=True)
        r = lax.rsqrt(jnp.mean(c * c, -1, keepdims=True) + EPS)
        n = c * r
        y = n * gain + shift
        n_out[rows, :] = n
        r_out[rows, :] = r
        y_out[rows, :] = y
        yb_out[rows, :] = y.astype(BF16)
        return 0
    lax.fori_loop(0, x.shape[0] // step, body, 0)


def feed_in(midb, wi, bias, hid, gp, j, cols):
    sl = slice(j * cols, (j + 1) * cols)
    pre = nt(midb[...], wi[sl, :]) + bias[:, sl]
    a, b = gelu_both(pre)
    hid[:, sl] = a.astype(BF16)
    gp[:, sl] = b.astype(BF16)


def project_cols(a, w, out, j, cols):
    sl = slice(j * cols, (j + 1) * cols)
    out[:, sl] = nt(a[...], w[sl, :])


def pool_rows(x, weights, keep, out, depth):
    v = x[...] * weights[...]
    out[depth, 0:1, :] = jnp.sum(v[0:LP], 0, keepdims=True) * keep[depth:depth + 1, :]
    out[depth, 1:2, :] = jnp.sum(v[LP:], 0, keepdims=True) * keep[depth:depth + 1, :]


def spread_small(sg, t24, t96, m24, m96, sp, ib, width):
    dev = sg.shape[0]
    e = nn(sg[...].reshape(dev * 16, 128), t24[...]).reshape(dev, 16, width)
    full = jnp.sum(e * m24[...][:, None, :], 0)
    sp[...] = full
    per = dev // 4
    for j in range(4):
        e = nn(sg[per * j:per * j + per].reshape(per * 16, 128), t96[...]).reshape(per, 16, width)
        ib[:, j * width:(j + 1) * width] = jnp.sum(e * m96[...][:, None, :], 0)


VM = pltpu.VMEM


class ForwardRefs:
    def __init__(self, *refs):
        (self.shard, self.small, self.x, self.kb, self.qb, self.pw, self.keep, self.t24, self.t96, self.m24, self.m96,
         self.gat, self.sgat, self.wq_o, self.wo_o, self.wd_o, self.sp, self.act, self.pooled, self.xb1_o, self.qkv_o,
         self.lse_o, self.ctx_o, self.n1_o, self.r1_o, self.midb_o, self.gp_o, self.hid_o, self.n2_o, self.r2_o,
         self.pk, self.wq, self.wo, self.wi, self.wd, self.sgv, self.ib, self.bq, self.xf, self.xb, self.qkv, self.lse,
         self.ctx, self.o, self.mid, self.midb, self.hid, self.gp, self.n1, self.r1, self.n2, self.r2, self.sz, self.rz,
         self.sb, self.rb, self.ssz, self.srz, self.ssb, self.srb, self.local, self.save) = refs


class SmallGather(Gather):
    def slot(self, i, t, x, c, z, y):
        return self.out.at[x, c, z, y]


def forward_kernel(nz, plan, s_len, width, ff, with_comm, *refs):
    r = ForwardRefs(*refs)
    place = Place(nz)
    p = place
    chunks = [(l, ch) for l in range(LAYERS) for ch in range(CHUNKS)]
    own = pltpu.make_async_copy(r.shard, r.gat.at[:, :, p.x, p.c, p.z, p.y], r.local.at[0])
    own.start()
    owns = pltpu.make_async_copy(r.small, r.sgat.at[p.x, p.c, p.z, p.y], r.local.at[1])
    owns.start()
    entry_barrier(place)
    g = Gather(place, r.shard, r.gat, r.sz, r.rz, r.sb, r.rb)
    sg = SmallGather(place, r.small, r.sgat, r.ssz, r.srz, r.ssb, r.srb)
    own.wait()
    owns.wait()
    pend = {}
    saves = (r.wq_o, r.wo_o, r.wd_o, r.xb1_o, r.qkv_o, r.lse_o, r.ctx_o, r.n1_o, r.r1_o, r.midb_o, r.gp_o, r.hid_o, r.n2_o, r.r2_o)

    def number(out):
        return [k for k, ref in enumerate(saves) if ref is out][0]

    def save(out, ref, l):
        k = number(out)
        cp = pltpu.make_async_copy(ref, out if out is r.xb1_o else out.at[l], r.save.at[k])
        cp.start()
        pend[k] = cp

    def settle(*outs):
        for out in outs:
            cp = pend.pop(number(out), None)
            if cp is not None:
                cp.wait()

    def load(l, ch):
        src = r.gat.at[l, ch]
        dst = r.wi if ch == 1 else r.pk
        return [pltpu.make_async_copy(src, dst, r.local.at[2])]

    def row(k, l):
        return r.sp[8 * l + k:8 * l + k + 1, :]

    def tile(name, l, j):
        if name == "load":
            for cp in load(l, j):
                cp.start()
            if l == 0 and j == 0:
                cp = pltpu.make_async_copy(r.sgat, r.sgv, r.local.at[1])
                cp.start()
        elif name in ("relay", "take"):
            for cp in load(l, j):
                cp.wait()
            if j == 0:
                if l == 0:
                    pltpu.make_async_copy(r.sgat, r.sgv, r.local.at[1]).wait()
                    spread_small(r.sgv.reshape(8 * nz, 16, 128), r.t24, r.t96, r.m24, r.m96, r.sp, r.ib, width)
                    r.xb[...] = r.x[...]
                    r.xf[...] = r.x[...].astype(F32)
                settle(r.wq_o, r.wo_o)
                relay_first(r.pk.reshape(8 * nz, ROWS, width), r.wq, r.wo, width)
                save(r.wq_o, r.wq, l)
                save(r.wo_o, r.wo, l)
                r.bq[:, 0:width] = row(2, l)
                r.bq[:, width:2 * width] = jnp.zeros((1, width), F32)
                r.bq[:, 2 * width:] = row(3, l)
            elif j == 2:
                settle(r.wd_o)
                relay_down(r.pk.reshape(8 * nz, ROWS, width), r.wd, width)
                save(r.wd_o, r.wd, l)
        elif name == "qkv":
            if j == 0:
                settle(r.qkv_o)
            project_qkv(r.xb, r.wq, r.bq, r.qkv, j, width)
            if j == 2:
                save(r.qkv_o, r.qkv, l)
                settle(r.lse_o, r.ctx_o)
        elif name == "attend":
            attend_pair(r.qkv, r.kb, r.ctx, r.lse, j, width)
        elif name == "query":
            attend_query(r.qkv, r.qb, r.ctx, HEADS, width)
            save(r.lse_o, r.lse, l)
            save(r.ctx_o, r.ctx, l)
        elif name == "out":
            for q in range(3):
                project_cols(r.ctx, r.wo, r.o, q, 256)
        elif name == "norm" and j == 0:
            settle(r.n1_o, r.r1_o, r.midb_o)
            norm_rows(r.xf, r.o, row(4, l), row(0, l), row(5, l), r.n1, r.r1, r.mid, r.midb)
            save(r.n1_o, r.n1, l)
            save(r.r1_o, r.r1, l)
            save(r.midb_o, r.midb, l)
            settle(r.gp_o, r.hid_o)
        elif name == "in":
            feed_in(r.midb, r.wi.reshape(ff, width), r.ib.at[8 * l:8 * l + 1], r.hid, r.gp, j, ff // 8)
            if j == 7:
                save(r.gp_o, r.gp, l)
                save(r.hid_o, r.hid, l)
        elif name == "down":
            project_cols(r.hid, r.wd, r.o, j, 256)
        elif name == "norm" and j == 1:
            settle(r.n2_o, r.r2_o)
            last = l == LAYERS - 1
            norm_rows(r.mid, r.o, row(6, l), row(1, l), row(7, l), r.n2, r.r2, r.xf, r.act if last else r.xb)
            save(r.n2_o, r.n2, l)
            save(r.r2_o, r.r2, l)
            if not last:
                save(r.xb1_o, r.xb, l)
            pool_rows(r.xf, r.pw, r.keep, r.pooled, l)

    for kind, a, b, c in plan:
        if kind == 0:
            a = "AB" if a == 0 else "CD"
            if with_comm:
                g.step(a, b, chunks[c])
                if c == 0 and a == "AB":
                    sg.step("S", b, chunks[0])
        else:
            tile(FORWARD_NAMES[a], b, c)
    settle(*saves)
    if with_comm:
        for i in chunks:
            g.finish(i)
        sg.finish(chunks[0], types=(0,))


def forward_call(plan, nz, args, cid=0, with_comm=True):
    shard, small, x = args[:3]
    s_len, width = x.shape
    ff = 4 * width
    dev = 8 * nz
    n = LAYERS * CHUNKS
    any_, vm = pl.BlockSpec(memory_space=pl.ANY), pl.BlockSpec(memory_space=pltpu.VMEM)
    sds = jax.ShapeDtypeStruct
    L = LAYERS
    outs = [
        (sds((L, CHUNKS, 2, 2, nz, 2, ROWS, width), BF16), any_), (sds((2, 2, nz, 2, 16, 128), BF16), any_),
        (sds((L, 3 * width, width), BF16), any_), (sds((L, width, width), BF16), any_), (sds((L, width, ff), BF16), any_),
        (sds((16, width), F32), vm), (sds((s_len, width), BF16), vm), (sds((2, 2, width), F32), vm),
        (sds((s_len, width), BF16), any_), (sds((L, s_len, 3 * width), BF16), any_), (sds((L, HEADS, 1, LP), F32), any_),
        (sds((L, s_len, width), BF16), any_), (sds((L, s_len, width), F32), any_), (sds((L, s_len, 1), F32), any_),
        (sds((L, s_len, width), BF16), any_), (sds((L, s_len, ff), BF16), any_), (sds((L, s_len, ff), BF16), any_),
        (sds((L, s_len, width), F32), any_), (sds((L, s_len, 1), F32), any_),
    ]
    dma = pltpu.SemaphoreType.DMA
    scratch = [
        VM((2, 2, nz, 2, ROWS, width), BF16), VM((3 * width, width), BF16), VM((width, width), BF16), VM((2, 2, nz, 2, ROWS, width), BF16), VM((width, ff), BF16),
        VM((2, 2, nz, 2, 16, 128), BF16), VM((16, ff), F32), VM((1, 3 * width), F32),
        VM((s_len, width), F32), VM((s_len, width), BF16), VM((s_len, 3 * width), BF16), VM((HEADS, 1, LP), F32),
        VM((s_len, width), BF16), VM((s_len, width), F32), VM((s_len, width), F32), VM((s_len, width), BF16),
        VM((s_len, ff), BF16), VM((s_len, ff), BF16),
        VM((s_len, width), F32), VM((s_len, 1), F32), VM((s_len, width), F32), VM((s_len, 1), F32),
        dma((n, 4, 2, nz - 1)), dma((n, 4, 2, nz - 1)), dma((n, 4, 3)), dma((n, 4, 3)),
        dma((1, 1, 2, nz - 1)), dma((1, 1, 2, nz - 1)), dma((1, 1, 3)), dma((1, 1, 3)),
        dma((3,)), dma((14,)),
    ]
    return pl.pallas_call(
        functools.partial(forward_kernel, nz, plan, s_len, width, ff, with_comm),
        out_shape=[o[0] for o in outs],
        in_specs=[vm] * 11,
        out_specs=[o[1] for o in outs],
        scratch_shapes=scratch,
        compiler_params=pltpu.CompilerParams(collective_id=cid, has_side_effects=True, vmem_limit_bytes=60 << 20),
        name="gather_forward",
    )(*args)


BACK_CHUNKS = tuple((l, ch) for l in (1, 0) for ch in (2, 1, 0))


def fold8(v):
    return jnp.sum(v.reshape(v.shape[0] // 8, 8, v.shape[1]), 0)


def col_total(v):
    return jnp.sum(v, 0, keepdims=True)


def norm_back(sources, n_ref, r_ref, gain, d_ref, db_ref, step=32):
    width = n_ref.shape[1]

    def body(i, carry):
        s0, s1, s2 = carry
        rows = pl.ds(pl.multiple_of(i * step, step), step)
        g = sources[0][rows, :]
        for other in sources[1:]:
            g = g + other[rows, :]
        n = n_ref[rows, :]
        e = g * gain
        d = r_ref[rows, :] * (e - jnp.mean(e, -1, keepdims=True) - n * jnp.mean(e * n, -1, keepdims=True))
        db = d.astype(BF16)
        d_ref[rows, :] = d
        db_ref[rows, :] = db
        return s0 + fold8(g * n), s1 + fold8(g), s2 + fold8(db.astype(F32))
    zero = jnp.zeros((8, width), F32)
    out = lax.fori_loop(0, n_ref.shape[0] // step, body, (zero, zero, zero))
    return [col_total(v) for v in out]


def attend_pair_back(qkv, key_bias, lse, dctx, dqkv, i, width):
    a = 128 * i
    scale = jnp.asarray(0.125, BF16)
    q2 = qkv[0:LP, a:a + 128] * scale
    k2 = qkv[0:LP, width + a:width + a + 128]
    v2 = qkv[0:LP, 2 * width + a:2 * width + a + 128]
    c2 = dctx[0:LP, a:a + 128]
    k2t = k2.T
    dqs, dks, dvs = [], [], []
    for half in (0, 1):
        mine = lane_is(q2.shape, half)
        qm = jnp.where(mine, q2, jnp.zeros_like(q2))
        cm = jnp.where(mine, c2, jnp.zeros_like(c2))
        p = jnp.exp(nt(k2, qm) + key_bias[...] - lse[2 * i + half])
        dp = nt(v2, cm)
        dvs.append(nn(p.astype(BF16), c2))
        t = p * dp
        ds = (t - p * jnp.sum(t, 0, keepdims=True)).astype(BF16)
        dks.append(nn(ds, q2))
        dqs.append(nn(k2t[HEAD * half:HEAD * half + HEAD], ds))
    first = lane_is(q2.shape, 0)
    dqkv[0:LP, a:a + 128] = (jnp.concatenate(dqs, 0).T * 0.125).astype(BF16)
    dqkv[0:LP, width + a:width + a + 128] = jnp.where(first, dks[0], dks[1]).astype(BF16)
    dqkv[0:LP, 2 * width + a:2 * width + a + 128] = jnp.where(first, dvs[0], dvs[1]).astype(BF16)


def attend_query_back(qkv, query_bias, dctx, dqkv, heads, width):
    rows = qkv.shape[0] - LP
    mine, p, qx = query_probs(qkv, query_bias, heads, width)
    k, v = qkv[LP:, width:2 * width], qkv[LP:, 2 * width:3 * width]
    cx = jnp.where(mine, dctx[LP:, :][None].astype(F32), 0.0).astype(BF16).reshape(heads * rows, width)
    dp = nt(cx, v)
    ds = (p * (dp - jnp.sum(p * dp, -1, keepdims=True)))
    dsb = ds.astype(BF16)
    dq = jnp.sum(jnp.where(mine, nn(dsb, k).reshape(heads, rows, width), 0.0), 0) * 0.125
    dqkv[LP:, 0:width] = dq.astype(BF16)
    dqkv[LP:, width:2 * width] = nn(ds.T.astype(BF16), qx).astype(BF16)
    dqkv[LP:, 2 * width:] = nn(p.T.astype(BF16), cx).astype(BF16)


class Scatter:
    def __init__(self, place, G, LC, LA, LB, L2, LZ, sends, recvs, zs, zr, cred, total):
        self.p = place
        self.G, self.LC, self.LA, self.LB, self.L2, self.LZ = G, LC, LA, LB, L2, LZ
        self.sends, self.recvs, self.zs, self.zr, self.cred, self.total = sends, recvs, zs, zr, cred, total
        self.waited = set()

    def copy(self, src, dst, s, r, dev):
        return pltpu.make_async_remote_copy(
            src_ref=src, dst_ref=dst, send_sem=s, recv_sem=r, device_id=dev, device_id_type=MESH)

    def credit(self, i, k):
        if i < 2 or (i, k) in self.waited:
            return
        self.waited.add((i, k))
        if k < 3:
            pl.semaphore_wait(self.cred.at[k], 1)
        else:
            @pl.when(self.p.has_z(k - 3, 1))
            def _():
                pl.semaphore_wait(self.cred.at[k], 1)

    def give_credits(self):
        p = self.p
        for k, dev in enumerate((p.over_c(), p.over_x(), p.over_y())):
            pl.semaphore_signal(self.cred.at[k], inc=1, device_id=dev, device_id_type=MESH)
        for way in (0, 1):
            @pl.when(p.has_z(1 - way, 1))
            def _():
                pl.semaphore_signal(self.cred.at[3 + way], inc=1, device_id=p.along_z(1 - way), device_id_type=MESH)

    def rows(self, t):
        return pl.ds(*PIECES[t])

    def landing(self, t):
        lo, n = PIECES[t]
        return pl.ds(0 if t < 2 else 16, n)

    def core_copy(self, i, grp):
        s, p = i % 2, self.p
        rows = pl.ds(0, 32) if grp == "AB" else pl.ds(32, 64)
        k = 0 if grp == "AB" else 1
        return self.copy(self.G.at[s, :, 1 - p.c, :, :, rows], self.LC.at[s, :, :, :, rows],
                         self.sends.at[s, k], self.recvs.at[s, k], p.over_c())

    def first_copy(self, i, t):
        s, p = i % 2, self.p
        al = slice(None)
        if t in (0, 2):
            return self.copy(self.G.at[s, :, p.c, :, 1 - p.y, self.rows(t)], self.LA.at[s, :, :, self.landing(t)],
                             self.sends.at[s, 2 + t], self.recvs.at[s, 2 + t], p.over_y())
        return self.copy(self.G.at[s, 1 - p.x, p.c, :, :, self.rows(t)], self.LB.at[s, :, :, self.landing(t)],
                         self.sends.at[s, 2 + t], self.recvs.at[s, 2 + t], p.over_x())

    def second_copy(self, i, t):
        s, p = i % 2, self.p
        sem = (self.sends.at[s, 6 + t], self.recvs.at[s, 6 + t])
        if t == 0:
            return self.copy(self.G.at[s, 1 - p.x, p.c, :, p.y, self.rows(t)], self.L2.at[s, :, self.rows(t)], *sem, p.over_x())
        if t == 1:
            return self.copy(self.G.at[s, p.x, p.c, :, 1 - p.y, self.rows(t)], self.L2.at[s, :, self.rows(t)], *sem, p.over_y())
        if t == 2:
            return self.copy(self.G.at[s, 1 - p.x, p.c, p.z, p.y, self.rows(t)], self.L2.at[s, 0, self.rows(t)], *sem, p.over_x())
        return self.copy(self.G.at[s, p.x, p.c, p.z, 1 - p.y, self.rows(t)], self.L2.at[s, 0, self.rows(t)], *sem, p.over_y())

    def plane(self, s, t, z):
        p = self.p
        if t == 2:
            return self.G.at[s, :, p.c, z, p.y, self.rows(t)]
        if t == 3:
            return self.G.at[s, p.x, p.c, z, :, self.rows(t)]
        return self.G.at[s, p.x, p.c, z, p.y, self.rows(t)]

    def zland(self, s, t, way, k):
        if t < 2:
            return self.LZ.at[s, way, k, 0, self.rows(t)]
        return self.LZ.at[s, way, k, :, self.rows(t)]

    def zcopy(self, i, t, way, k, zt):
        s = i % 2
        return self.copy(self.plane(s, t, zt), self.zland(s, t, way, k),
                         self.zs.at[s, t, way, k], self.zr.at[s, t, way, k], self.p.along_z(way))

    def ztarget(self, way, k):
        m = self.p.nz - 1 - k
        return self.p.z + m if way == 0 else self.p.z - m

    def zsend_ok(self, way, k):
        return self.p.has_z(way, self.p.nz - 1 - k)

    def zstep(self, i, t, k):
        p, s = self.p, i % 2
        for way in (0, 1):
            if k >= 1:
                ok = p.has_z(1 - way, 1)
                if k < p.nz - 1:
                    ok = jnp.logical_and(ok, p.has_z(way, p.nz - 1 - k))
                zt = self.ztarget(way, k)

                @pl.when(ok)
                def _():
                    self.zcopy(i, t, way, k - 1, zt).wait_recv()
                    ref, add = self.plane(s, t, zt), self.zland(s, t, way, k - 1)
                    ref[...] = ref[...] + add[...]
            if k <= p.nz - 2:
                self.credit(i, 3 + way)
                zt2 = self.ztarget(way, k)

                @pl.when(self.zsend_ok(way, k))
                def _():
                    self.zcopy(i, t, way, k, zt2).start()

    def step(self, grp, st, i):
        p, s = self.p, i % 2
        types = (0, 1) if grp == "AB" else (2, 3)
        if st == 0:
            self.credit(i, 0)
            self.core_copy(i, grp).start()
            return
        if st == 1:
            self.core_copy(i, grp).wait_recv()
            lo, n = (0, 32) if grp == "AB" else (32, 64)
            rows = pl.ds(lo, n)

            def add(z, _):
                for x in (0, 1):
                    for y in (0, 1):
                        self.G[s, x, p.c, z, y, rows] = self.G[s, x, p.c, z, y, rows] + self.LC[s, x, z, y, rows]
                return 0
            lax.fori_loop(0, p.nz, add, 0)
            self.credit(i, 1)
            self.credit(i, 2)
            for t in types:
                self.first_copy(i, t).start()
            return
        for t in types:
            rows = self.rows(t)
            if st == 2:
                self.first_copy(i, t).wait_recv()
                land = self.landing(t)

                def add(z, _):
                    for o in (0, 1):
                        if t in (0, 2):
                            self.G[s, o, p.c, z, p.y, rows] = self.G[s, o, p.c, z, p.y, rows] + self.LA[s, o, z, land]
                        else:
                            self.G[s, p.x, p.c, z, o, rows] = self.G[s, p.x, p.c, z, o, rows] + self.LB[s, z, o, land]
                    return 0
                lax.fori_loop(0, p.nz, add, 0)
                if t < 2:
                    self.second_copy(i, t).start()
                else:
                    self.zstep(i, t, 0)
            elif t < 2:
                if st == 3:
                    self.second_copy(i, t).wait_recv()

                    def add2(z, _):
                        self.G[s, p.x, p.c, z, p.y, rows] = self.G[s, p.x, p.c, z, p.y, rows] + self.L2[s, z, rows]
                        return 0
                    lax.fori_loop(0, p.nz, add2, 0)
                self.zstep(i, t, st - 3)
                if st == 6:
                    self.total[s, rows, :] = self.G[s, p.x, p.c, p.z, p.y, rows].astype(F32)
            else:
                if st <= 5:
                    self.zstep(i, t, st - 2)
                if st == 5:
                    self.second_copy(i, t).start()
                if st == 6:
                    self.second_copy(i, t).wait_recv()
                    self.total[s, rows, :] = self.G[s, p.x, p.c, p.z, p.y, rows].astype(F32) + self.L2[s, 0, rows].astype(F32)

    def finish(self, i):
        for grp in ("AB", "CD"):
            self.core_copy(i, grp).wait_send()
        for t in range(4):
            self.first_copy(i, t).wait_send()
            self.second_copy(i, t).wait_send()
            for way in (0, 1):
                for k in range(self.p.nz - 1):
                    @pl.when(self.zsend_ok(way, k))
                    def _():
                        self.zcopy(i, t, way, k, self.ztarget(way, k)).wait_send()


class SmallSum:
    def __init__(self, place, acc, land, ss, rs):
        self.p, self.acc, self.land, self.ss, self.rs = place, acc, land, ss, rs

    def partner(self, k):
        p = self.p
        if k < 3:
            return (p.over_c, p.over_y, p.over_x)[k]()
        d = 1 << (k - 3)
        return p.device(z=p.z + d - 2 * d * lax.rem(p.z // d, 2))

    def copy(self, l, k):
        return pltpu.make_async_remote_copy(
            src_ref=self.acc.at[l, k], dst_ref=self.land.at[l, k], send_sem=self.ss.at[l, k], recv_sem=self.rs.at[l, k],
            device_id=self.partner(k), device_id_type=MESH)

    def step(self, l, k):
        if k > 0:
            self.copy(l, k - 1).wait_recv()
            self.acc[l, k] = self.acc[l, k - 1] + self.land[l, k - 1]
        if k < 5:
            self.copy(l, k).start()

    def finish(self, l):
        for k in range(5):
            self.copy(l, k).wait_send()


def backward_barrier(place, far):
    bar = pltpu.get_barrier_semaphore()
    for dev in (place.over_x(), place.over_y(), place.over_c(), far):
        pl.semaphore_signal(bar, inc=1, device_id=dev, device_id_type=MESH)
    for way in (0, 1):
        @pl.when(place.has_z(way, 1))
        def _():
            pl.semaphore_signal(bar, inc=1, device_id=place.along_z(way), device_id_type=MESH)
    pl.semaphore_wait(bar, 4 + place.has_z(0, 1).astype(jnp.int32) + place.has_z(1, 1).astype(jnp.int32))


class Refs:
    def __init__(self, *refs):
        (self.kb, self.qb, self.sp, self.og, self.wq_h, self.wo_h, self.wd_h, self.wi_h, self.xb0_h, self.xb1_h, self.qkv_h, self.lse_h,
         self.ctx_h, self.n1_h, self.r1_h, self.midb_h, self.gp_h, self.hid_h, self.n2_h, self.r2_h,
         self.dx_h, self.gq, self.ga, self.gi, self.gd, self.smalls,
         self.G, self.LC, self.LA, self.LB, self.L2, self.LZ, self.total, self.sacc, self.sland,
         self.wd, self.wi, self.gp, self.wo, self.wq, self.g, self.da, self.db, self.n, self.r, self.low, self.lowt,
         self.x1, self.ctx, self.u1, self.dqkv, self.gattn, self.lse,
         self.sends, self.recvs, self.zs, self.zr, self.cred, self.ss, self.rs, self.sem) = refs


FETCHES = ("n2", "r2", "n1", "r1", "og", "hid", "qkv", "midb", "xb", "ctx", "wo", "wq", "lse", "out",
           "wd0", "wd1", "wi0", "wi1", "gp0", "gp1")


def backward_kernel(nz, plan, width, ff, with_comm, *refs):
    r = Refs(*refs)
    place = Place(nz)
    p = place
    sc = Scatter(place, r.G, r.LC, r.LA, r.LB, r.L2, r.LZ, r.sends, r.recvs, r.zs, r.zr, r.cred, r.total)
    ssum = SmallSum(place, r.sacc, r.sland, r.ss, r.rs)
    pend = {}

    def fetch(name, l):
        if l < 0:
            return
        src, dst = {
            "n2": lambda: (r.n2_h.at[l], r.n), "r2": lambda: (r.r2_h.at[l], r.r), "n1": lambda: (r.n1_h.at[l], r.n), "r1": lambda: (r.r1_h.at[l], r.r),
            "og": lambda: (r.og, r.low), "hid": lambda: (r.hid_h.at[l], r.u1), "qkv": lambda: (r.qkv_h.at[l], r.u1.at[:, 0:3 * width]),
            "midb": lambda: (r.midb_h.at[l], r.x1), "xb": lambda: (r.xb1_h if l == 1 else r.xb0_h, r.x1), "ctx": lambda: (r.ctx_h.at[l], r.ctx),
            "wo": lambda: (r.wo_h.at[l], r.wo), "wq": lambda: (r.wq_h.at[l], r.wq), "lse": lambda: (r.lse_h.at[l], r.lse),
        }[name]()
        cp = pltpu.make_async_copy(src, dst, r.sem.at[FETCHES.index(name)])
        cp.start()
        pend[name] = cp

    def fetch_tile(l, j):
        if l < 0:
            return
        s = j % 2
        cols = slice(j * width, (j + 1) * width)
        for name, src, dst in (("wd", r.wd_h.at[l, :, cols], r.wd.at[s]), ("wi", r.wi_h.at[l, 1, j // 2, j % 2], r.wi.at[s]), ("gp", r.gp_h.at[l, :, cols], r.gp.at[s])):
            key = name + str(s)
            cp = pltpu.make_async_copy(src, dst, r.sem.at[FETCHES.index(key)])
            cp.start()
            pend[key] = cp

    def need(*names):
        for name in names:
            pend.pop(name).wait()

    last = LAYERS - 1
    fetch("og", last); fetch("n2", last); fetch("r2", last); fetch("hid", last)
    fetch_tile(last, 0); fetch_tile(last, 1)
    fetch("midb", last); fetch("ctx", last); fetch("wo", last); fetch("wq", last)
    if with_comm:
        backward_barrier(place, ssum.partner(4))

    def gain(k, l):
        return r.sp[8 * l + k:8 * l + k + 1, :]

    def keep(l, k, v):
        r.sacc[l, 0, k:k + 1, :] = v

    def tile(name, l, j):
        if name == "norm" and j == 1:
            if l == last:
                need("og")
                r.g[...] = r.low[...].astype(F32)
            need("n2", "r2")
            gn, gs, ds = norm_back([r.g], r.n, r.r, gain(1, l), r.da, r.low)
            keep(l, 1, gn); keep(l, 7, gs); keep(l, 6, ds)
            r.lowt[...] = r.low[...].T
            fetch("n1", l); fetch("r1", l)
            need("hid")
        elif name == "gdown":
            a, b = j // 2, j % 2
            s = BACK_CHUNKS.index((l, 2)) % 2
            h = width // 2
            res = nn(r.lowt[a * h:(a + 1) * h, :], r.u1[:, 2 * b * width:2 * (b + 1) * width])
            res = res.reshape(4 * nz, h // (4 * nz), 2 * width)
            res = jnp.concatenate([res[:, :, :width], res[:, :, width:]], 1).astype(BF16)
            n = ROWS // 2
            r.G[s, a, :, :, :, b * n:(b + 1) * n, :] = res.reshape(2, nz, 2, n, width)
            if j == 3:
                fetch("qkv", l)
        elif name == "ff":
            s = BACK_CHUNKS.index((l, 1)) % 2
            k = j % 2
            if j == 0:
                need("midb")
            need("wd" + str(k), "gp" + str(k))
            dpre = (nn(r.low[...], r.wd[k]) * r.gp[k].astype(F32)).astype(BF16)
            keep(l, 8 + j, col_total(dpre.astype(F32)))
            r.G[s, j // 2, j % 2] = nn(dpre.T, r.x1[...]).astype(BF16).reshape(nz, 2, ROWS, width)
            need("wi" + str(k))
            wi = r.wi[k].reshape(width, width)
            if j == 0:
                r.db[...] = nn(dpre, wi)
            else:
                r.db[...] = r.db[...] + nn(dpre, wi)
            if j + 2 < 4:
                fetch_tile(l, j + 2)
            else:
                fetch_tile(l - 1, j - 2)
            if j == 3:
                fetch("xb", l)
        elif name == "norm" and j == 0:
            need("n1", "r1")
            gn, gs, ds = norm_back([r.da, r.db], r.n, r.r, gain(0, l), r.da, r.low)
            keep(l, 0, gn); keep(l, 5, gs); keep(l, 4, ds)
            r.lowt[...] = r.low[...].T
            fetch("n2", l - 1); fetch("r2", l - 1)
        elif name == "gattn":
            need("ctx")
            r.gattn[...] = nn(r.lowt[...], r.ctx[...]).astype(BF16)
        elif name == "dctx":
            need("wo")
            r.ctx[...] = nn(r.low[...], r.wo[...]).astype(BF16)
            fetch("wo", l - 1)
            need("qkv")
            fetch("lse", l)
            need("lse")
        elif name == "attend":
            attend_pair_back(r.u1, r.kb, r.lse, r.ctx, r.dqkv, j, width)
        elif name == "query":
            attend_query_back(r.u1, r.qb, r.ctx, r.dqkv, HEADS, width)
            fetch("hid", l - 1); fetch("ctx", l - 1)
            keep(l, 2, col_total(r.dqkv[:, 0:width].astype(F32)))
            keep(l, 3, col_total(r.dqkv[:, 2 * width:].astype(F32)))
            need("xb")
        elif name == "gqkv":
            s = BACK_CHUNKS.index((l, 0)) % 2
            n = 3 * width // 2
            res = nn(r.dqkv[:, j * n:(j + 1) * n].T, r.x1[...]).reshape(4 * nz, n // (4 * nz), width)
            m = width // 2
            att = r.gattn[j * m:(j + 1) * m, :].astype(F32).reshape(4 * nz, m // (4 * nz), width)
            r.G[s, j] = jnp.concatenate([res, att], 1).astype(BF16).reshape(2, nz, 2, ROWS, width)
            if j == 1:
                fetch("midb", l - 1)
        elif name == "dx":
            need("wq")
            r.g[...] = r.da[...] + nn(r.dqkv[...], r.wq[...])
            fetch("wq", l - 1)
            if l == 0:
                r.low[...] = r.g[...].astype(BF16)
                cp = pltpu.make_async_copy(r.low, r.dx_h, r.sem.at[FETCHES.index("out")])
                cp.start()
                pend["out"] = cp
        elif name == "small":
            r.sacc[l, 0, 12:16, :] = jnp.zeros((4, width), F32)

    def finish(i):
        sc.finish(i)
        if i + 2 < len(BACK_CHUNKS):
            sc.give_credits()
        l, ch = BACK_CHUNKS[i]
        s = i % 2
        own = ROWS // 4
        if ch == 0:
            r.gq[l] = r.total[s, 0:3 * own, :]
            r.ga[l] = r.total[s, 3 * own:, :]
        elif ch == 1:
            r.gi[l] = r.total[s]
        else:
            for q in range(4):
                r.gd[l, :, q * width:(q + 1) * width] = r.total[s, q * own:(q + 1) * own, :]

    for kind, a, b, c in plan:
        if kind == 1:
            tile(BACKWARD_NAMES[a], b, c)
        elif with_comm:
            if kind == 0:
                sc.step("AB" if a == 0 else "CD", b, c)
            elif kind == 2:
                finish(c)
            elif kind == 3:
                ssum.step(b, c)
    if with_comm:
        for l in range(LAYERS):
            ssum.finish(l)
            r.smalls[l] = r.sacc[l, 5]
    need(*list(pend))


def backward_call(plan, nz, args, cid=1, with_comm=True):
    s_len, width = args[3].shape
    ff = 4 * width
    dev = 8 * nz
    any_, vm = pl.BlockSpec(memory_space=pl.ANY), pl.BlockSpec(memory_space=pltpu.VMEM)
    sds = jax.ShapeDtypeStruct
    L = LAYERS
    own = ROWS // 4
    outs = [(sds((s_len, width), BF16), any_), (sds((L, 3 * own, width), F32), vm), (sds((L, own, width), F32), vm),
            (sds((L, ROWS, width), F32), vm), (sds((L, own, ff), F32), vm), (sds((L, 16, width), F32), vm)]
    dma = pltpu.SemaphoreType.DMA
    scratch = [
        VM((2, 2, 2, nz, 2, ROWS, width), BF16), VM((2, 2, nz, 2, ROWS, width), BF16),
        VM((2, 2, nz, ROWS // 2, width), BF16), VM((2, nz, 2, ROWS // 2, width), BF16), VM((2, nz, ROWS, width), BF16),
        VM((2, 2, nz - 1, 2, ROWS, width), BF16), VM((2, ROWS, width), F32),
        VM((L, 6, 16, width), F32), VM((L, 5, 16, width), F32),
        VM((2, width, width), BF16), VM((2, nz, 2, ROWS, width), BF16), VM((2, s_len, width), BF16), VM((width, width), BF16), VM((3 * width, width), BF16),
        VM((s_len, width), F32), VM((s_len, width), F32), VM((s_len, width), F32), VM((s_len, width), F32), VM((s_len, 1), F32),
        VM((s_len, width), BF16), VM((width, s_len), BF16), VM((s_len, width), BF16), VM((s_len, width), BF16), VM((s_len, ff), BF16),
        VM((s_len, 3 * width), BF16), VM((width, width), BF16), VM((HEADS, 1, LP), F32),
        dma((2, 10)), dma((2, 10)), dma((2, 4, 2, nz - 1)), dma((2, 4, 2, nz - 1)), pltpu.SemaphoreType.REGULAR((5,)),
        dma((L, 5)), dma((L, 5)), dma((len(FETCHES),)),
    ]
    return pl.pallas_call(
        functools.partial(backward_kernel, nz, plan, width, ff, with_comm),
        out_shape=[o[0] for o in outs],
        in_specs=[vm, vm, vm] + [any_] * 17,
        out_specs=[o[1] for o in outs],
        scratch_shapes=scratch,
        compiler_params=pltpu.CompilerParams(collective_id=cid if with_comm else None, has_side_effects=True, vmem_limit_bytes=63 << 20),
        name="backward_scatter",
    )(*args)


F32, BF16 = jnp.float32, jnp.bfloat16
def pack_weights(qkv_w, attn_w, in_w, down_w):
    L, r, W = qkv_w.shape
    a = jnp.concatenate([qkv_w, attn_w], 1)
    d = down_w.reshape(L, down_w.shape[1], 4, W).transpose(0, 2, 1, 3).reshape(L, -1, W)
    return jnp.stack([a, in_w, d], 1)
def pack_small(gains, biases, in_bias):
    L = gains.shape[0]
    rows = jnp.concatenate([gains, biases], 1)
    rows = jnp.pad(rows, ((0, 0), (0, 0), (0, 8)))
    ib = jnp.pad(in_bias[:, None, :], ((0, 0), (0, 7), (0, 0)))
    return jnp.concatenate([rows, ib], 2).reshape(8 * L, 128)
def spread_tables(dev, width):
    n = np.arange(width)
    per = width // dev
    t24 = np.zeros((128, width), np.float32); t24[n % per, n] = 1
    t96 = np.zeros((128, width), np.float32); t96[32 + n % (4 * per), n] = 1
    m24 = (n[None] // per == np.arange(dev)[:, None]).astype(np.float32)
    m96 = (n[None] // (4 * per) == np.arange(dev // 4)[:, None]).astype(np.float32)
    return jnp.asarray(t24, BF16), jnp.asarray(t96, BF16), jnp.asarray(m24), jnp.asarray(m96)
def masks(passage_len, query_len, prefix_units, s_len, lp, width):
    pos = jnp.arange(s_len)
    live = jnp.where(pos < lp, pos < passage_len[0], pos - lp < query_len[0])
    bias = jnp.where(live, 0.0, -1e30).astype(F32)
    kb, qb = bias[:lp, None], bias[None, lp:]
    count = jnp.where(pos < lp, passage_len[0], query_len[0]).astype(F32)
    pw = (jnp.where(live, 1.0, 0.0) / count)[:, None]
    keep = (jnp.arange(width)[None] < 64 * prefix_units[0][:, None]).astype(F32)
    return kb, qb, pw, keep


FORWARD_NAMES = ("load", "relay", "take", "qkv", "attend", "query", "out", "norm", "in", "down")
BACKWARD_NAMES = ("norm", "gdown", "ff", "gattn", "dctx", "attend", "query", "gqkv", "dx", "small")
FORWARD_PLAN = (
    (0, 0, 0, 0), (0, 0, 0, 1), (0, 1, 0, 0), (0, 0, 0, 2), (0, 0, 1, 0), (0, 1, 1, 0), (0, 1, 0, 4), (0, 0, 2, 0),
    (0, 0, 3, 0), (0, 0, 0, 5), (0, 1, 2, 0), (0, 0, 4, 0), (0, 1, 0, 1), (0, 1, 0, 5), (0, 0, 1, 2), (0, 1, 0, 2),
    (0, 0, 0, 3), (0, 1, 3, 0), (0, 0, 1, 1), (0, 0, 2, 2), (0, 0, 5, 0), (0, 0, 1, 5), (0, 1, 4, 0), (0, 0, 2, 1),
    (0, 1, 1, 1), (0, 0, 1, 3), (0, 1, 0, 3), (0, 1, 2, 1), (0, 0, 3, 1), (0, 1, 5, 0), (0, 0, 3, 2), (0, 1, 1, 2),
    (0, 0, 6, 0), (0, 0, 2, 3), (0, 0, 4, 1), (0, 0, 4, 2), (0, 1, 6, 0), (0, 1, 3, 1), (1, 0, 0, 0), (0, 0, 0, 4),
    (1, 1, 0, 0), (0, 0, 3, 3), (1, 3, 0, 0), (1, 3, 0, 1), (0, 1, 2, 2), (1, 3, 0, 2), (1, 4, 0, 0), (0, 1, 4, 1),
    (0, 0, 5, 2), (0, 1, 1, 3), (1, 4, 0, 1), (1, 4, 0, 2), (0, 0, 4, 3), (0, 0, 5, 1), (1, 4, 0, 3), (1, 4, 0, 4),
    (1, 4, 0, 5), (0, 0, 1, 4), (0, 0, 6, 1), (1, 5, 0, 0), (0, 1, 3, 2), (1, 6, 0, 0), (0, 1, 5, 1), (0, 0, 2, 4),
    (0, 0, 2, 5), (0, 1, 2, 3), (0, 1, 4, 2), (1, 7, 0, 0), (0, 0, 5, 3), (0, 0, 3, 5), (0, 1, 6, 1), (1, 0, 0, 1),
    (1, 2, 0, 1), (0, 0, 6, 2), (0, 1, 3, 3), (1, 8, 0, 0), (0, 1, 1, 4), (0, 1, 1, 5), (0, 0, 6, 3), (1, 8, 0, 1),
    (0, 1, 5, 2), (0, 1, 4, 3), (1, 8, 0, 2), (1, 8, 0, 3), (1, 8, 0, 4), (0, 0, 3, 4), (0, 0, 4, 5), (1, 8, 0, 5),
    (1, 8, 0, 6), (1, 8, 0, 7), (0, 1, 6, 2), (1, 0, 0, 2), (0, 1, 2, 4), (1, 1, 0, 2), (0, 1, 5, 3), (1, 9, 0, 0),
    (1, 9, 0, 1), (1, 9, 0, 2), (0, 1, 3, 4), (1, 7, 0, 1), (0, 1, 6, 3), (1, 0, 1, 0), (0, 1, 4, 4), (1, 1, 1, 0),
    (1, 3, 1, 0), (1, 3, 1, 1), (0, 1, 2, 5), (1, 3, 1, 2), (0, 0, 4, 4), (1, 4, 1, 0), (0, 0, 5, 5), (1, 4, 1, 1),
    (0, 1, 3, 5), (1, 4, 1, 2), (0, 1, 5, 4), (1, 4, 1, 3), (1, 4, 1, 4), (0, 1, 4, 5), (1, 4, 1, 5), (1, 5, 1, 0),
    (0, 0, 5, 4), (1, 6, 1, 0), (1, 7, 1, 0), (0, 1, 6, 4), (0, 0, 6, 4), (1, 0, 1, 1), (1, 2, 1, 1), (1, 8, 1, 0),
    (0, 1, 5, 5), (1, 8, 1, 1), (1, 8, 1, 2), (1, 8, 1, 3), (1, 8, 1, 4), (1, 8, 1, 5), (0, 0, 6, 5), (1, 8, 1, 6),
    (1, 8, 1, 7), (0, 1, 6, 5), (1, 0, 1, 2), (1, 1, 1, 2), (1, 9, 1, 0), (1, 9, 1, 1), (1, 9, 1, 2), (1, 7, 1, 1),
)
BACKWARD_PLAN = (
    (1, 0, 1, 1), (1, 1, 1, 0), (1, 1, 1, 1), (1, 1, 1, 2), (1, 1, 1, 3), (0, 1, 0, 0), (1, 2, 1, 0), (0, 0, 0, 0),
    (1, 2, 1, 1), (0, 1, 1, 0), (1, 2, 1, 2), (0, 0, 1, 0), (1, 2, 1, 3), (0, 1, 0, 1), (1, 0, 1, 0), (0, 1, 2, 0),
    (0, 0, 0, 1), (1, 3, 1, 0), (1, 4, 1, 0), (0, 0, 2, 0), (0, 1, 1, 1), (0, 1, 3, 0), (1, 5, 1, 0), (1, 5, 1, 1),
    (1, 5, 1, 2), (0, 0, 3, 0), (0, 1, 4, 0), (1, 5, 1, 3), (0, 0, 1, 1), (0, 0, 4, 0), (1, 5, 1, 4), (1, 5, 1, 5),
    (0, 0, 5, 0), (0, 1, 5, 0), (1, 6, 1, 0), (0, 0, 2, 1), (0, 1, 6, 0), (0, 0, 6, 0), (2, 0, 0, 0), (1, 7, 1, 0),
    (1, 7, 1, 1), (0, 1, 0, 2), (0, 0, 3, 1), (0, 0, 4, 1), (0, 1, 2, 1), (1, 8, 1, 0), (0, 0, 5, 1), (0, 1, 1, 2),
    (0, 1, 3, 1), (0, 0, 0, 2), (1, 9, 1, 0), (0, 1, 4, 1), (0, 0, 1, 2), (1, 0, 0, 1), (0, 1, 2, 2), (0, 1, 5, 1),
    (3, 0, 1, 0), (0, 0, 2, 2), (0, 0, 6, 1), (0, 1, 3, 2), (0, 1, 6, 1), (2, 0, 0, 1), (1, 1, 0, 0), (1, 1, 0, 1),
    (1, 1, 0, 2), (3, 0, 1, 1), (0, 0, 3, 2), (0, 1, 4, 2), (1, 1, 0, 3), (0, 1, 0, 3), (0, 0, 0, 3), (0, 0, 4, 2),
    (0, 1, 5, 2), (0, 0, 5, 2), (0, 1, 1, 3), (0, 1, 6, 2), (0, 0, 1, 3), (0, 0, 6, 2), (2, 0, 0, 2), (1, 2, 0, 0),
    (1, 2, 0, 1), (1, 2, 0, 2), (0, 1, 2, 3), (1, 2, 0, 3), (0, 1, 0, 4), (0, 1, 3, 3), (1, 0, 0, 0), (1, 3, 0, 0),
    (0, 1, 4, 3), (0, 0, 2, 3), (1, 4, 0, 0), (0, 1, 1, 4), (1, 5, 0, 0), (1, 5, 0, 1), (3, 0, 1, 2), (0, 0, 3, 3),
    (1, 5, 0, 2), (1, 5, 0, 3), (0, 0, 4, 3), (0, 0, 0, 4), (0, 1, 5, 3), (1, 5, 0, 4), (0, 0, 5, 3), (1, 5, 0, 5),
    (0, 1, 2, 4), (0, 1, 6, 3), (1, 6, 0, 0), (0, 0, 1, 4), (0, 0, 6, 3), (3, 0, 1, 3), (2, 0, 0, 3), (1, 7, 0, 0),
    (1, 7, 0, 1), (0, 1, 0, 5), (0, 0, 0, 5), (0, 0, 2, 4), (0, 1, 3, 4), (0, 0, 3, 4), (0, 0, 4, 4), (0, 1, 1, 5),
    (0, 0, 5, 4), (0, 1, 4, 4), (1, 8, 0, 0), (1, 9, 0, 0), (3, 0, 1, 4), (3, 0, 0, 0), (0, 0, 6, 4), (0, 0, 1, 5),
    (0, 1, 2, 5), (3, 0, 0, 1), (0, 1, 3, 5), (0, 0, 2, 5), (3, 0, 0, 2), (0, 1, 5, 4), (0, 0, 3, 5), (0, 0, 4, 5),
    (3, 0, 0, 3), (0, 1, 4, 5), (0, 1, 6, 4), (0, 0, 5, 5), (2, 0, 0, 4), (3, 0, 1, 5), (3, 0, 0, 4), (0, 1, 5, 5),
    (0, 0, 6, 5), (0, 1, 6, 5), (2, 0, 0, 5), (3, 0, 0, 5),
)


def fast_body(nz, hidden_in, out_grad, passage_len, query_len, prefix_units, qkv_weight, attn_weight, in_weight, down_weight,
              norm_gains, bias_rows, in_bias):
    slot_count, model_width = hidden_in.shape[1:]
    dev_total = 8 * nz
    shard = pack_weights(qkv_weight, attn_weight, in_weight, down_weight)
    small = pack_small(norm_gains, bias_rows, in_bias)
    kb, qb, pw, keep = masks(passage_len, query_len, prefix_units, slot_count, LP, model_width)
    (gat, sgat, wq, wo, wd, sp, act, pooled, xb1, qkv, lse, ctx, n1, r1, midb, gp, hid, n2, r2) = forward_call(
        FORWARD_PLAN, nz, [shard, small, hidden_in[0], kb, qb, pw, keep, *spread_tables(dev_total, model_width)])
    dx, gq, ga, gi, gd, smalls = backward_call(
        BACKWARD_PLAN, nz, [kb, qb, sp, out_grad[0], wq, wo, wd, gat, hidden_in[0], xb1, qkv, lse, ctx, n1, r1, midb, gp, hid, n2, r2])
    me = lax.axis_index(AX)
    own = model_width // dev_total
    rows = lax.dynamic_slice(smalls[:, :8], (0, 0, me * own), (LAYERS, 8, own))
    inner = lax.dynamic_slice(smalls[:, 8:12].reshape(LAYERS, 4 * model_width), (0, me * 4 * own), (LAYERS, 4 * own))
    return act[None], pooled[None], dx[None], gq, ga, gi, gd, rows[:, :2], rows[:, 2:], inner


def solution(mesh):
    dp, fsdp = mesh.shape["dp"], mesh.shape["fsdp"]
    fast = dp == 4 and fsdp == 8
    return jax.shard_map(
        partial(fast_body, fsdp // 2) if fast else body,
        mesh=mesh,
        in_specs=(
            P(AX, None, None),
            P(AX, None, None),
            P(AX),
            P(AX),
            P(AX, None),
            P(None, AX, None),
            P(None, AX, None),
            P(None, AX, None),
            P(None, AX, None),
            P(None, None, AX),
            P(None, None, AX),
            P(None, AX),
        ),
        out_specs=(
            P(AX, None, None),
            P(AX, None, None, None),
            P(AX, None, None),
            P(None, AX, None),
            P(None, AX, None),
            P(None, AX, None),
            P(None, AX, None),
            P(None, None, AX),
            P(None, None, AX),
            P(None, AX),
        ),
        check_vma=False,
    )
```

```python
import functools
import math
from functools import partial

import jax
import jax.numpy as jnp
import numpy as np
from jax import lax
from jax.experimental import pallas as pl
from jax.experimental.pallas import tpu as pltpu
from jax.sharding import PartitionSpec as P

AX = ("dp", "fsdp")

HEADS = 12
HEAD_DIM = 64
LP = 512


ln_eps = 1e-12
neg_big = -1e30
prefix_step = 64


def product_t(left, right):
    return lax.dot_general(
        left, right, (((1,), (1,)), ((), ())), preferred_element_type=jnp.float32
    )


def product_n(left, right):
    return jnp.dot(left, right, preferred_element_type=jnp.float32)


def product_tn(left, right):
    return lax.dot_general(
        left, right, (((0,), (0,)), ((), ())), preferred_element_type=jnp.float32
    )


def norm_forward(values, gain_row, shift_row):
    center = values - jnp.mean(values, -1, keepdims=True)
    inverse = lax.rsqrt(jnp.mean(center * center, -1, keepdims=True) + ln_eps)
    normed = center * inverse
    return (normed * gain_row + shift_row, normed, inverse)


def norm_backward(output_gradient, normed, inverse, gain_row):
    scaled = output_gradient * gain_row
    grad_input = inverse * (
        scaled
        - jnp.mean(scaled, -1, keepdims=True)
        - normed * jnp.mean(scaled * normed, -1, keepdims=True)
    )
    return (grad_input, jnp.sum(output_gradient * normed, 0), jnp.sum(output_gradient, 0))


def column_sum(values):
    return jnp.sum(values.astype(jnp.float32), 0)


def fetch_forward(shards, depth_index):
    return (
        lax.all_gather(shards[0][depth_index], AX, axis=0, tiled=True),
        lax.all_gather(shards[1][depth_index], AX, axis=0, tiled=True),
        lax.all_gather(shards[2][depth_index], AX, axis=0, tiled=True),
        lax.all_gather(shards[3][depth_index], AX, axis=0, tiled=True),
        lax.all_gather(shards[4][depth_index], AX, axis=1, tiled=True),
        lax.all_gather(shards[5][depth_index], AX, axis=1, tiled=True),
        lax.all_gather(shards[6][depth_index], AX, axis=0, tiled=True),
    )


def fetch_backward(shards, depth_index):
    return (
        lax.all_gather(shards[0][depth_index], AX, axis=0, tiled=True),
        lax.all_gather(shards[1][depth_index], AX, axis=0, tiled=True),
        lax.all_gather(shards[2][depth_index], AX, axis=0, tiled=True),
        lax.all_gather(shards[3][depth_index], AX, axis=0, tiled=True),
        lax.all_gather(shards[4][depth_index], AX, axis=1, tiled=True),
        lax.all_gather(shards[5][depth_index], AX, axis=1, tiled=True),
        lax.all_gather(shards[6][depth_index], AX, axis=0, tiled=True),
    )


def owner_term(operands, dev_count, dev_total):
    (
        grad_qkv_low,
        inputs_low,
        grad_attn_low,
        context_low,
        grad_pre_low,
        mid_low,
        grad_down_low,
        hidden_low,
    ) = operands
    rows_here = inputs_low.shape[0]
    width = inputs_low.shape[1]

    def select_cols(values):
        per_device = values.shape[1] // dev_total
        chosen = values.reshape(rows_here, dev_total, per_device)
        return chosen.reshape(rows_here, dev_count * per_device)

    pieces = [
        product_tn(select_cols(grad_qkv_low), inputs_low),
        product_tn(select_cols(grad_attn_low), context_low),
        product_tn(select_cols(grad_pre_low), mid_low),
        product_tn(select_cols(grad_down_low), hidden_low),
    ]
    return jnp.concatenate([piece.astype(jnp.bfloat16).reshape(dev_count, -1, width) for piece in pieces], axis=1)


def split_owned(owned_rows, dev_total, model_width, hidden_width):
    qkv_rows = 3 * model_width // dev_total
    attn_rows = model_width // dev_total
    in_rows = hidden_width // dev_total
    grad_w_qkv = owned_rows[:qkv_rows]
    grad_w_attn = owned_rows[qkv_rows : qkv_rows + attn_rows]
    grad_w_in = owned_rows[qkv_rows + attn_rows : qkv_rows + attn_rows + in_rows]
    grad_w_down = owned_rows[qkv_rows + attn_rows + in_rows :].reshape(
        model_width // dev_total, hidden_width
    )
    return (grad_w_qkv, grad_w_attn, grad_w_in, grad_w_down)


def body(
    hidden_in,
    out_grad,
    passage_len,
    query_len,
    prefix_units,
    qkv_weight,
    attn_weight,
    in_weight,
    down_weight,
    norm_gains,
    bias_rows,
    in_bias,
):
    pair_count = hidden_in.shape[0]
    slot_count = hidden_in.shape[1]
    model_width = hidden_in.shape[2]
    hidden_width = in_bias.shape[1] * lax.axis_size(AX)
    dev_total = lax.axis_size(AX)
    row_count = pair_count * slot_count
    head_scale = HEAD_DIM ** (-0.5)
    position = jnp.arange(slot_count)
    in_query = position >= LP
    valid_slot = jnp.where(
        in_query[None, :],
        (position - LP)[None, :] < query_len[:, None],
        position[None, :] < passage_len[:, None],
    )
    allowed = (in_query[:, None] == in_query[None, :])[None] & valid_slot[:, None, :]

    def masked_scores(query_matrix, key_matrix):
        scores = (
            jnp.einsum("ifm,igm->ifg", query_matrix, key_matrix, preferred_element_type=jnp.float32)
            * head_scale
        )
        return jnp.where(allowed, scores, neg_big)

    def attend_head(operands):
        query_matrix, key_matrix, value_matrix = operands
        scores = masked_scores(query_matrix, key_matrix)
        row_max = jnp.max(scores, -1, keepdims=True)
        exp_terms = jnp.exp(scores - row_max)
        row_total = jnp.sum(exp_terms, -1, keepdims=True)
        attention_weights_norm = (exp_terms / row_total).astype(jnp.bfloat16)
        context = jnp.einsum(
            "exr,erl->exl", attention_weights_norm, value_matrix, preferred_element_type=jnp.float32
        )
        return (context.astype(jnp.bfloat16), (row_max + jnp.log(row_total))[..., 0])

    def attend_back(operands):
        query_matrix, key_matrix, value_matrix, context_gradient, log_totals = operands
        scores = masked_scores(query_matrix, key_matrix)
        attention_weights_norm = jnp.exp(scores - log_totals[..., None])
        grad_values = jnp.einsum(
            "cza,czj->caj",
            attention_weights_norm.astype(jnp.bfloat16),
            context_gradient,
            preferred_element_type=jnp.float32,
        )
        grad_probs = jnp.einsum(
            "ifm,igm->ifg", context_gradient, value_matrix, preferred_element_type=jnp.float32
        )
        inner_sum = jnp.sum(attention_weights_norm * grad_probs, -1, keepdims=True)
        score_gradient = (attention_weights_norm * (grad_probs - inner_sum)).astype(jnp.bfloat16)
        grad_query = (
            jnp.einsum(
                "exr,erl->exl", score_gradient, key_matrix, preferred_element_type=jnp.float32
            )
            * head_scale
        )
        grad_keys = (
            jnp.einsum(
                "cza,czj->caj", score_gradient, query_matrix, preferred_element_type=jnp.float32
            )
            * head_scale
        )
        return (
            grad_query.astype(jnp.bfloat16),
            grad_keys.astype(jnp.bfloat16),
            grad_values.astype(jnp.bfloat16),
        )

    def layer_backward(output_gradient, saved, params):
        w_qkv, w_attn, w_in, w_down, gain_rows, shift_rows, hidden_bias = params
        (
            inputs_low,
            head_stack,
            log_totals,
            context_low,
            normed_a,
            inverse_a,
            mid_low,
            hidden_pre,
            hidden_low,
            normed_b,
            inverse_b,
        ) = saved
        gain_f = gain_rows.astype(jnp.float32)
        grad_second, grad_gain_b, grad_shift_b = norm_backward(
            output_gradient, normed_b, inverse_b, gain_f[1]
        )
        grad_down_low = grad_second.astype(jnp.bfloat16)
        grad_hidden = product_n(grad_down_low, w_down)
        unused_value, gelu_back = jax.vjp(partial(jax.nn.gelu, approximate=False), hidden_pre)
        grad_pre_low = gelu_back(grad_hidden)[0].astype(jnp.bfloat16)
        middle_gradient = grad_second + product_n(grad_pre_low, w_in)
        grad_attn_sum, grad_gain_a, grad_shift_a = norm_backward(
            middle_gradient, normed_a, inverse_a, gain_f[0]
        )
        grad_attn_low = grad_attn_sum.astype(jnp.bfloat16)
        context_gradient = product_n(grad_attn_low, w_attn).astype(jnp.bfloat16)
        context_heads = context_gradient.reshape(pair_count, slot_count, HEADS, HEAD_DIM).transpose(
            2, 0, 1, 3
        )
        grads_query, grads_keys, grads_values = lax.map(
            attend_back, (head_stack[0], head_stack[1], head_stack[2], context_heads, log_totals)
        )
        grad_qkv_low = (
            jnp.stack([grads_query, grads_keys, grads_values])
            .transpose(2, 3, 0, 1, 4)
            .reshape(row_count, 3 * model_width)
        )
        grad_inputs = grad_attn_sum + product_n(grad_qkv_low, w_qkv)
        qkv_sums = column_sum(grad_qkv_low)
        grad_shift_rows = jnp.stack(
            [
                qkv_sums[:model_width],
                qkv_sums[2 * model_width :],
                column_sum(grad_attn_low),
                grad_shift_a,
                column_sum(grad_down_low),
                grad_shift_b,
            ]
        )
        grad_gain_rows = jnp.stack([grad_gain_a, grad_gain_b])
        small_terms = (grad_gain_rows, grad_shift_rows, column_sum(grad_pre_low))
        operands = (
            grad_qkv_low,
            inputs_low,
            grad_attn_low,
            context_low,
            grad_pre_low,
            mid_low,
            grad_down_low,
            hidden_low,
        )
        return (grad_inputs, small_terms, operands)

    pass_w = (
        jnp.where((~in_query)[None, :] & valid_slot, 1.0, 0.0)
        / passage_len.astype(jnp.float32)[:, None]
    )
    ques_w = (
        jnp.where(in_query[None, :] & valid_slot, 1.0, 0.0) / query_len.astype(jnp.float32)[:, None]
    )
    pool_weights = jnp.stack([pass_w, ques_w], axis=1)
    feature = jnp.arange(model_width)
    shards = (qkv_weight, attn_weight, in_weight, down_weight, norm_gains, bias_rows, in_bias)
    current = hidden_in.reshape(row_count, model_width).astype(jnp.float32)
    current_low = hidden_in.reshape(row_count, model_width)
    saved_all = []
    params_all = []
    pooled_list = []
    for depth_index in range(2):
        params = fetch_forward(shards, depth_index)
        (
            layer_w_qkv,
            layer_w_attn,
            layer_w_in,
            layer_w_down,
            layer_gain_rows,
            layer_shift_rows,
            layer_hidden_bias,
        ) = params
        layer_gain_f = layer_gain_rows.astype(jnp.float32)
        shift_f = layer_shift_rows.astype(jnp.float32)
        qkv_bias = jnp.concatenate([shift_f[0], jnp.zeros_like(shift_f[0]), shift_f[1]])
        qkv_low = (product_t(current_low, layer_w_qkv) + qkv_bias).astype(jnp.bfloat16)
        layer_head_stack = qkv_low.reshape(pair_count, slot_count, 3, HEADS, HEAD_DIM).transpose(
            2, 3, 0, 1, 4
        )
        contexts, layer_log_totals = lax.map(
            attend_head, (layer_head_stack[0], layer_head_stack[1], layer_head_stack[2])
        )
        layer_context_low = contexts.transpose(1, 2, 0, 3).reshape(row_count, model_width)
        attn_out = product_t(layer_context_low, layer_w_attn) + shift_f[2]
        depth_mid, layer_normed_a, layer_inverse_a = norm_forward(
            current + attn_out, layer_gain_f[0], shift_f[3]
        )
        layer_mid_low = depth_mid.astype(jnp.bfloat16)
        layer_hidden_pre = product_t(layer_mid_low, layer_w_in) + layer_hidden_bias.astype(
            jnp.float32
        )
        layer_hidden_low = jax.nn.gelu(layer_hidden_pre, approximate=False).astype(jnp.bfloat16)
        down_out = product_t(layer_hidden_low, layer_w_down) + shift_f[4]
        layer_out, layer_normed_b, layer_inverse_b = norm_forward(
            depth_mid + down_out, layer_gain_f[1], shift_f[5]
        )
        layer_saved = (
            current_low,
            layer_head_stack,
            layer_log_totals,
            layer_context_low,
            layer_normed_a,
            layer_inverse_a,
            layer_mid_low,
            layer_hidden_pre,
            layer_hidden_low,
            layer_normed_b,
            layer_inverse_b,
        )
        current = layer_out
        saved = layer_saved
        current_low = current.astype(jnp.bfloat16)
        saved_all.append(saved)
        params_all.append(params)
        keep_cols = (feature[None, :] < prefix_step * prefix_units[:, depth_index][:, None]).astype(
            jnp.float32
        )
        pooled_sums = jnp.einsum(
            "bct,btd->bcd",
            pool_weights,
            current.reshape(pair_count, slot_count, model_width),
            precision=lax.Precision.HIGHEST,
        )
        pooled_list.append(pooled_sums * keep_cols[:, None, :])
    activations = current_low.reshape(pair_count, slot_count, model_width)
    pooled = jnp.stack(pooled_list, axis=1)
    layer_rows = (4 * model_width + 2 * hidden_width) // dev_total
    gradient = out_grad.reshape(row_count, model_width).astype(jnp.float32)
    small_by_depth = [None, None]
    operands_by_depth = [None, None]
    matrices_by_depth = [None, None]
    for depth_index in (1, 0):
        params = fetch_backward(shards, depth_index)
        gradient, small_terms, operands = layer_backward(gradient, saved_all[depth_index], params)
        small_by_depth[depth_index] = small_terms
        operands_by_depth[depth_index] = operands

        def layer_fn(row_start, row_number, operands=operands):
            return owner_term(operands, row_number // layer_rows, dev_total).reshape(
                row_number, model_width
            )

        owned_rows = lax.psum_scatter(
            layer_fn(jnp.int32(0), lax.axis_size(AX) * layer_rows),
            AX,
            scatter_dimension=0,
            tiled=True,
        ).astype(jnp.float32)
        matrices_by_depth[depth_index] = split_owned(
            owned_rows, dev_total, model_width, hidden_width
        )
    small_stacks = [
        jnp.stack([small_by_depth[0][slot_index], small_by_depth[1][slot_index]])
        for slot_index in range(3)
    ]
    grad_gains, grad_biases, grad_in_bias = (
        lax.psum_scatter(small_stacks[0], AX, scatter_dimension=2, tiled=True),
        lax.psum_scatter(small_stacks[1], AX, scatter_dimension=2, tiled=True),
        lax.psum_scatter(small_stacks[2], AX, scatter_dimension=1, tiled=True),
    )
    matrix_out = tuple(
        (
            jnp.stack([matrices_by_depth[0][slot_index], matrices_by_depth[1][slot_index]])
            for slot_index in range(4)
        )
    )
    input_grad = gradient.astype(jnp.bfloat16).reshape(pair_count, slot_count, model_width)
    return (
        activations,
        pooled,
        input_grad,
        matrix_out[0],
        matrix_out[1],
        matrix_out[2],
        matrix_out[3],
        grad_gains,
        grad_biases,
        grad_in_bias,
    )


MESH = pl.DeviceIdType.MESH

PIECES = ((0, 16), (16, 16), (32, 32), (64, 32), (0, 32), (32, 64))
SLOT_OF = (0, 1, 2, 3, 0, 2)
LAYERS, CHUNKS, ROWS, WIDTH = 2, 3, 96, 768


class Place:
    def __init__(self, nz):
        dp, fs = lax.axis_index("dp"), lax.axis_index("fsdp")
        self.nz = nz
        self.x, self.c = dp // 2, lax.rem(dp, 2)
        self.z, self.y = fs // 2, lax.rem(fs, 2)

    def device(self, x=None, c=None, z=None, y=None):
        x = self.x if x is None else x
        c = self.c if c is None else c
        z = self.z if z is None else z
        y = self.y if y is None else y
        return (x * 2 + c, z * 2 + y)

    def over_x(self):
        return self.device(x=1 - self.x)

    def over_y(self):
        return self.device(y=1 - self.y)

    def over_c(self):
        return self.device(c=1 - self.c)

    def along_z(self, way):
        return self.device(z=self.z + (1 if way == 0 else -1))

    def has_z(self, way, steps):
        return self.z + steps < self.nz if way == 0 else self.z - steps >= 0


def entry_barrier(place):
    bar = pltpu.get_barrier_semaphore()
    for dev in (place.over_x(), place.over_y(), place.over_c()):
        pl.semaphore_signal(bar, inc=1, device_id=dev, device_id_type=MESH)
    for way in (0, 1):
        @pl.when(place.has_z(way, 1))
        def _():
            pl.semaphore_signal(bar, inc=1, device_id=place.along_z(way), device_id_type=MESH)
    pl.semaphore_wait(bar, 3 + place.has_z(0, 1).astype(jnp.int32) + place.has_z(1, 1).astype(jnp.int32))


class Gather:
    def __init__(self, place, shard, out, sz, rz, sb, rb, ps=None, pr=None):
        self.p, self.shard, self.out = place, shard, out
        self.sz, self.rz, self.sb, self.rb, self.ps, self.pr = sz, rz, sb, rb, ps, pr

    def slot(self, i, t, x, c, z, y):
        lo, n = PIECES[t]
        l, ch = i
        return self.out.at[l, ch, x, c, z, y, pl.ds(lo, n)]

    def copy(self, src, dst, s, r, dev):
        return pltpu.make_async_remote_copy(
            src_ref=src, dst_ref=dst, send_sem=s, recv_sem=r, device_id=dev, device_id_type=MESH)

    def zcopy(self, i, t, way, dist, zs):
        p = self.p
        x = slice(None) if t == 2 else p.x
        y = slice(None) if t == 3 else p.y
        ref = self.slot(i, t, x, p.c, zs, y)
        src = self.shard.at[i[0], i[1], pl.ds(*PIECES[t])] if t == 4 and dist == 1 else ref
        n = i[0] * CHUNKS + i[1]
        return self.copy(src, ref, self.sz.at[n, SLOT_OF[t], way, dist - 1], self.rz.at[n, SLOT_OF[t], way, dist - 1], p.along_z(way))

    def zsend(self, i, t, way, dist):
        p = self.p
        zs = p.z - (dist - 1) if way == 0 else p.z + (dist - 1)
        ok = p.has_z(way, 1)
        if dist > 1:
            ok = jnp.logical_and(ok, p.has_z(1 - way, dist - 1))
        return ok, lambda: self.zcopy(i, t, way, dist, zs)

    def zrecv(self, i, t, way, dist):
        p = self.p
        zs = p.z - dist if way == 0 else p.z + dist
        return p.has_z(1 - way, dist), lambda: self.zcopy(i, t, way, dist, zs)

    def zstep(self, i, t, dist, after=None):
        for way in (0, 1):
            ok, mk = self.zrecv(i, t, way, dist)

            @pl.when(ok)
            def _():
                mk().wait_recv()
            if dist + 1 < self.p.nz:
                ok2, mk2 = self.zsend(i, t, way, dist + 1)

                @pl.when(ok2)
                def _():
                    mk2().start()
            if after is not None:
                @pl.when(ok)
                def _():
                    after(self.p.z - dist if way == 0 else self.p.z + dist)

    def zfirst(self, i, t):
        for way in (0, 1):
            ok, mk = self.zsend(i, t, way, 1)

            @pl.when(ok)
            def _():
                mk().start()

    def bulk(self, i, t, axis, mine):
        p = self.p
        al = slice(None)
        n = i[0] * CHUNKS + i[1]
        if axis == "c":
            c = p.c if mine else 1 - p.c
            ref, dev, k = self.slot(i, t, al, c, al, al), p.over_c(), 2
        elif axis == "x":
            x = p.x if mine else 1 - p.x
            z = p.z if t == 2 else al
            y = al if t in (1, 3) else p.y
            ref, dev, k = self.slot(i, t, x, p.c, z, y), p.over_x(), 0
        else:
            y = p.y if mine else 1 - p.y
            z = p.z if t == 3 else al
            x = al if t in (0, 2) else p.x
            ref, dev, k = self.slot(i, t, x, p.c, z, y), p.over_y(), 1
        src = self.shard.at[i[0], i[1], pl.ds(*PIECES[t])] if t in (2, 3) else ref
        return self.copy(src, ref, self.sb.at[n, SLOT_OF[t], k], self.rb.at[n, SLOT_OF[t], k], dev)

    def part(self, i, t, nth, q, mine):
        p = self.p
        al = slice(None)
        n = i[0] * CHUNKS + i[1]
        if (t in (0, 2)) == (nth == 2):
            y = p.y if mine else 1 - p.y
            ref, dev = self.slot(i, t, al if nth == 2 else p.x, p.c, q, y), p.over_y()
        else:
            x = p.x if mine else 1 - p.x
            ref, dev = self.slot(i, t, x, p.c, q, al if nth == 2 else p.y), p.over_x()
        return self.copy(ref, ref, self.ps.at[n, t, nth - 1, q], self.pr.at[n, t, nth - 1, q], dev)

    def step(self, grp, st, i):
        if grp == "AB":
            if st == 0:
                self.zfirst(i, 4)
            elif st <= 3:
                self.zstep(i, 4, st)
                if st == 3:
                    self.bulk(i, 0, "x", True).start()
                    self.bulk(i, 1, "y", True).start()
            elif st == 4:
                self.bulk(i, 0, "x", False).wait_recv()
                self.bulk(i, 0, "y", True).start()
                self.bulk(i, 1, "y", False).wait_recv()
                self.bulk(i, 1, "x", True).start()
            elif st == 5:
                self.bulk(i, 0, "y", False).wait_recv()
                self.bulk(i, 1, "x", False).wait_recv()
                self.bulk(i, 4, "c", True).start()
            else:
                self.bulk(i, 4, "c", False).wait_recv()
            return

        def send(t):
            return lambda q: self.part(i, t, 2, q, True).start()
        for t, first in ((2, "x"), (3, "y")):
            if st == 0:
                self.bulk(i, t, first, True).start()
            elif st == 1:
                self.bulk(i, t, first, False).wait_recv()
                self.zfirst(i, t)
                send(t)(self.p.z)
            elif st <= 4:
                self.zstep(i, t, st - 1, send(t))
            elif st == 5:
                for q in range(self.p.nz):
                    self.part(i, t, 2, q, False).wait_recv()
        if st == 5:
            self.bulk(i, 5, "c", True).start()
        elif st == 6:
            self.bulk(i, 5, "c", False).wait_recv()

    def plain_step(self, st, i):
        if st == 0:
            self.zfirst(i, 0)
        elif st <= 3:
            self.zstep(i, 0, st)
            if st == 3:
                self.bulk(i, 0, "x", True).start()
        elif st == 4:
            self.bulk(i, 0, "x", False).wait_recv()
            self.bulk(i, 0, "y", True).start()
        elif st == 5:
            self.bulk(i, 0, "y", False).wait_recv()
            self.bulk(i, 0, "c", True).start()
        else:
            self.bulk(i, 0, "c", False).wait_recv()

    def finish(self, i, types=(4, 2, 3)):
        for t in types:
            if t == 4:
                for k, axis in ((0, "x"), (0, "y"), (1, "x"), (1, "y"), (4, "c"), (5, "c")):
                    self.bulk(i, k, axis, True).wait_send()
            elif t == 0:
                for axis in ("x", "y", "c"):
                    self.bulk(i, t, axis, True).wait_send()
            else:
                self.bulk(i, t, "x" if t == 2 else "y", True).wait_send()
                for q in range(self.p.nz):
                    self.part(i, t, 2, q, True).wait_send()
            for way in (0, 1):
                for dist in range(1, self.p.nz):
                    ok, mk = self.zsend(i, t, way, dist)

                    @pl.when(ok)
                    def _():
                        mk().wait_send()


F32, BF16 = jnp.float32, jnp.bfloat16
HEAD = 64
EPS = 1e-12


def nt(a, b):
    return lax.dot_general(a, b, (((1,), (1,)), ((), ())), preferred_element_type=F32)


def nn(a, b):
    return jnp.dot(a, b, preferred_element_type=F32)


def lane_is(shape, half):
    lane = lax.broadcasted_iota(jnp.int32, shape, len(shape) - 1)
    return (lane < HEAD) if half == 0 else (lane >= HEAD)


def gelu_both(x):
    e = jnp.exp(x * x * -0.5)
    k = 1.0 / (1.0 + (0.3275911 / math.sqrt(2.0)) * jnp.abs(x))
    poly = k * (0.254829592 + k * (-0.284496736 + k * (1.421413741 + k * (-1.453152027 + k * 1.061405429))))
    tail = 0.5 * poly * e
    cdf = jnp.where(x >= 0, 1.0 - tail, tail)
    return x * cdf, cdf + x * (e * (1.0 / math.sqrt(2.0 * math.pi)))


def relay_first(pk, wq, wo, width):
    def body(i, _):
        blk = pk[pl.ds(2 * i, 2)].astype(F32)
        q = jnp.concatenate([blk[0, :72], blk[1, :72]], 0).astype(BF16)
        o = jnp.concatenate([blk[0, 72:], blk[1, 72:]], 0).astype(BF16)
        wq[pl.ds(pl.multiple_of(144 * i, 16), 144), :] = q
        wo[pl.ds(pl.multiple_of(48 * i, 16), 48), :] = o
        return 0
    lax.fori_loop(0, pk.shape[0] // 2, body, 0)


def relay_down(pk, wd, width):
    def body(i, _):
        blk = pk[pl.ds(2 * i, 2)].astype(F32)
        for q in range(4):
            part = jnp.concatenate([blk[0, 24 * q:24 * q + 24], blk[1, 24 * q:24 * q + 24]], 0).astype(BF16)
            wd[pl.ds(pl.multiple_of(48 * i, 16), 48), q * width:(q + 1) * width] = part
        return 0
    lax.fori_loop(0, pk.shape[0] // 2, body, 0)


def project_qkv(xb, wq, bias, out, j, cols):
    sl = slice(j * cols, (j + 1) * cols)
    out[:, sl] = (nt(xb[...], wq[sl, :]) + bias[:, sl]).astype(BF16)


def attend_pair(qkv, key_bias, ctx, lse, i, width):
    a = 128 * i
    q2 = qkv[0:LP, a:a + 128] * jnp.asarray(0.125, BF16)
    k2 = qkv[0:LP, width + a:width + a + 128]
    v2 = qkv[0:LP, 2 * width + a:2 * width + a + 128]
    v2t = v2.T
    parts = []
    for half in (0, 1):
        qm = jnp.where(lane_is(q2.shape, half), q2, jnp.zeros_like(q2))
        s = nt(k2, qm) + key_bias[...]
        m = jnp.max(s, 0, keepdims=True)
        p = jnp.exp(s - m)
        total = jnp.sum(p, 0, keepdims=True)
        pb = (p * (1.0 / total)).astype(BF16)
        lse[2 * i + half] = m + jnp.log(total)
        parts.append(nn(v2t[HEAD * half:HEAD * half + HEAD], pb))
    ctx[0:LP, a:a + 128] = jnp.concatenate(parts, 0).T.astype(BF16)


def query_probs(qkv, query_bias, heads, width):
    rows = qkv.shape[0] - LP
    q = qkv[LP:, 0:width] * jnp.asarray(0.125, BF16)
    lane = lax.broadcasted_iota(jnp.int32, (heads, rows, width), 2)
    head = lax.broadcasted_iota(jnp.int32, (heads, rows, width), 0)
    mine = jnp.logical_and(lane >= head * HEAD, lane < head * HEAD + HEAD)
    qx = jnp.where(mine, q[None].astype(F32), 0.0).astype(BF16).reshape(heads * rows, width)
    s = nt(qx, qkv[LP:, width:2 * width]) + query_bias[...]
    m = jnp.max(s, -1, keepdims=True)
    p = jnp.exp(s - m)
    return mine, p * (1.0 / jnp.sum(p, -1, keepdims=True)), qx


def attend_query(qkv, query_bias, ctx, heads, width):
    rows = qkv.shape[0] - LP
    mine, p, _ = query_probs(qkv, query_bias, heads, width)
    c = nn(p.astype(BF16), qkv[LP:, 2 * width:]).reshape(heads, rows, width)
    ctx[LP:, :] = jnp.sum(jnp.where(mine, c, 0.0), 0).astype(BF16)


def norm_rows(x, o, bias, gain, shift, n_out, r_out, y_out, yb_out, step=32):
    def body(i, _):
        rows = pl.ds(pl.multiple_of(i * step, step), step)
        v = x[rows, :] + o[rows, :] + bias
        c = v - jnp.mean(v, -1, keepdims=True)
        r = lax.rsqrt(jnp.mean(c * c, -1, keepdims=True) + EPS)
        n = c * r
        y = n * gain + shift
        n_out[rows, :] = n
        r_out[rows, :] = jnp.broadcast_to(r, (step, 128))
        y_out[rows, :] = y
        yb_out[rows, :] = y.astype(BF16)
        return 0
    lax.fori_loop(0, x.shape[0] // step, body, 0, unroll=True)


def feed_in(midb, wi, bias, hid, gp, j, cols):
    sl = slice(j * cols, (j + 1) * cols)
    pre = nt(midb[...], wi[sl, :]) + bias[:, sl]
    a, b = gelu_both(pre)
    hid[:, sl] = a.astype(BF16)
    gp[:, sl] = b.astype(BF16)


def project_cols(a, w, out, j, cols):
    sl = slice(j * cols, (j + 1) * cols)
    out[:, sl] = nt(a[...], w[sl, :])


def pool_rows(x, weights, keep, out, depth):
    v = x[...] * weights[...]
    out[depth, 0:1, :] = jnp.sum(v[0:LP], 0, keepdims=True) * keep[depth:depth + 1, :]
    out[depth, 1:2, :] = jnp.sum(v[LP:], 0, keepdims=True) * keep[depth:depth + 1, :]


def spread_small(sg, t24, t96, m24, m96, sp, ib, width):
    dev = sg.shape[0]
    e = nn(sg[...].reshape(dev * 16, 128), t24[...]).reshape(dev, 16, width)
    full = jnp.sum(e * m24[...][:, None, :], 0)
    sp[...] = full
    per = dev // 4
    for j in range(4):
        e = nn(sg[per * j:per * j + per].reshape(per * 16, 128), t96[...]).reshape(per, 16, width)
        ib[:, j * width:(j + 1) * width] = jnp.sum(e * m96[...][:, None, :], 0)


def dead_bias(shape, axis, live):
    return jnp.where(lax.broadcasted_iota(jnp.int32, shape, axis) < live, 0.0, -1e30).astype(F32)


def pool_weights(shape, plen, qlen):
    t = lax.broadcasted_iota(jnp.int32, shape, 0)
    passage = t < LP
    live = jnp.logical_or(jnp.logical_and(passage, t < plen), jnp.logical_and(t >= LP, t < LP + qlen))
    count = jnp.where(passage, plen, qlen).astype(F32)
    return jnp.where(live, 1.0, 0.0) / count


def pack_block(r, l, ch):
    width = r.shard.shape[3]
    if ch == 0:
        r.shard[l, 0] = jnp.concatenate([r.qkv_v[l].astype(F32), r.attn_v[l].astype(F32)], 0).astype(BF16)
    elif ch == 1:
        r.shard[l, 1] = r.in_v[l]
    else:
        d = r.down_v[l].astype(F32)
        r.shard[l, 2] = jnp.concatenate([d[:, q * width:(q + 1) * width] for q in range(4)], 0).astype(BF16)


def pack_small(r):
    r.small32[...] = jnp.zeros_like(r.small32)
    own = r.gains.shape[2]
    for l in range(r.gains.shape[0]):
        r.small32[8 * l:8 * l + 2, 0:own] = r.gains[l].astype(F32)
        r.small32[8 * l + 2:8 * l + 8, 0:own] = r.biases[l].astype(F32)
        r.small32[8 * l:8 * l + 1, 32:32 + 4 * own] = r.in_bias[l:l + 1].astype(F32)
    r.small[...] = r.small32[...].astype(BF16)


VM = pltpu.VMEM


class ForwardRefs:
    def __init__(self, *refs):
        (self.plen, self.qlen, self.units, self.x, self.qkv_w, self.attn_w, self.in_w, self.down_w, self.gains, self.biases, self.in_bias,
         self.t24, self.t96, self.m24, self.m96,
         self.gat, self.sgat, self.wq_o, self.wo_o, self.wd_o, self.sp, self.act, self.pooled, self.xb1_o, self.qkv_o,
         self.lse_o, self.ctx_o, self.n1_o, self.r1_o, self.midb_o, self.gp_o, self.hid_o, self.n2_o, self.r2_o,
         self.pk, self.wq, self.wo, self.wi, self.wd, self.sgv, self.ib, self.bq, self.xf, self.xb, self.qkv, self.lse,
         self.ctx, self.o, self.mid, self.midb, self.hid, self.gp, self.n1, self.r1, self.n2, self.r2, self.sz, self.rz,
         self.sb, self.rb, self.ssz, self.srz, self.ssb, self.srb, self.ps, self.pr, self.local, self.save,
         self.shard, self.small, self.small32, self.kb, self.qb, self.pw, self.keep,
         self.qkv_v, self.attn_v, self.in_v, self.down_v, self.t24_v, self.t96_v, self.m24_v, self.m96_v, self.given) = refs


class SmallGather(Gather):
    def slot(self, i, t, x, c, z, y):
        return self.out.at[x, c, z, y]


def forward_kernel(nz, plan, s_len, width, ff, with_comm, *refs):
    r = ForwardRefs(*refs)
    place = Place(nz)
    p = place
    chunks = [(l, ch) for l in range(LAYERS) for ch in range(CHUNKS)]
    fetched = {}
    for k, (src, dst) in enumerate(((r.qkv_w, r.qkv_v), (r.attn_w, r.attn_v), (r.in_w, r.in_v), (r.down_w, r.down_v), (r.x.at[0], r.xb),
                                    (r.t24, r.t24_v), (r.t96, r.t96_v), (r.m24, r.m24_v), (r.m96, r.m96_v))):
        fetched[k] = pltpu.make_async_copy(src, dst, r.given.at[k])
        fetched[k].start()

    def given(*ks):
        for k in ks:
            if k in fetched:
                fetched.pop(k).wait()

    owned = {}

    def pack(i):
        l, ch = i
        given(*((0, 1), (2,), (3,))[ch])
        pack_block(r, l, ch)
        owned[i] = pltpu.make_async_copy(r.shard.at[l, ch], r.gat.at[l, ch, p.x, p.c, p.z, p.y], r.local.at[3 + l * CHUNKS + ch])
        owned[i].start()

    pack_small(r)
    owns = pltpu.make_async_copy(r.small, r.sgat.at[p.x, p.c, p.z, p.y], r.local.at[1])
    owns.start()
    if with_comm:
        pack(chunks[0])
    r.kb[...] = dead_bias(r.kb.shape, 0, r.plen[0])
    r.qb[...] = dead_bias(r.qb.shape, 1, r.qlen[0])
    r.pw[...] = pool_weights(r.pw.shape, r.plen[0], r.qlen[0])
    for e in range(2):
        lane = lax.broadcasted_iota(jnp.int32, (1, width), 1)
        r.keep[e:e + 1, :] = jnp.where(lane < HEAD * r.units[0, e], 1.0, 0.0).astype(F32)
    entry_barrier(place)
    g = Gather(place, r.shard, r.gat, r.sz, r.rz, r.sb, r.rb, r.ps, r.pr)
    sg = SmallGather(place, r.small, r.sgat, r.ssz, r.srz, r.ssb, r.srb)
    owns.wait()
    pend = {}
    saves = (r.wq_o, r.wo_o, r.wd_o, r.xb1_o, r.qkv_o, r.lse_o, r.ctx_o, r.n1_o, r.r1_o, r.midb_o, r.gp_o, r.hid_o, r.n2_o, r.r2_o)

    def number(out):
        return [k for k, ref in enumerate(saves) if ref is out][0]

    def save(out, ref, l):
        k = number(out)
        cp = pltpu.make_async_copy(ref, out if out is r.xb1_o else out.at[l], r.save.at[k])
        cp.start()
        pend[k] = cp

    def settle(*outs):
        for out in outs:
            cp = pend.pop(number(out), None)
            if cp is not None:
                cp.wait()

    def load(l, ch):
        src = r.gat.at[l, ch]
        dst = r.wi if ch == 1 else r.pk
        return [pltpu.make_async_copy(src, dst, r.local.at[2])]

    def row(k, l):
        return r.sp[8 * l + k:8 * l + k + 1, :]

    def tile(name, l, j):
        if name == "load":
            for cp in load(l, j):
                cp.start()
            if l == 0 and j == 0:
                cp = pltpu.make_async_copy(r.sgat, r.sgv, r.local.at[1])
                cp.start()
        elif name in ("relay", "take"):
            for cp in load(l, j):
                cp.wait()
            if j == 0:
                if l == 0:
                    pltpu.make_async_copy(r.sgat, r.sgv, r.local.at[1]).wait()
                    given(4, 5, 6, 7, 8)
                    spread_small(r.sgv.reshape(8 * nz, 16, 128), r.t24_v, r.t96_v, r.m24_v, r.m96_v, r.sp, r.ib, width)
                    r.xf[...] = r.xb[...].astype(F32)
                settle(r.wq_o, r.wo_o)
                relay_first(r.pk.reshape(8 * nz, ROWS, width), r.wq, r.wo, width)
                save(r.wq_o, r.wq, l)
                save(r.wo_o, r.wo, l)
                r.bq[:, 0:width] = row(2, l)
                r.bq[:, width:2 * width] = jnp.zeros((1, width), F32)
                r.bq[:, 2 * width:] = row(3, l)
            elif j == 2:
                settle(r.wd_o)
                relay_down(r.pk.reshape(8 * nz, ROWS, width), r.wd, width)
                save(r.wd_o, r.wd, l)
        elif name == "qkv":
            if j == 0:
                settle(r.qkv_o)
            project_qkv(r.xb, r.wq, r.bq, r.qkv, j, width)
            if j == 2:
                save(r.qkv_o, r.qkv, l)
                settle(r.lse_o, r.ctx_o)
        elif name == "attend":
            attend_pair(r.qkv, r.kb, r.ctx, r.lse, j, width)
        elif name == "query":
            attend_query(r.qkv, r.qb, r.ctx, HEADS, width)
            save(r.lse_o, r.lse, l)
            save(r.ctx_o, r.ctx, l)
        elif name == "out":
            for q in range(3):
                project_cols(r.ctx, r.wo, r.o, q, 256)
        elif name == "norm" and j == 0:
            settle(r.n1_o, r.r1_o, r.midb_o)
            norm_rows(r.xf, r.o, row(4, l), row(0, l), row(5, l), r.n1, r.r1, r.mid, r.midb)
            save(r.n1_o, r.n1, l)
            save(r.r1_o, r.r1, l)
            save(r.midb_o, r.midb, l)
            settle(r.gp_o, r.hid_o)
        elif name == "in":
            feed_in(r.midb, r.wi.reshape(ff, width), r.ib.at[8 * l:8 * l + 1], r.hid, r.gp, j, ff // 8)
            if j == 7:
                save(r.gp_o, r.gp, l)
                save(r.hid_o, r.hid, l)
        elif name == "down":
            project_cols(r.hid, r.wd, r.o, j, 256)
        elif name == "norm" and j == 1:
            settle(r.n2_o, r.r2_o)
            last = l == LAYERS - 1
            norm_rows(r.mid, r.o, row(6, l), row(1, l), row(7, l), r.n2, r.r2, r.xf, r.act if last else r.xb)
            save(r.n2_o, r.n2, l)
            save(r.r2_o, r.r2, l)
            if not last:
                save(r.xb1_o, r.xb, l)
            pool_rows(r.xf, r.pw, r.keep, r.pooled, l)

    packed = set()
    for kind, a, b, c in plan:
        if kind == 0:
            a = "AB" if a == 0 else "CD"
            if with_comm:
                i = chunks[c]
                if b == 0 and i not in packed:
                    packed.add(i)
                    if c > 0:
                        pack(i)
                if b > 0 and i in owned and (a == "CD" or b == 3):
                    owned.pop(i).wait()
                g.step(a, b, i)
                if c == 0 and a == "AB":
                    sg.plain_step(b, i)
        elif kind == 2:
            if with_comm:
                g.finish(chunks[c])
        else:
            tile(FORWARD_NAMES[a], b, c)
    given(*range(9))
    settle(*saves)
    if with_comm:
        sg.finish(chunks[0], types=(0,))


def forward_call(plan, nz, args, cid=0, with_comm=True):
    s_len, width = args[3].shape[1:]
    ff = 4 * width
    dev = 8 * nz
    n = LAYERS * CHUNKS
    any_, vm, sm = (pl.BlockSpec(memory_space=m) for m in (pl.ANY, pltpu.VMEM, pltpu.SMEM))
    sds = jax.ShapeDtypeStruct
    L = LAYERS
    outs = [
        (sds((L, CHUNKS, 2, 2, nz, 2, ROWS, width), BF16), any_), (sds((2, 2, nz, 2, 16, 128), BF16), any_),
        (sds((L, 3 * width, width), BF16), any_), (sds((L, width, width), BF16), any_), (sds((L, width, ff), BF16), any_),
        (sds((16, width), F32), vm), (sds((s_len, width), BF16), vm), (sds((2, 2, width), F32), vm),
        (sds((s_len, width), BF16), any_), (sds((L, s_len, 3 * width), BF16), any_), (sds((L, HEADS, 1, LP), F32), any_),
        (sds((L, s_len, width), BF16), any_), (sds((L, s_len, width), F32), any_), (sds((L, s_len, 128), F32), any_),
        (sds((L, s_len, width), BF16), any_), (sds((L, s_len, ff), BF16), any_), (sds((L, s_len, ff), BF16), any_),
        (sds((L, s_len, width), F32), any_), (sds((L, s_len, 128), F32), any_),
    ]
    dma = pltpu.SemaphoreType.DMA
    scratch = [
        VM((2, 2, nz, 2, ROWS, width), BF16), VM((3 * width, width), BF16), VM((width, width), BF16), VM((2, 2, nz, 2, ROWS, width), BF16), VM((width, ff), BF16),
        VM((2, 2, nz, 2, 16, 128), BF16), VM((16, ff), F32), VM((1, 3 * width), F32),
        VM((s_len, width), F32), VM((s_len, width), BF16), VM((s_len, 3 * width), BF16), VM((HEADS, 1, LP), F32),
        VM((s_len, width), BF16), VM((s_len, width), F32), VM((s_len, width), F32), VM((s_len, width), BF16),
        VM((s_len, ff), BF16), VM((s_len, ff), BF16),
        VM((s_len, width), F32), VM((s_len, 128), F32), VM((s_len, width), F32), VM((s_len, 128), F32),
        dma((n, 4, 2, nz - 1)), dma((n, 4, 2, nz - 1)), dma((n, 4, 3)), dma((n, 4, 3)),
        dma((1, 1, 2, nz - 1)), dma((1, 1, 2, nz - 1)), dma((1, 1, 3)), dma((1, 1, 3)),
        dma((n, 4, 2, nz)), dma((n, 4, 2, nz)), dma((3 + n,)), dma((14,)),
        VM((L, CHUNKS, ROWS, width), BF16), VM((16, 128), BF16), VM((16, 128), F32),
        VM((LP, 1), F32), VM((1, s_len - LP), F32), VM((s_len, 1), F32), VM((2, width), F32),
        VM(args[4].shape, BF16), VM(args[5].shape, BF16), VM(args[6].shape, BF16), VM(args[7].shape, BF16),
        VM(args[11].shape, BF16), VM(args[12].shape, BF16), VM(args[13].shape, F32), VM(args[14].shape, F32), dma((9,)),
    ]
    return pl.pallas_call(
        functools.partial(forward_kernel, nz, plan, s_len, width, ff, with_comm),
        out_shape=[o[0] for o in outs],
        in_specs=[sm] * 3 + [any_] * 5 + [vm] * 3 + [any_] * 4,
        out_specs=[o[1] for o in outs],
        scratch_shapes=scratch,
        compiler_params=pltpu.CompilerParams(collective_id=cid, has_side_effects=True, vmem_limit_bytes=60 << 20),
        name="gather_forward",
    )(*args)


BACK_CHUNKS = tuple((l, ch) for l in (1, 0) for ch in (2, 1, 0))


def fold8(v):
    return jnp.sum(v.reshape(v.shape[0] // 8, 8, v.shape[1]), 0)


def col_total(v):
    return jnp.sum(v, 0, keepdims=True)


def norm_back(sources, n_ref, r_ref, gain, d_ref, db_ref, step=32):
    width = n_ref.shape[1]

    def body(i, carry):
        s0, s1, s2 = carry
        rows = pl.ds(pl.multiple_of(i * step, step), step)
        g = sources[0][rows, :]
        for other in sources[1:]:
            g = g + other[rows, :]
        n = n_ref[rows, :]
        e = g * gain
        d = r_ref[rows, 0:1] * (e - jnp.mean(e, -1, keepdims=True) - n * jnp.mean(e * n, -1, keepdims=True))
        db = d.astype(BF16)
        d_ref[rows, :] = d
        db_ref[rows, :] = db
        return s0 + fold8(g * n), s1 + fold8(g), s2 + fold8(db.astype(F32))
    zero = jnp.zeros((8, width), F32)
    out = lax.fori_loop(0, n_ref.shape[0] // step, body, (zero, zero, zero), unroll=True)
    return [col_total(v) for v in out]


def attend_pair_back(qkv, key_bias, lse, dctx, dqkv, i, width):
    a = 128 * i
    scale = jnp.asarray(0.125, BF16)
    q2 = qkv[0:LP, a:a + 128] * scale
    k2 = qkv[0:LP, width + a:width + a + 128]
    v2 = qkv[0:LP, 2 * width + a:2 * width + a + 128]
    c2 = dctx[0:LP, a:a + 128]
    k2t = k2.T
    dqs, dks, dvs = [], [], []
    for half in (0, 1):
        mine = lane_is(q2.shape, half)
        qm = jnp.where(mine, q2, jnp.zeros_like(q2))
        cm = jnp.where(mine, c2, jnp.zeros_like(c2))
        p = jnp.exp(nt(k2, qm) + key_bias[...] - lse[2 * i + half])
        dp = nt(v2, cm)
        dvs.append(nn(p.astype(BF16), c2))
        t = p * dp
        ds = (t - p * jnp.sum(t, 0, keepdims=True)).astype(BF16)
        dks.append(nn(ds, q2))
        dqs.append(nn(k2t[HEAD * half:HEAD * half + HEAD], ds))
    first = lane_is(q2.shape, 0)
    dqkv[0:LP, a:a + 128] = (jnp.concatenate(dqs, 0).T * 0.125).astype(BF16)
    dqkv[0:LP, width + a:width + a + 128] = jnp.where(first, dks[0], dks[1]).astype(BF16)
    dqkv[0:LP, 2 * width + a:2 * width + a + 128] = jnp.where(first, dvs[0], dvs[1]).astype(BF16)


def attend_query_back(qkv, query_bias, dctx, dqkv, heads, width):
    rows = qkv.shape[0] - LP
    mine, p, qx = query_probs(qkv, query_bias, heads, width)
    k, v = qkv[LP:, width:2 * width], qkv[LP:, 2 * width:3 * width]
    cx = jnp.where(mine, dctx[LP:, :][None].astype(F32), 0.0).astype(BF16).reshape(heads * rows, width)
    dp = nt(cx, v)
    ds = (p * (dp - jnp.sum(p * dp, -1, keepdims=True)))
    dsb = ds.astype(BF16)
    dq = jnp.sum(jnp.where(mine, nn(dsb, k).reshape(heads, rows, width), 0.0), 0) * 0.125
    dqkv[LP:, 0:width] = dq.astype(BF16)
    dqkv[LP:, width:2 * width] = nn(ds.T.astype(BF16), qx).astype(BF16)
    dqkv[LP:, 2 * width:] = nn(p.T.astype(BF16), cx).astype(BF16)


class Scatter:
    def __init__(self, place, G, LC, LA, LB, L2, LZ, sends, recvs, zs, zr, fs, fr, cred, total):
        self.p, self.fs, self.fr = place, fs, fr
        self.G, self.LC, self.LA, self.LB, self.L2, self.LZ = G, LC, LA, LB, L2, LZ
        self.sends, self.recvs, self.zs, self.zr, self.cred, self.total = sends, recvs, zs, zr, cred, total
        self.waited = set()

    def copy(self, src, dst, s, r, dev):
        return pltpu.make_async_remote_copy(
            src_ref=src, dst_ref=dst, send_sem=s, recv_sem=r, device_id=dev, device_id_type=MESH)

    def credit(self, i, k):
        if i < 2 or (i, k) in self.waited:
            return
        self.waited.add((i, k))
        if k < 3:
            pl.semaphore_wait(self.cred.at[k], 1)
        else:
            @pl.when(self.p.has_z(k - 3, 1))
            def _():
                pl.semaphore_wait(self.cred.at[k], 1)

    def give_credits(self):
        p = self.p
        for k, dev in enumerate((p.over_c(), p.over_x(), p.over_y())):
            pl.semaphore_signal(self.cred.at[k], inc=1, device_id=dev, device_id_type=MESH)
        for way in (0, 1):
            @pl.when(p.has_z(1 - way, 1))
            def _():
                pl.semaphore_signal(self.cred.at[3 + way], inc=1, device_id=p.along_z(1 - way), device_id_type=MESH)

    def rows(self, t):
        return pl.ds(*PIECES[t])

    def landing(self, t):
        lo, n = PIECES[t]
        return pl.ds(0 if t < 2 else 16, n)

    def core_copy(self, i, grp):
        s, p = i % 2, self.p
        rows = pl.ds(0, 32) if grp == "AB" else pl.ds(32, 64)
        k = 0 if grp == "AB" else 1
        return self.copy(self.G.at[s, :, 1 - p.c, :, :, rows], self.LC.at[s, :, :, :, rows],
                         self.sends.at[s, k], self.recvs.at[s, k], p.over_c())

    def first_copy(self, i, t):
        s, p = i % 2, self.p
        al = slice(None)
        if t in (0, 2):
            return self.copy(self.G.at[s, :, p.c, :, 1 - p.y, self.rows(t)], self.LA.at[s, :, :, self.landing(t)],
                             self.sends.at[s, 2 + t], self.recvs.at[s, 2 + t], p.over_y())
        return self.copy(self.G.at[s, 1 - p.x, p.c, :, :, self.rows(t)], self.LB.at[s, :, :, self.landing(t)],
                         self.sends.at[s, 2 + t], self.recvs.at[s, 2 + t], p.over_x())

    def second_copy(self, i, t):
        s, p = i % 2, self.p
        sem = (self.sends.at[s, 6 + t], self.recvs.at[s, 6 + t])
        if t == 0:
            return self.copy(self.G.at[s, 1 - p.x, p.c, :, p.y, self.rows(t)], self.L2.at[s, :, self.rows(t)], *sem, p.over_x())
        if t == 1:
            return self.copy(self.G.at[s, p.x, p.c, :, 1 - p.y, self.rows(t)], self.L2.at[s, :, self.rows(t)], *sem, p.over_y())
        if t == 2:
            return self.copy(self.G.at[s, 1 - p.x, p.c, p.z, p.y, self.rows(t)], self.L2.at[s, 0, self.rows(t)], *sem, p.over_x())
        return self.copy(self.G.at[s, p.x, p.c, p.z, 1 - p.y, self.rows(t)], self.L2.at[s, 0, self.rows(t)], *sem, p.over_y())

    def plane(self, s, t, z):
        p = self.p
        if t == 2:
            return self.G.at[s, :, p.c, z, p.y, self.rows(t)]
        if t == 3:
            return self.G.at[s, p.x, p.c, z, :, self.rows(t)]
        return self.G.at[s, p.x, p.c, z, p.y, self.rows(t)]

    def zland(self, s, t, way, k):
        if t == 4:
            return self.LZ.at[s, way, k, 0, self.rows(t)]
        return self.LZ.at[s, way, k, :, self.rows(t)]

    def zcopy(self, i, t, way, k, zt):
        s = i % 2
        return self.copy(self.plane(s, t, zt), self.zland(s, t, way, k),
                         self.zs.at[s, SLOT_OF[t], way, k], self.zr.at[s, SLOT_OF[t], way, k], self.p.along_z(way))

    def ztarget(self, way, k):
        m = self.p.nz - 1 - k
        return self.p.z + m if way == 0 else self.p.z - m

    def zsend_ok(self, way, k):
        return self.p.has_z(way, self.p.nz - 1 - k)

    def zstep(self, i, t, k):
        p, s = self.p, i % 2
        for way in (0, 1):
            if k >= 1:
                ok = p.has_z(1 - way, 1)
                if k < p.nz - 1:
                    ok = jnp.logical_and(ok, p.has_z(way, p.nz - 1 - k))
                zt = self.ztarget(way, k)

                @pl.when(ok)
                def _():
                    self.zcopy(i, t, way, k - 1, zt).wait_recv()
                    ref, add = self.plane(s, t, zt), self.zland(s, t, way, k - 1)
                    ref[...] = ref[...] + add[...]
            if k <= p.nz - 2:
                self.credit(i, 3 + way)
                zt2 = self.ztarget(way, k)

                @pl.when(self.zsend_ok(way, k))
                def _():
                    self.zcopy(i, t, way, k, zt2).start()

    def step(self, grp, st, i):
        p, s = self.p, i % 2
        types = (0, 1) if grp == "AB" else (2, 3)
        if st == 0:
            self.credit(i, 0)
            self.core_copy(i, grp).start()
            return
        if st == 1:
            self.core_copy(i, grp).wait_recv()
            lo, n = (0, 32) if grp == "AB" else (32, 64)
            rows = pl.ds(lo, n)

            def add(z, _):
                for x in (0, 1):
                    for y in (0, 1):
                        self.G[s, x, p.c, z, y, rows] = self.G[s, x, p.c, z, y, rows] + self.LC[s, x, z, y, rows]
                return 0
            lax.fori_loop(0, p.nz, add, 0)
            self.credit(i, 1)
            self.credit(i, 2)
            if grp == "AB":
                for t in types:
                    self.first_copy(i, t).start()
            else:
                for k in range(p.nz - 1, -1, -1):
                    for t in types:
                        self.by_distance(k, lambda q: self.part(i, t, q).start())
            return
        if grp == "AB":
            if st == 2:
                for t in types:
                    rows, land = self.rows(t), self.landing(t)
                    self.first_copy(i, t).wait_recv()

                    def add(z, _):
                        for o in (0, 1):
                            if t == 0:
                                self.G[s, o, p.c, z, p.y, rows] = self.G[s, o, p.c, z, p.y, rows] + self.LA[s, o, z, land]
                            else:
                                self.G[s, p.x, p.c, z, o, rows] = self.G[s, p.x, p.c, z, o, rows] + self.LB[s, z, o, land]
                        return 0
                    lax.fori_loop(0, p.nz, add, 0)
                    self.second_copy(i, t).start()
                return
            if st == 3:
                for t in types:
                    self.second_copy(i, t).wait_recv()
                rows = self.rows(4)

                def add2(z, _):
                    self.G[s, p.x, p.c, z, p.y, rows] = self.G[s, p.x, p.c, z, p.y, rows] + self.L2[s, z, rows]
                    return 0
                lax.fori_loop(0, p.nz, add2, 0)
            self.zstep(i, 4, st - 3)
            if st == 6:
                rows = self.rows(4)
                self.total[s, rows, :] = self.G[s, p.x, p.c, p.z, p.y, rows].astype(F32)
            return
        for t in types:
            rows = self.rows(t)
            if st <= 5:
                self.by_distance(p.nz - 1 - (st - 2), lambda q: self.take_first(i, t, q))
                self.zstep(i, t, st - 2)
            if st == 5:
                self.second_copy(i, t).start()
            if st == 6:
                self.second_copy(i, t).wait_recv()
                self.total[s, rows, :] = self.G[s, p.x, p.c, p.z, p.y, rows].astype(F32) + self.L2[s, 0, rows].astype(F32)

    def part(self, i, t, q):
        s, p = i % 2, self.p
        rows, land = self.rows(t), self.landing(t)
        sem = (self.fs.at[s, t - 2, q], self.fr.at[s, t - 2, q])
        if t == 2:
            return self.copy(self.G.at[s, :, p.c, q, 1 - p.y, rows], self.LA.at[s, :, q, land], *sem, p.over_y())
        return self.copy(self.G.at[s, 1 - p.x, p.c, q, :, rows], self.LB.at[s, q, :, land], *sem, p.over_x())

    def take_first(self, i, t, q):
        s, p = i % 2, self.p
        rows, land = self.rows(t), self.landing(t)
        self.part(i, t, q).wait_recv()
        for o in (0, 1):
            if t == 2:
                self.G[s, o, p.c, q, p.y, rows] = self.G[s, o, p.c, q, p.y, rows] + self.LA[s, o, q, land]
            else:
                self.G[s, p.x, p.c, q, o, rows] = self.G[s, p.x, p.c, q, o, rows] + self.LB[s, q, o, land]

    def by_distance(self, k, run):
        p = self.p
        if k == 0:
            run(p.z)
            return
        for way in (0, 1):
            @pl.when(p.has_z(way, k))
            def _():
                run(p.z + k if way == 0 else p.z - k)

    def finish(self, i):
        for grp in ("AB", "CD"):
            self.core_copy(i, grp).wait_send()
        for t in range(4):
            if t < 2:
                self.first_copy(i, t).wait_send()
            else:
                for q in range(self.p.nz):
                    self.part(i, t, q).wait_send()
            self.second_copy(i, t).wait_send()
        for t in (4, 2, 3):
            for way in (0, 1):
                for k in range(self.p.nz - 1):
                    @pl.when(self.zsend_ok(way, k))
                    def _():
                        self.zcopy(i, t, way, k, self.ztarget(way, k)).wait_send()


class SmallSum:
    def __init__(self, place, acc, land, ss, rs):
        self.p, self.acc, self.land, self.ss, self.rs = place, acc, land, ss, rs

    def partner(self, k):
        p = self.p
        if k < 3:
            return (p.over_c, p.over_y, p.over_x)[k]()
        d = 1 << (k - 3)
        return p.device(z=p.z + d - 2 * d * lax.rem(p.z // d, 2))

    def copy(self, l, k):
        return pltpu.make_async_remote_copy(
            src_ref=self.acc.at[l, k], dst_ref=self.land.at[l, k], send_sem=self.ss.at[l, k], recv_sem=self.rs.at[l, k],
            device_id=self.partner(k), device_id_type=MESH)

    def step(self, l, k):
        if k > 0:
            self.copy(l, k - 1).wait_recv()
            self.acc[l, k] = self.acc[l, k - 1] + self.land[l, k - 1]
        if k < 5:
            self.copy(l, k).start()

    def finish(self, l):
        for k in range(5):
            self.copy(l, k).wait_send()


def backward_barrier(place, far):
    bar = pltpu.get_barrier_semaphore()
    for dev in (place.over_x(), place.over_y(), place.over_c(), far):
        pl.semaphore_signal(bar, inc=1, device_id=dev, device_id_type=MESH)
    for way in (0, 1):
        @pl.when(place.has_z(way, 1))
        def _():
            pl.semaphore_signal(bar, inc=1, device_id=place.along_z(way), device_id_type=MESH)
    pl.semaphore_wait(bar, 4 + place.has_z(0, 1).astype(jnp.int32) + place.has_z(1, 1).astype(jnp.int32))


class Refs:
    def __init__(self, *refs):
        (self.plen, self.qlen, self.sp, self.og, self.wq_h, self.wo_h, self.wd_h, self.wi_h, self.xb0_h, self.xb1_h, self.qkv_h, self.lse_h,
         self.ctx_h, self.n1_h, self.r1_h, self.midb_h, self.gp_h, self.hid_h, self.n2_h, self.r2_h,
         self.dx_h, self.owned, self.smalls,
         self.G, self.LC, self.LA, self.LB, self.L2, self.LZ, self.total, self.sacc, self.sland,
         self.wd, self.wi, self.gp, self.wo, self.wq, self.g, self.da, self.db, self.n, self.r, self.low, self.lowt,
         self.x1, self.ctx, self.u1, self.dqkv, self.gattn, self.lse,
         self.kb, self.qb, self.sends, self.recvs, self.zs, self.zr, self.fs, self.fr, self.cred, self.ss, self.rs, self.sem) = refs


FETCHES = ("n2", "r2", "n1", "r1", "og", "hid", "qkv", "midb", "xb", "ctx", "wo", "wq", "lse", "out",
           "wd0", "wd1", "wi0", "wi1", "gp0", "gp1")


def backward_kernel(nz, plan, width, ff, with_comm, *refs):
    r = Refs(*refs)
    place = Place(nz)
    p = place
    sc = Scatter(place, r.G, r.LC, r.LA, r.LB, r.L2, r.LZ, r.sends, r.recvs, r.zs, r.zr, r.fs, r.fr, r.cred, r.total)
    ssum = SmallSum(place, r.sacc, r.sland, r.ss, r.rs)
    pend = {}

    def fetch(name, l):
        if l < 0:
            return
        src, dst = {
            "n2": lambda: (r.n2_h.at[l], r.n), "r2": lambda: (r.r2_h.at[l], r.r), "n1": lambda: (r.n1_h.at[l], r.n), "r1": lambda: (r.r1_h.at[l], r.r),
            "og": lambda: (r.og.at[0], r.low), "hid": lambda: (r.hid_h.at[l], r.u1), "qkv": lambda: (r.qkv_h.at[l], r.u1.at[:, 0:3 * width]),
            "midb": lambda: (r.midb_h.at[l], r.x1), "xb": lambda: (r.xb1_h if l == 1 else r.xb0_h.at[0], r.x1), "ctx": lambda: (r.ctx_h.at[l], r.ctx),
            "wo": lambda: (r.wo_h.at[l], r.wo), "wq": lambda: (r.wq_h.at[l], r.wq), "lse": lambda: (r.lse_h.at[l], r.lse),
        }[name]()
        cp = pltpu.make_async_copy(src, dst, r.sem.at[FETCHES.index(name)])
        cp.start()
        pend[name] = cp

    def fetch_tile(l, j):
        if l < 0:
            return
        s = j % 2
        cols = slice(j * width, (j + 1) * width)
        for name, src, dst in (("wd", r.wd_h.at[l, :, cols], r.wd.at[s]), ("wi", r.wi_h.at[l, 1, j // 2, j % 2], r.wi.at[s]), ("gp", r.gp_h.at[l, :, cols], r.gp.at[s])):
            key = name + str(s)
            cp = pltpu.make_async_copy(src, dst, r.sem.at[FETCHES.index(key)])
            cp.start()
            pend[key] = cp

    def need(*names):
        for name in names:
            pend.pop(name).wait()

    r.kb[...] = dead_bias((LP, 1), 0, r.plen[0])
    r.qb[...] = dead_bias(r.qb.shape, 1, r.qlen[0])
    last = LAYERS - 1
    fetch("og", last); fetch("n2", last); fetch("r2", last); fetch("hid", last)
    fetch_tile(last, 0); fetch_tile(last, 1)
    fetch("midb", last); fetch("ctx", last); fetch("wo", last); fetch("wq", last)
    if with_comm:
        backward_barrier(place, ssum.partner(4))

    def gain(k, l):
        return r.sp[8 * l + k:8 * l + k + 1, :]

    def keep(l, k, v):
        r.sacc[l, 0, k:k + 1, :] = v

    def tile(name, l, j):
        if name == "norm" and j == 1:
            if l == last:
                need("og")
                r.g[...] = r.low[...].astype(F32)
            need("n2", "r2")
            gn, gs, ds = norm_back([r.g], r.n, r.r, gain(1, l), r.da, r.low)
            keep(l, 1, gn); keep(l, 7, gs); keep(l, 6, ds)
            r.lowt[...] = r.low[...].T
            fetch("n1", l); fetch("r1", l)
            need("hid")
        elif name == "gdown":
            a, b = j // 2, j % 2
            s = BACK_CHUNKS.index((l, 2)) % 2
            h = width // 2
            res = nn(r.lowt[a * h:(a + 1) * h, :], r.u1[:, 2 * b * width:2 * (b + 1) * width])
            res = res.reshape(4 * nz, h // (4 * nz), 2 * width)
            res = jnp.concatenate([res[:, :, :width], res[:, :, width:]], 1).astype(BF16)
            n = ROWS // 2
            r.G[s, a, :, :, :, b * n:(b + 1) * n, :] = res.reshape(2, nz, 2, n, width)
            if j == 3:
                fetch("qkv", l)
        elif name == "ff":
            s = BACK_CHUNKS.index((l, 1)) % 2
            k = j % 2
            if j == 0:
                need("midb")
            need("wd" + str(k), "gp" + str(k))
            dpre = (nn(r.low[...], r.wd[k]) * r.gp[k].astype(F32)).astype(BF16)
            keep(l, 8 + j, col_total(dpre.astype(F32)))
            r.G[s, j // 2, j % 2] = nn(dpre.T, r.x1[...]).astype(BF16).reshape(nz, 2, ROWS, width)
            need("wi" + str(k))
            wi = r.wi[k].reshape(width, width)
            if j == 0:
                r.db[...] = nn(dpre, wi)
            else:
                r.db[...] = r.db[...] + nn(dpre, wi)
            if j + 2 < 4:
                fetch_tile(l, j + 2)
            else:
                fetch_tile(l - 1, j - 2)
            if j == 3:
                fetch("xb", l)
        elif name == "norm" and j == 0:
            need("n1", "r1")
            gn, gs, ds = norm_back([r.da, r.db], r.n, r.r, gain(0, l), r.da, r.low)
            keep(l, 0, gn); keep(l, 5, gs); keep(l, 4, ds)
            r.lowt[...] = r.low[...].T
            fetch("n2", l - 1); fetch("r2", l - 1)
        elif name == "gattn":
            need("ctx")
            r.gattn[...] = nn(r.lowt[...], r.ctx[...]).astype(BF16)
        elif name == "dctx":
            need("wo")
            r.ctx[...] = nn(r.low[...], r.wo[...]).astype(BF16)
            fetch("wo", l - 1)
            need("qkv")
            fetch("lse", l)
            need("lse")
        elif name == "attend":
            attend_pair_back(r.u1, r.kb, r.lse, r.ctx, r.dqkv, j, width)
        elif name == "query":
            attend_query_back(r.u1, r.qb, r.ctx, r.dqkv, HEADS, width)
            fetch("hid", l - 1); fetch("ctx", l - 1)
            keep(l, 2, col_total(r.dqkv[:, 0:width].astype(F32)))
            keep(l, 3, col_total(r.dqkv[:, 2 * width:].astype(F32)))
            need("xb")
        elif name == "gqkv":
            s = BACK_CHUNKS.index((l, 0)) % 2
            n = 3 * width // 2
            res = nn(r.dqkv[:, j * n:(j + 1) * n].T, r.x1[...]).reshape(4 * nz, n // (4 * nz), width)
            m = width // 2
            att = r.gattn[j * m:(j + 1) * m, :].astype(F32).reshape(4 * nz, m // (4 * nz), width)
            r.G[s, j] = jnp.concatenate([res, att], 1).astype(BF16).reshape(2, nz, 2, ROWS, width)
            if j == 1:
                fetch("midb", l - 1)
        elif name == "dx":
            need("wq")
            r.g[...] = r.da[...] + nn(r.dqkv[...], r.wq[...])
            fetch("wq", l - 1)
            if l == 0:
                r.low[...] = r.g[...].astype(BF16)
                cp = pltpu.make_async_copy(r.low, r.dx_h, r.sem.at[FETCHES.index("out")])
                cp.start()
                pend["out"] = cp
        elif name == "small":
            r.sacc[l, 0, 12:16, :] = jnp.zeros((4, width), F32)

    def finish(i):
        sc.finish(i)
        if i + 2 < len(BACK_CHUNKS):
            sc.give_credits()
        l, ch = BACK_CHUNKS[i]
        r.owned[l, ch] = r.total[i % 2]

    for kind, a, b, c in plan:
        if kind == 1:
            tile(BACKWARD_NAMES[a], b, c)
        elif with_comm:
            if kind == 0:
                sc.step("AB" if a == 0 else "CD", b, c)
            elif kind == 2:
                finish(c)
            elif kind == 3:
                ssum.step(b, c)
    if with_comm:
        for l in range(LAYERS):
            ssum.finish(l)
            r.smalls[l] = r.sacc[l, 5]
    need(*list(pend))


def backward_call(plan, nz, args, cid=1, with_comm=True):
    s_len, width = args[3].shape[1:]
    ff = 4 * width
    dev = 8 * nz
    any_, vm, sm = (pl.BlockSpec(memory_space=m) for m in (pl.ANY, pltpu.VMEM, pltpu.SMEM))
    sds = jax.ShapeDtypeStruct
    L = LAYERS
    outs = [(sds((s_len, width), BF16), any_), (sds((L, CHUNKS, ROWS, width), F32), vm), (sds((L, 16, width), F32), vm)]
    dma = pltpu.SemaphoreType.DMA
    scratch = [
        VM((2, 2, 2, nz, 2, ROWS, width), BF16), VM((2, 2, nz, 2, ROWS, width), BF16),
        VM((2, 2, nz, ROWS // 2, width), BF16), VM((2, nz, 2, ROWS // 2, width), BF16), VM((2, nz, ROWS, width), BF16),
        VM((2, 2, nz - 1, 2, ROWS, width), BF16), VM((2, ROWS, width), F32),
        VM((L, 6, 16, width), F32), VM((L, 5, 16, width), F32),
        VM((2, width, width), BF16), VM((2, nz, 2, ROWS, width), BF16), VM((2, s_len, width), BF16), VM((width, width), BF16), VM((3 * width, width), BF16),
        VM((s_len, width), F32), VM((s_len, width), F32), VM((s_len, width), F32), VM((s_len, width), F32), VM((s_len, 128), F32),
        VM((s_len, width), BF16), VM((width, s_len), BF16), VM((s_len, width), BF16), VM((s_len, width), BF16), VM((s_len, ff), BF16),
        VM((s_len, 3 * width), BF16), VM((width, width), BF16), VM((HEADS, 1, LP), F32),
        VM((LP, 1), F32), VM((1, s_len - LP), F32),
        dma((2, 10)), dma((2, 10)), dma((2, 4, 2, nz - 1)), dma((2, 4, 2, nz - 1)), dma((2, 2, nz)), dma((2, 2, nz)), pltpu.SemaphoreType.REGULAR((5,)),
        dma((L, 5)), dma((L, 5)), dma((len(FETCHES),)),
    ]
    return pl.pallas_call(
        functools.partial(backward_kernel, nz, plan, width, ff, with_comm),
        out_shape=[o[0] for o in outs],
        in_specs=[sm, sm, vm] + [any_] * 17,
        out_specs=[o[1] for o in outs],
        scratch_shapes=scratch,
        compiler_params=pltpu.CompilerParams(collective_id=cid if with_comm else None, has_side_effects=True, vmem_limit_bytes=63 << 20),
        name="backward_scatter",
    )(*args)


def hand_out_kernel(dev, act, pooled, dx, owned, smalls, act_o, pooled_o, dx_o, gq, ga, gi, gd, gains, biases, in_bias):
    me = lax.axis_index("dp") * (dev // 4) + lax.axis_index("fsdp")
    width = act.shape[1]
    own = width // dev
    act_o[0] = act[...]
    pooled_o[0] = pooled[...]
    dx_o[0] = dx[...]
    for l in range(LAYERS):
        gq[l] = owned[l, 0, 0:3 * own, :]
        ga[l] = owned[l, 0, 3 * own:, :]
        gi[l] = owned[l, 1]
        for q in range(4):
            gd[l, :, q * width:(q + 1) * width] = owned[l, 2, q * own:(q + 1) * own, :]
        turned = pltpu.roll(smalls[l, 0:8, :], lax.rem(width - own * me, width), 1)
        gains[l] = turned[0:2, 0:own]
        biases[l] = turned[2:8, 0:own]
        per = dev // 4
        row = smalls[l, pl.ds(8 + me // per, 1), :]
        turned = pltpu.roll(row, lax.rem(width - 4 * own * lax.rem(me, per), width), 1)
        in_bias[l:l + 1, :] = turned[:, 0:4 * own]


def hand_out(dev, act, pooled, dx, owned, smalls):
    s_len, width = act.shape
    own = width // dev
    sds = jax.ShapeDtypeStruct
    L = LAYERS
    outs = [sds((1, s_len, width), BF16), sds((1, 2, 2, width), F32), sds((1, s_len, width), BF16),
            sds((L, 3 * own, width), F32), sds((L, own, width), F32), sds((L, 4 * own, width), F32), sds((L, own, 4 * width), F32),
            sds((L, 2, own), F32), sds((L, 6, own), F32), sds((L, 4 * own), F32)]
    vm = pl.BlockSpec(memory_space=pltpu.VMEM)
    return pl.pallas_call(functools.partial(hand_out_kernel, dev), out_shape=outs, in_specs=[vm] * 5, out_specs=[vm] * len(outs),
                          compiler_params=pltpu.CompilerParams(vmem_limit_bytes=32 << 20), name="hand_out")(act, pooled, dx, owned, smalls)

F32, BF16 = jnp.float32, jnp.bfloat16
def spread_tables(dev, width):
    n = np.arange(width)
    per = width // dev
    t24 = np.zeros((128, width), np.float32); t24[n % per, n] = 1
    t96 = np.zeros((128, width), np.float32); t96[32 + n % (4 * per), n] = 1
    m24 = (n[None] // per == np.arange(dev)[:, None]).astype(np.float32)
    m96 = (n[None] // (4 * per) == np.arange(dev // 4)[:, None]).astype(np.float32)
    return jnp.asarray(t24, BF16), jnp.asarray(t96, BF16), jnp.asarray(m24), jnp.asarray(m96)


FORWARD_NAMES = ("load", "relay", "take", "qkv", "attend", "query", "out", "norm", "in", "down")
BACKWARD_NAMES = ("norm", "gdown", "ff", "gattn", "dctx", "attend", "query", "gqkv", "dx", "small")
FORWARD_PLAN = (
    (0, 0, 0, 0), (0, 1, 0, 0), (0, 0, 0, 5), (0, 0, 0, 1), (0, 0, 1, 0), (0, 1, 1, 0), (0, 1, 0, 1), (0, 1, 0, 2),
    (0, 0, 2, 0), (0, 0, 3, 0), (0, 1, 2, 0), (0, 0, 0, 2), (0, 1, 3, 0), (0, 0, 1, 1), (0, 1, 0, 3), (0, 0, 1, 2),
    (0, 0, 4, 0), (0, 0, 2, 2), (0, 0, 2, 1), (0, 1, 1, 1), (0, 1, 4, 0), (0, 0, 3, 2), (0, 0, 3, 1), (0, 0, 0, 3),
    (0, 1, 5, 0), (0, 1, 2, 1), (0, 0, 5, 0), (0, 0, 1, 3), (0, 1, 6, 0), (0, 0, 4, 1), (0, 1, 3, 1), (0, 0, 6, 0),
    (0, 1, 1, 2), (0, 0, 0, 4), (1, 0, 0, 0), (1, 1, 0, 0), (1, 3, 0, 0), (0, 0, 2, 3), (0, 1, 4, 1), (0, 0, 4, 2),
    (1, 3, 0, 1), (1, 3, 0, 2), (1, 4, 0, 0), (0, 1, 1, 3), (0, 0, 5, 1), (2, 0, 0, 0), (1, 4, 0, 1), (0, 1, 2, 2),
    (0, 1, 5, 1), (1, 4, 0, 2), (0, 1, 6, 1), (1, 4, 0, 3), (1, 4, 0, 4), (0, 0, 6, 1), (0, 0, 3, 3), (0, 1, 2, 3),
    (0, 1, 0, 4), (1, 4, 0, 5), (0, 0, 5, 2), (1, 5, 0, 0), (1, 6, 0, 0), (1, 7, 0, 0), (0, 1, 3, 2), (0, 1, 0, 5),
    (1, 0, 0, 1), (1, 2, 0, 1), (0, 1, 3, 3), (0, 0, 1, 4), (0, 0, 6, 2), (1, 8, 0, 0), (1, 8, 0, 1), (0, 1, 4, 2),
    (1, 8, 0, 2), (0, 0, 4, 3), (0, 1, 1, 4), (1, 8, 0, 3), (0, 0, 1, 5), (1, 8, 0, 4), (0, 1, 5, 2), (1, 8, 0, 5),
    (0, 0, 2, 4), (1, 8, 0, 6), (1, 8, 0, 7), (0, 1, 4, 3), (0, 1, 6, 2), (1, 0, 0, 2), (1, 1, 0, 2), (0, 0, 2, 5),
    (0, 0, 3, 4), (0, 0, 5, 3), (1, 9, 0, 0), (0, 1, 2, 4), (0, 0, 3, 5), (0, 1, 5, 3), (1, 9, 0, 1), (1, 9, 0, 2),
    (0, 0, 6, 3), (1, 7, 0, 1), (0, 1, 3, 4), (0, 1, 1, 5), (0, 0, 4, 4), (0, 1, 6, 3), (1, 0, 1, 0), (1, 1, 1, 0),
    (1, 3, 1, 0), (1, 3, 1, 1), (1, 3, 1, 2), (1, 4, 1, 0), (0, 1, 4, 4), (1, 4, 1, 1), (1, 4, 1, 2), (1, 4, 1, 3),
    (0, 1, 2, 5), (1, 4, 1, 4), (1, 4, 1, 5), (0, 0, 5, 4), (1, 5, 1, 0), (1, 6, 1, 0), (0, 0, 4, 5), (0, 1, 5, 4),
    (2, 0, 0, 2), (0, 1, 3, 5), (0, 0, 6, 4), (1, 7, 1, 0), (2, 0, 0, 3), (0, 1, 6, 4), (1, 0, 1, 1), (1, 2, 1, 1),
    (1, 8, 1, 0), (0, 0, 5, 5), (2, 0, 0, 4), (0, 1, 4, 5), (1, 8, 1, 1), (1, 8, 1, 2), (2, 0, 0, 1), (0, 1, 5, 5),
    (1, 8, 1, 3), (1, 8, 1, 4), (1, 8, 1, 5), (1, 8, 1, 6), (1, 8, 1, 7), (0, 1, 6, 5), (0, 0, 6, 5), (1, 0, 1, 2),
    (1, 1, 1, 2), (1, 9, 1, 0), (1, 9, 1, 1), (1, 9, 1, 2), (1, 7, 1, 1), (2, 0, 0, 5),
)
BACKWARD_PLAN = (
    (1, 0, 1, 1), (1, 1, 1, 0), (1, 1, 1, 1), (1, 1, 1, 2), (1, 1, 1, 3), (0, 1, 0, 0), (1, 2, 1, 0), (1, 2, 1, 1),
    (0, 1, 1, 0), (0, 0, 0, 0), (1, 2, 1, 2), (0, 1, 2, 0), (1, 2, 1, 3), (0, 1, 0, 1), (0, 0, 1, 0), (1, 0, 1, 0),
    (0, 1, 3, 0), (1, 3, 1, 0), (1, 4, 1, 0), (1, 5, 1, 0), (0, 1, 4, 0), (0, 0, 2, 0), (1, 5, 1, 1), (0, 1, 1, 1),
    (1, 5, 1, 2), (0, 0, 3, 0), (0, 0, 4, 0), (1, 5, 1, 3), (0, 1, 2, 1), (0, 1, 5, 0), (0, 0, 5, 0), (0, 0, 0, 1),
    (1, 5, 1, 4), (1, 5, 1, 5), (0, 1, 3, 1), (1, 6, 1, 0), (0, 0, 1, 1), (0, 0, 6, 0), (0, 1, 6, 0), (2, 0, 0, 0),
    (1, 7, 1, 0), (1, 7, 1, 1), (0, 1, 0, 2), (0, 1, 4, 1), (0, 0, 2, 1), (0, 1, 1, 2), (0, 0, 3, 1), (0, 0, 4, 1),
    (1, 8, 1, 0), (1, 9, 1, 0), (0, 0, 0, 2), (0, 1, 2, 2), (0, 1, 5, 1), (0, 0, 5, 1), (3, 0, 1, 0), (0, 1, 3, 2),
    (0, 0, 1, 2), (1, 0, 0, 1), (0, 0, 6, 1), (0, 1, 6, 1), (0, 1, 4, 2), (2, 0, 0, 1), (1, 1, 0, 0), (0, 0, 2, 2),
    (1, 1, 0, 1), (1, 1, 0, 2), (1, 1, 0, 3), (0, 1, 0, 3), (0, 0, 0, 3), (0, 0, 3, 2), (0, 0, 4, 2), (0, 1, 5, 2),
    (0, 0, 5, 2), (0, 1, 1, 3), (0, 1, 2, 3), (0, 0, 1, 3), (0, 1, 6, 2), (0, 0, 6, 2), (2, 0, 0, 2), (1, 2, 0, 0),
    (1, 2, 0, 1), (0, 1, 3, 3), (1, 2, 0, 2), (1, 2, 0, 3), (0, 1, 0, 4), (0, 1, 4, 3), (1, 0, 0, 0), (0, 0, 2, 3),
    (1, 3, 0, 0), (1, 4, 0, 0), (0, 1, 1, 4), (1, 5, 0, 0), (0, 0, 0, 4), (0, 0, 3, 3), (0, 1, 5, 3), (0, 0, 4, 3),
    (1, 5, 0, 1), (1, 5, 0, 2), (0, 0, 5, 3), (0, 1, 2, 4), (3, 0, 1, 1), (0, 0, 1, 4), (1, 5, 0, 3), (1, 5, 0, 4),
    (1, 5, 0, 5), (0, 0, 6, 3), (0, 1, 3, 4), (0, 1, 6, 3), (1, 6, 0, 0), (2, 0, 0, 3), (3, 0, 1, 2), (1, 7, 0, 0),
    (1, 7, 0, 1), (0, 1, 0, 5), (0, 0, 2, 4), (0, 1, 4, 4), (0, 1, 1, 5), (0, 0, 0, 5), (0, 0, 3, 4), (0, 0, 4, 4),
    (3, 0, 1, 3), (1, 8, 0, 0), (1, 9, 0, 0), (3, 0, 0, 0), (0, 1, 2, 5), (0, 0, 5, 4), (0, 0, 1, 5), (0, 1, 3, 5),
    (3, 0, 0, 1), (0, 1, 4, 5), (0, 0, 2, 5), (0, 0, 6, 4), (3, 0, 0, 2), (0, 0, 3, 5), (0, 0, 4, 5), (0, 1, 5, 4),
    (3, 0, 1, 4), (3, 0, 0, 3), (0, 0, 5, 5), (0, 1, 5, 5), (0, 1, 6, 4), (3, 0, 0, 4), (3, 0, 1, 5), (2, 0, 0, 4),
    (0, 1, 6, 5), (0, 0, 6, 5), (2, 0, 0, 5), (3, 0, 0, 5),
)


def fast_body(nz, hidden_in, out_grad, passage_len, query_len, prefix_units, qkv_weight, attn_weight, in_weight, down_weight,
              norm_gains, bias_rows, in_bias):
    model_width = hidden_in.shape[2]
    dev_total = 8 * nz
    (gat, sgat, wq, wo, wd, sp, act, pooled, xb1, qkv, lse, ctx, n1, r1, midb, gp, hid, n2, r2) = forward_call(
        FORWARD_PLAN, nz, [passage_len, query_len, prefix_units, hidden_in, qkv_weight, attn_weight, in_weight, down_weight,
                           norm_gains, bias_rows, in_bias, *spread_tables(dev_total, model_width)])
    dx, owned, smalls = backward_call(
        BACKWARD_PLAN, nz, [passage_len, query_len, sp, out_grad, wq, wo, wd, gat, hidden_in, xb1, qkv, lse, ctx, n1, r1, midb, gp, hid, n2, r2])
    return tuple(hand_out(dev_total, act, pooled, dx, owned, smalls))


def solution(mesh):
    dp, fsdp = mesh.shape["dp"], mesh.shape["fsdp"]
    fast = dp == 4 and fsdp == 8
    return jax.shard_map(
        partial(fast_body, fsdp // 2) if fast else body,
        mesh=mesh,
        in_specs=(
            P(AX, None, None),
            P(AX, None, None),
            P(AX),
            P(AX),
            P(AX, None),
            P(None, AX, None),
            P(None, AX, None),
            P(None, AX, None),
            P(None, AX, None),
            P(None, None, AX),
            P(None, None, AX),
            P(None, AX),
        ),
        out_specs=(
            P(AX, None, None),
            P(AX, None, None, None),
            P(AX, None, None),
            P(None, AX, None),
            P(None, AX, None),
            P(None, AX, None),
            P(None, AX, None),
            P(None, None, AX),
            P(None, None, AX),
            P(None, AX),
        ),
        check_vma=False,
    )
```

```python
import functools
import math
from functools import partial

import jax
import jax.numpy as jnp
import numpy as np
from jax import lax
from jax.experimental import pallas as pl
from jax.experimental.pallas import tpu as pltpu
from jax.sharding import PartitionSpec as P

AX = ("dp", "fsdp")

HEADS = 12
HEAD_DIM = 64
LP = 512


ln_eps = 1e-12
neg_big = -1e30
prefix_step = 64


def product_t(left, right):
    return lax.dot_general(
        left, right, (((1,), (1,)), ((), ())), preferred_element_type=jnp.float32
    )


def product_n(left, right):
    return jnp.dot(left, right, preferred_element_type=jnp.float32)


def product_tn(left, right):
    return lax.dot_general(
        left, right, (((0,), (0,)), ((), ())), preferred_element_type=jnp.float32
    )


def norm_forward(values, gain_row, shift_row):
    center = values - jnp.mean(values, -1, keepdims=True)
    inverse = lax.rsqrt(jnp.mean(center * center, -1, keepdims=True) + ln_eps)
    normed = center * inverse
    return (normed * gain_row + shift_row, normed, inverse)


def norm_backward(output_gradient, normed, inverse, gain_row):
    scaled = output_gradient * gain_row
    grad_input = inverse * (
        scaled
        - jnp.mean(scaled, -1, keepdims=True)
        - normed * jnp.mean(scaled * normed, -1, keepdims=True)
    )
    return (grad_input, jnp.sum(output_gradient * normed, 0), jnp.sum(output_gradient, 0))


def column_sum(values):
    return jnp.sum(values.astype(jnp.float32), 0)


def fetch_forward(shards, depth_index):
    return (
        lax.all_gather(shards[0][depth_index], AX, axis=0, tiled=True),
        lax.all_gather(shards[1][depth_index], AX, axis=0, tiled=True),
        lax.all_gather(shards[2][depth_index], AX, axis=0, tiled=True),
        lax.all_gather(shards[3][depth_index], AX, axis=0, tiled=True),
        lax.all_gather(shards[4][depth_index], AX, axis=1, tiled=True),
        lax.all_gather(shards[5][depth_index], AX, axis=1, tiled=True),
        lax.all_gather(shards[6][depth_index], AX, axis=0, tiled=True),
    )


def fetch_backward(shards, depth_index):
    return (
        lax.all_gather(shards[0][depth_index], AX, axis=0, tiled=True),
        lax.all_gather(shards[1][depth_index], AX, axis=0, tiled=True),
        lax.all_gather(shards[2][depth_index], AX, axis=0, tiled=True),
        lax.all_gather(shards[3][depth_index], AX, axis=0, tiled=True),
        lax.all_gather(shards[4][depth_index], AX, axis=1, tiled=True),
        lax.all_gather(shards[5][depth_index], AX, axis=1, tiled=True),
        lax.all_gather(shards[6][depth_index], AX, axis=0, tiled=True),
    )


def owner_term(operands, dev_count, dev_total):
    (
        grad_qkv_low,
        inputs_low,
        grad_attn_low,
        context_low,
        grad_pre_low,
        mid_low,
        grad_down_low,
        hidden_low,
    ) = operands
    rows_here = inputs_low.shape[0]
    width = inputs_low.shape[1]

    def select_cols(values):
        per_device = values.shape[1] // dev_total
        chosen = values.reshape(rows_here, dev_total, per_device)
        return chosen.reshape(rows_here, dev_count * per_device)

    pieces = [
        product_tn(select_cols(grad_qkv_low), inputs_low),
        product_tn(select_cols(grad_attn_low), context_low),
        product_tn(select_cols(grad_pre_low), mid_low),
        product_tn(select_cols(grad_down_low), hidden_low),
    ]
    return jnp.concatenate([piece.astype(jnp.bfloat16).reshape(dev_count, -1, width) for piece in pieces], axis=1)


def split_owned(owned_rows, dev_total, model_width, hidden_width):
    qkv_rows = 3 * model_width // dev_total
    attn_rows = model_width // dev_total
    in_rows = hidden_width // dev_total
    grad_w_qkv = owned_rows[:qkv_rows]
    grad_w_attn = owned_rows[qkv_rows : qkv_rows + attn_rows]
    grad_w_in = owned_rows[qkv_rows + attn_rows : qkv_rows + attn_rows + in_rows]
    grad_w_down = owned_rows[qkv_rows + attn_rows + in_rows :].reshape(
        model_width // dev_total, hidden_width
    )
    return (grad_w_qkv, grad_w_attn, grad_w_in, grad_w_down)


def body(
    hidden_in,
    out_grad,
    passage_len,
    query_len,
    prefix_units,
    qkv_weight,
    attn_weight,
    in_weight,
    down_weight,
    norm_gains,
    bias_rows,
    in_bias,
):
    pair_count = hidden_in.shape[0]
    slot_count = hidden_in.shape[1]
    model_width = hidden_in.shape[2]
    hidden_width = in_bias.shape[1] * lax.axis_size(AX)
    dev_total = lax.axis_size(AX)
    row_count = pair_count * slot_count
    head_scale = HEAD_DIM ** (-0.5)
    position = jnp.arange(slot_count)
    in_query = position >= LP
    valid_slot = jnp.where(
        in_query[None, :],
        (position - LP)[None, :] < query_len[:, None],
        position[None, :] < passage_len[:, None],
    )
    allowed = (in_query[:, None] == in_query[None, :])[None] & valid_slot[:, None, :]

    def masked_scores(query_matrix, key_matrix):
        scores = (
            jnp.einsum("ifm,igm->ifg", query_matrix, key_matrix, preferred_element_type=jnp.float32)
            * head_scale
        )
        return jnp.where(allowed, scores, neg_big)

    def attend_head(operands):
        query_matrix, key_matrix, value_matrix = operands
        scores = masked_scores(query_matrix, key_matrix)
        row_max = jnp.max(scores, -1, keepdims=True)
        exp_terms = jnp.exp(scores - row_max)
        row_total = jnp.sum(exp_terms, -1, keepdims=True)
        attention_weights_norm = (exp_terms / row_total).astype(jnp.bfloat16)
        context = jnp.einsum(
            "exr,erl->exl", attention_weights_norm, value_matrix, preferred_element_type=jnp.float32
        )
        return (context.astype(jnp.bfloat16), (row_max + jnp.log(row_total))[..., 0])

    def attend_back(operands):
        query_matrix, key_matrix, value_matrix, context_gradient, log_totals = operands
        scores = masked_scores(query_matrix, key_matrix)
        attention_weights_norm = jnp.exp(scores - log_totals[..., None])
        grad_values = jnp.einsum(
            "cza,czj->caj",
            attention_weights_norm.astype(jnp.bfloat16),
            context_gradient,
            preferred_element_type=jnp.float32,
        )
        grad_probs = jnp.einsum(
            "ifm,igm->ifg", context_gradient, value_matrix, preferred_element_type=jnp.float32
        )
        inner_sum = jnp.sum(attention_weights_norm * grad_probs, -1, keepdims=True)
        score_gradient = (attention_weights_norm * (grad_probs - inner_sum)).astype(jnp.bfloat16)
        grad_query = (
            jnp.einsum(
                "exr,erl->exl", score_gradient, key_matrix, preferred_element_type=jnp.float32
            )
            * head_scale
        )
        grad_keys = (
            jnp.einsum(
                "cza,czj->caj", score_gradient, query_matrix, preferred_element_type=jnp.float32
            )
            * head_scale
        )
        return (
            grad_query.astype(jnp.bfloat16),
            grad_keys.astype(jnp.bfloat16),
            grad_values.astype(jnp.bfloat16),
        )

    def layer_backward(output_gradient, saved, params):
        w_qkv, w_attn, w_in, w_down, gain_rows, shift_rows, hidden_bias = params
        (
            inputs_low,
            head_stack,
            log_totals,
            context_low,
            normed_a,
            inverse_a,
            mid_low,
            hidden_pre,
            hidden_low,
            normed_b,
            inverse_b,
        ) = saved
        gain_f = gain_rows.astype(jnp.float32)
        grad_second, grad_gain_b, grad_shift_b = norm_backward(
            output_gradient, normed_b, inverse_b, gain_f[1]
        )
        grad_down_low = grad_second.astype(jnp.bfloat16)
        grad_hidden = product_n(grad_down_low, w_down)
        unused_value, gelu_back = jax.vjp(partial(jax.nn.gelu, approximate=False), hidden_pre)
        grad_pre_low = gelu_back(grad_hidden)[0].astype(jnp.bfloat16)
        middle_gradient = grad_second + product_n(grad_pre_low, w_in)
        grad_attn_sum, grad_gain_a, grad_shift_a = norm_backward(
            middle_gradient, normed_a, inverse_a, gain_f[0]
        )
        grad_attn_low = grad_attn_sum.astype(jnp.bfloat16)
        context_gradient = product_n(grad_attn_low, w_attn).astype(jnp.bfloat16)
        context_heads = context_gradient.reshape(pair_count, slot_count, HEADS, HEAD_DIM).transpose(
            2, 0, 1, 3
        )
        grads_query, grads_keys, grads_values = lax.map(
            attend_back, (head_stack[0], head_stack[1], head_stack[2], context_heads, log_totals)
        )
        grad_qkv_low = (
            jnp.stack([grads_query, grads_keys, grads_values])
            .transpose(2, 3, 0, 1, 4)
            .reshape(row_count, 3 * model_width)
        )
        grad_inputs = grad_attn_sum + product_n(grad_qkv_low, w_qkv)
        qkv_sums = column_sum(grad_qkv_low)
        grad_shift_rows = jnp.stack(
            [
                qkv_sums[:model_width],
                qkv_sums[2 * model_width :],
                column_sum(grad_attn_low),
                grad_shift_a,
                column_sum(grad_down_low),
                grad_shift_b,
            ]
        )
        grad_gain_rows = jnp.stack([grad_gain_a, grad_gain_b])
        small_terms = (grad_gain_rows, grad_shift_rows, column_sum(grad_pre_low))
        operands = (
            grad_qkv_low,
            inputs_low,
            grad_attn_low,
            context_low,
            grad_pre_low,
            mid_low,
            grad_down_low,
            hidden_low,
        )
        return (grad_inputs, small_terms, operands)

    pass_w = (
        jnp.where((~in_query)[None, :] & valid_slot, 1.0, 0.0)
        / passage_len.astype(jnp.float32)[:, None]
    )
    ques_w = (
        jnp.where(in_query[None, :] & valid_slot, 1.0, 0.0) / query_len.astype(jnp.float32)[:, None]
    )
    pool_weights = jnp.stack([pass_w, ques_w], axis=1)
    feature = jnp.arange(model_width)
    shards = (qkv_weight, attn_weight, in_weight, down_weight, norm_gains, bias_rows, in_bias)
    current = hidden_in.reshape(row_count, model_width).astype(jnp.float32)
    current_low = hidden_in.reshape(row_count, model_width)
    saved_all = []
    params_all = []
    pooled_list = []
    for depth_index in range(2):
        params = fetch_forward(shards, depth_index)
        (
            layer_w_qkv,
            layer_w_attn,
            layer_w_in,
            layer_w_down,
            layer_gain_rows,
            layer_shift_rows,
            layer_hidden_bias,
        ) = params
        layer_gain_f = layer_gain_rows.astype(jnp.float32)
        shift_f = layer_shift_rows.astype(jnp.float32)
        qkv_bias = jnp.concatenate([shift_f[0], jnp.zeros_like(shift_f[0]), shift_f[1]])
        qkv_low = (product_t(current_low, layer_w_qkv) + qkv_bias).astype(jnp.bfloat16)
        layer_head_stack = qkv_low.reshape(pair_count, slot_count, 3, HEADS, HEAD_DIM).transpose(
            2, 3, 0, 1, 4
        )
        contexts, layer_log_totals = lax.map(
            attend_head, (layer_head_stack[0], layer_head_stack[1], layer_head_stack[2])
        )
        layer_context_low = contexts.transpose(1, 2, 0, 3).reshape(row_count, model_width)
        attn_out = product_t(layer_context_low, layer_w_attn) + shift_f[2]
        depth_mid, layer_normed_a, layer_inverse_a = norm_forward(
            current + attn_out, layer_gain_f[0], shift_f[3]
        )
        layer_mid_low = depth_mid.astype(jnp.bfloat16)
        layer_hidden_pre = product_t(layer_mid_low, layer_w_in) + layer_hidden_bias.astype(
            jnp.float32
        )
        layer_hidden_low = jax.nn.gelu(layer_hidden_pre, approximate=False).astype(jnp.bfloat16)
        down_out = product_t(layer_hidden_low, layer_w_down) + shift_f[4]
        layer_out, layer_normed_b, layer_inverse_b = norm_forward(
            depth_mid + down_out, layer_gain_f[1], shift_f[5]
        )
        layer_saved = (
            current_low,
            layer_head_stack,
            layer_log_totals,
            layer_context_low,
            layer_normed_a,
            layer_inverse_a,
            layer_mid_low,
            layer_hidden_pre,
            layer_hidden_low,
            layer_normed_b,
            layer_inverse_b,
        )
        current = layer_out
        saved = layer_saved
        current_low = current.astype(jnp.bfloat16)
        saved_all.append(saved)
        params_all.append(params)
        keep_cols = (feature[None, :] < prefix_step * prefix_units[:, depth_index][:, None]).astype(
            jnp.float32
        )
        pooled_sums = jnp.einsum(
            "bct,btd->bcd",
            pool_weights,
            current.reshape(pair_count, slot_count, model_width),
            precision=lax.Precision.HIGHEST,
        )
        pooled_list.append(pooled_sums * keep_cols[:, None, :])
    activations = current_low.reshape(pair_count, slot_count, model_width)
    pooled = jnp.stack(pooled_list, axis=1)
    layer_rows = (4 * model_width + 2 * hidden_width) // dev_total
    gradient = out_grad.reshape(row_count, model_width).astype(jnp.float32)
    small_by_depth = [None, None]
    operands_by_depth = [None, None]
    matrices_by_depth = [None, None]
    for depth_index in (1, 0):
        params = fetch_backward(shards, depth_index)
        gradient, small_terms, operands = layer_backward(gradient, saved_all[depth_index], params)
        small_by_depth[depth_index] = small_terms
        operands_by_depth[depth_index] = operands

        def layer_fn(row_start, row_number, operands=operands):
            return owner_term(operands, row_number // layer_rows, dev_total).reshape(
                row_number, model_width
            )

        owned_rows = lax.psum_scatter(
            layer_fn(jnp.int32(0), lax.axis_size(AX) * layer_rows),
            AX,
            scatter_dimension=0,
            tiled=True,
        ).astype(jnp.float32)
        matrices_by_depth[depth_index] = split_owned(
            owned_rows, dev_total, model_width, hidden_width
        )
    small_stacks = [
        jnp.stack([small_by_depth[0][slot_index], small_by_depth[1][slot_index]])
        for slot_index in range(3)
    ]
    grad_gains, grad_biases, grad_in_bias = (
        lax.psum_scatter(small_stacks[0], AX, scatter_dimension=2, tiled=True),
        lax.psum_scatter(small_stacks[1], AX, scatter_dimension=2, tiled=True),
        lax.psum_scatter(small_stacks[2], AX, scatter_dimension=1, tiled=True),
    )
    matrix_out = tuple(
        (
            jnp.stack([matrices_by_depth[0][slot_index], matrices_by_depth[1][slot_index]])
            for slot_index in range(4)
        )
    )
    input_grad = gradient.astype(jnp.bfloat16).reshape(pair_count, slot_count, model_width)
    return (
        activations,
        pooled,
        input_grad,
        matrix_out[0],
        matrix_out[1],
        matrix_out[2],
        matrix_out[3],
        grad_gains,
        grad_biases,
        grad_in_bias,
    )


MESH = pl.DeviceIdType.MESH

PIECES = ((0, 16), (16, 16), (32, 32), (64, 32), (0, 32), (32, 64))
SLOT_OF = (0, 1, 2, 3, 0, 2)
LAYERS, CHUNKS, ROWS, WIDTH = 2, 3, 96, 768


class Place:
    def __init__(self, nz):
        dp, fs = lax.axis_index("dp"), lax.axis_index("fsdp")
        self.nz = nz
        self.x, self.c = dp // 2, lax.rem(dp, 2)
        self.z, self.y = fs // 2, lax.rem(fs, 2)

    def device(self, x=None, c=None, z=None, y=None):
        x = self.x if x is None else x
        c = self.c if c is None else c
        z = self.z if z is None else z
        y = self.y if y is None else y
        return (x * 2 + c, z * 2 + y)

    def over_x(self):
        return self.device(x=1 - self.x)

    def over_y(self):
        return self.device(y=1 - self.y)

    def over_c(self):
        return self.device(c=1 - self.c)

    def along_z(self, way):
        return self.device(z=self.z + (1 if way == 0 else -1))

    def has_z(self, way, steps):
        return self.z + steps < self.nz if way == 0 else self.z - steps >= 0


def entry_barrier(place):
    bar = pltpu.get_barrier_semaphore()
    for dev in (place.over_x(), place.over_y(), place.over_c()):
        pl.semaphore_signal(bar, inc=1, device_id=dev, device_id_type=MESH)
    for way in (0, 1):
        @pl.when(place.has_z(way, 1))
        def _():
            pl.semaphore_signal(bar, inc=1, device_id=place.along_z(way), device_id_type=MESH)
    pl.semaphore_wait(bar, 3 + place.has_z(0, 1).astype(jnp.int32) + place.has_z(1, 1).astype(jnp.int32))


class Gather:
    def __init__(self, place, shard, out, sz, rz, sb, rb, ps=None, pr=None):
        self.p, self.shard, self.out = place, shard, out
        self.sz, self.rz, self.sb, self.rb, self.ps, self.pr = sz, rz, sb, rb, ps, pr

    def slot(self, i, t, x, c, z, y):
        lo, n = PIECES[t]
        l, ch = i
        return self.out.at[l, ch, x, c, z, y, pl.ds(lo, n)]

    def copy(self, src, dst, s, r, dev):
        return pltpu.make_async_remote_copy(
            src_ref=src, dst_ref=dst, send_sem=s, recv_sem=r, device_id=dev, device_id_type=MESH)

    def zcopy(self, i, t, way, dist, zs):
        p = self.p
        x = slice(None) if t == 2 else p.x
        y = slice(None) if t == 3 else p.y
        ref = self.slot(i, t, x, p.c, zs, y)
        src = self.shard.at[i[0], i[1], pl.ds(*PIECES[t])] if t == 4 and dist == 1 else ref
        n = i[0] * CHUNKS + i[1]
        return self.copy(src, ref, self.sz.at[n, SLOT_OF[t], way, dist - 1], self.rz.at[n, SLOT_OF[t], way, dist - 1], p.along_z(way))

    def zsend(self, i, t, way, dist):
        p = self.p
        zs = p.z - (dist - 1) if way == 0 else p.z + (dist - 1)
        ok = p.has_z(way, 1)
        if dist > 1:
            ok = jnp.logical_and(ok, p.has_z(1 - way, dist - 1))
        return ok, lambda: self.zcopy(i, t, way, dist, zs)

    def zrecv(self, i, t, way, dist):
        p = self.p
        zs = p.z - dist if way == 0 else p.z + dist
        return p.has_z(1 - way, dist), lambda: self.zcopy(i, t, way, dist, zs)

    def zstep(self, i, t, dist, after=None):
        for way in (0, 1):
            ok, mk = self.zrecv(i, t, way, dist)

            @pl.when(ok)
            def _():
                mk().wait_recv()
            if dist + 1 < self.p.nz:
                ok2, mk2 = self.zsend(i, t, way, dist + 1)

                @pl.when(ok2)
                def _():
                    mk2().start()
            if after is not None:
                @pl.when(ok)
                def _():
                    after(self.p.z - dist if way == 0 else self.p.z + dist)

    def zfirst(self, i, t):
        for way in (0, 1):
            ok, mk = self.zsend(i, t, way, 1)

            @pl.when(ok)
            def _():
                mk().start()

    def bulk(self, i, t, axis, mine):
        p = self.p
        al = slice(None)
        n = i[0] * CHUNKS + i[1]
        if axis == "c":
            c = p.c if mine else 1 - p.c
            ref, dev, k = self.slot(i, t, al, c, al, al), p.over_c(), 2
        elif axis == "x":
            x = p.x if mine else 1 - p.x
            z = p.z if t == 2 else al
            y = al if t in (1, 3) else p.y
            ref, dev, k = self.slot(i, t, x, p.c, z, y), p.over_x(), 0
        else:
            y = p.y if mine else 1 - p.y
            z = p.z if t == 3 else al
            x = al if t in (0, 2) else p.x
            ref, dev, k = self.slot(i, t, x, p.c, z, y), p.over_y(), 1
        src = self.shard.at[i[0], i[1], pl.ds(*PIECES[t])] if t in (2, 3) else ref
        return self.copy(src, ref, self.sb.at[n, SLOT_OF[t], k], self.rb.at[n, SLOT_OF[t], k], dev)

    def part(self, i, t, nth, q, mine):
        p = self.p
        al = slice(None)
        n = i[0] * CHUNKS + i[1]
        if (t in (0, 2)) == (nth == 2):
            y = p.y if mine else 1 - p.y
            ref, dev = self.slot(i, t, al if nth == 2 else p.x, p.c, q, y), p.over_y()
        else:
            x = p.x if mine else 1 - p.x
            ref, dev = self.slot(i, t, x, p.c, q, al if nth == 2 else p.y), p.over_x()
        return self.copy(ref, ref, self.ps.at[n, t, nth - 1, q], self.pr.at[n, t, nth - 1, q], dev)

    def step(self, grp, st, i):
        if grp == "AB":
            if st == 0:
                self.zfirst(i, 4)
            elif st <= 3:
                self.zstep(i, 4, st)
                if st == 3:
                    self.bulk(i, 0, "x", True).start()
                    self.bulk(i, 1, "y", True).start()
            elif st == 4:
                self.bulk(i, 0, "x", False).wait_recv()
                self.bulk(i, 0, "y", True).start()
                self.bulk(i, 1, "y", False).wait_recv()
                self.bulk(i, 1, "x", True).start()
            elif st == 5:
                self.bulk(i, 0, "y", False).wait_recv()
                self.bulk(i, 1, "x", False).wait_recv()
                self.bulk(i, 4, "c", True).start()
            else:
                self.bulk(i, 4, "c", False).wait_recv()
            return

        def send(t):
            return lambda q: self.part(i, t, 2, q, True).start()
        for t, first in ((2, "x"), (3, "y")):
            if st == 0:
                self.bulk(i, t, first, True).start()
            elif st == 1:
                self.bulk(i, t, first, False).wait_recv()
                self.zfirst(i, t)
                send(t)(self.p.z)
            elif st <= 4:
                self.zstep(i, t, st - 1, send(t))
            elif st == 5:
                for q in range(self.p.nz):
                    self.part(i, t, 2, q, False).wait_recv()
        if st == 5:
            self.bulk(i, 5, "c", True).start()
        elif st == 6:
            self.bulk(i, 5, "c", False).wait_recv()

    def plain_step(self, st, i):
        if st == 0:
            self.zfirst(i, 0)
        elif st <= 3:
            self.zstep(i, 0, st)
            if st == 3:
                self.bulk(i, 0, "x", True).start()
        elif st == 4:
            self.bulk(i, 0, "x", False).wait_recv()
            self.bulk(i, 0, "y", True).start()
        elif st == 5:
            self.bulk(i, 0, "y", False).wait_recv()
            self.bulk(i, 0, "c", True).start()
        else:
            self.bulk(i, 0, "c", False).wait_recv()

    def finish(self, i, types=(4, 2, 3)):
        for t in types:
            if t == 4:
                for k, axis in ((0, "x"), (0, "y"), (1, "x"), (1, "y"), (4, "c"), (5, "c")):
                    self.bulk(i, k, axis, True).wait_send()
            elif t == 0:
                for axis in ("x", "y", "c"):
                    self.bulk(i, t, axis, True).wait_send()
            else:
                self.bulk(i, t, "x" if t == 2 else "y", True).wait_send()
                for q in range(self.p.nz):
                    self.part(i, t, 2, q, True).wait_send()
            for way in (0, 1):
                for dist in range(1, self.p.nz):
                    ok, mk = self.zsend(i, t, way, dist)

                    @pl.when(ok)
                    def _():
                        mk().wait_send()


F32, BF16 = jnp.float32, jnp.bfloat16
HEAD = 64
EPS = 1e-12


def nt(a, b):
    return lax.dot_general(a, b, (((1,), (1,)), ((), ())), preferred_element_type=F32)


def nn(a, b):
    return jnp.dot(a, b, preferred_element_type=F32)


def lane_is(shape, half):
    lane = lax.broadcasted_iota(jnp.int32, shape, len(shape) - 1)
    return (lane < HEAD) if half == 0 else (lane >= HEAD)


def gelu_both(x):
    e = jnp.exp(x * x * -0.5)
    k = 1.0 / (1.0 + (0.3275911 / math.sqrt(2.0)) * jnp.abs(x))
    poly = k * (0.254829592 + k * (-0.284496736 + k * (1.421413741 + k * (-1.453152027 + k * 1.061405429))))
    tail = 0.5 * poly * e
    cdf = jnp.where(x >= 0, 1.0 - tail, tail)
    return x * cdf, cdf + x * (e * (1.0 / math.sqrt(2.0 * math.pi)))


def relay_first(pk, wq, wo, width):
    def body(i, _):
        blk = pk[pl.ds(2 * i, 2)].astype(F32)
        q = jnp.concatenate([blk[0, :72], blk[1, :72]], 0).astype(BF16)
        o = jnp.concatenate([blk[0, 72:], blk[1, 72:]], 0).astype(BF16)
        wq[pl.ds(pl.multiple_of(144 * i, 16), 144), :] = q
        wo[pl.ds(pl.multiple_of(48 * i, 16), 48), :] = o
        return 0
    lax.fori_loop(0, pk.shape[0] // 2, body, 0)


def relay_down(pk, wd, width):
    def body(i, _):
        blk = pk[pl.ds(2 * i, 2)].astype(F32)
        for q in range(4):
            part = jnp.concatenate([blk[0, 24 * q:24 * q + 24], blk[1, 24 * q:24 * q + 24]], 0).astype(BF16)
            wd[pl.ds(pl.multiple_of(48 * i, 16), 48), q * width:(q + 1) * width] = part
        return 0
    lax.fori_loop(0, pk.shape[0] // 2, body, 0)


def project_qkv(xb, wq, bias, out, j, cols):
    sl = slice(j * cols, (j + 1) * cols)
    out[:, sl] = (nt(xb[...], wq[sl, :]) + bias[:, sl]).astype(BF16)


def attend_pair(qkv, key_bias, ctx, lse, i, width):
    a = 128 * i
    q2 = qkv[0:LP, a:a + 128] * jnp.asarray(0.125, BF16)
    k2 = qkv[0:LP, width + a:width + a + 128]
    v2 = qkv[0:LP, 2 * width + a:2 * width + a + 128]
    v2t = v2.T
    parts = []
    for half in (0, 1):
        qm = jnp.where(lane_is(q2.shape, half), q2, jnp.zeros_like(q2))
        s = nt(k2, qm) + key_bias[...]
        m = jnp.max(s, 0, keepdims=True)
        p = jnp.exp(s - m)
        total = jnp.sum(p, 0, keepdims=True)
        pb = (p * (1.0 / total)).astype(BF16)
        lse[2 * i + half] = m + jnp.log(total)
        parts.append(nn(v2t[HEAD * half:HEAD * half + HEAD], pb))
    ctx[0:LP, a:a + 128] = jnp.concatenate(parts, 0).T.astype(BF16)


def query_probs(qkv, query_bias, heads, width):
    rows = qkv.shape[0] - LP
    q = qkv[LP:, 0:width] * jnp.asarray(0.125, BF16)
    lane = lax.broadcasted_iota(jnp.int32, (heads, rows, width), 2)
    head = lax.broadcasted_iota(jnp.int32, (heads, rows, width), 0)
    mine = jnp.logical_and(lane >= head * HEAD, lane < head * HEAD + HEAD)
    qx = jnp.where(mine, q[None].astype(F32), 0.0).astype(BF16).reshape(heads * rows, width)
    s = nt(qx, qkv[LP:, width:2 * width]) + query_bias[...]
    m = jnp.max(s, -1, keepdims=True)
    p = jnp.exp(s - m)
    return mine, p * (1.0 / jnp.sum(p, -1, keepdims=True)), qx


def attend_query(qkv, query_bias, ctx, heads, width):
    rows = qkv.shape[0] - LP
    mine, p, _ = query_probs(qkv, query_bias, heads, width)
    c = nn(p.astype(BF16), qkv[LP:, 2 * width:]).reshape(heads, rows, width)
    ctx[LP:, :] = jnp.sum(jnp.where(mine, c, 0.0), 0).astype(BF16)


def norm_rows(x, o, bias, gain, shift, n_out, r_out, y_out, yb_out, step=32):
    def body(i, _):
        rows = pl.ds(pl.multiple_of(i * step, step), step)
        v = x[rows, :] + o[rows, :] + bias
        c = v - jnp.mean(v, -1, keepdims=True)
        r = lax.rsqrt(jnp.mean(c * c, -1, keepdims=True) + EPS)
        n = c * r
        y = n * gain + shift
        n_out[rows, :] = n
        r_out[rows, :] = jnp.broadcast_to(r, (step, 128))
        y_out[rows, :] = y
        yb_out[rows, :] = y.astype(BF16)
        return 0
    lax.fori_loop(0, x.shape[0] // step, body, 0, unroll=True)


def feed_in(midb, wi, bias, hid, gp, j, cols):
    sl = slice(j * cols, (j + 1) * cols)
    pre = nt(midb[...], wi[sl, :]) + bias[:, sl]
    a, b = gelu_both(pre)
    hid[:, sl] = a.astype(BF16)
    gp[:, sl] = b.astype(BF16)


def project_cols(a, w, out, j, cols):
    sl = slice(j * cols, (j + 1) * cols)
    out[:, sl] = nt(a[...], w[sl, :])


def pool_rows(x, weights, keep, out, depth):
    v = x[...] * weights[...]
    out[depth, 0:1, :] = jnp.sum(v[0:LP], 0, keepdims=True) * keep[depth:depth + 1, :]
    out[depth, 1:2, :] = jnp.sum(v[LP:], 0, keepdims=True) * keep[depth:depth + 1, :]


def spread_small(sg, t24, t96, m24, m96, sp, ib, width):
    dev = sg.shape[0]
    e = nn(sg[...].reshape(dev * 16, 128), t24[...]).reshape(dev, 16, width)
    full = jnp.sum(e * m24[...][:, None, :], 0)
    sp[...] = full
    per = dev // 4
    for j in range(4):
        e = nn(sg[per * j:per * j + per].reshape(per * 16, 128), t96[...]).reshape(per, 16, width)
        ib[:, j * width:(j + 1) * width] = jnp.sum(e * m96[...][:, None, :], 0)


def dead_bias(shape, axis, live):
    return jnp.where(lax.broadcasted_iota(jnp.int32, shape, axis) < live, 0.0, -1e30).astype(F32)


def pool_weights(shape, plen, qlen):
    t = lax.broadcasted_iota(jnp.int32, shape, 0)
    passage = t < LP
    live = jnp.logical_or(jnp.logical_and(passage, t < plen), jnp.logical_and(t >= LP, t < LP + qlen))
    count = jnp.where(passage, plen, qlen).astype(F32)
    return jnp.where(live, 1.0, 0.0) / count


def pack_block(r, l, ch):
    width = r.shard.shape[3]
    if ch == 0:
        r.shard[l, 0] = jnp.concatenate([r.qkv_v[l].astype(F32), r.attn_v[l].astype(F32)], 0).astype(BF16)
    elif ch == 1:
        r.shard[l, 1] = r.in_v[l]
    else:
        d = r.down_v[l].astype(F32)
        r.shard[l, 2] = jnp.concatenate([d[:, q * width:(q + 1) * width] for q in range(4)], 0).astype(BF16)


def pack_small(r):
    r.small32[...] = jnp.zeros_like(r.small32)
    own = r.gains.shape[2]
    for l in range(r.gains.shape[0]):
        r.small32[8 * l:8 * l + 2, 0:own] = r.gains[l].astype(F32)
        r.small32[8 * l + 2:8 * l + 8, 0:own] = r.biases[l].astype(F32)
        r.small32[8 * l:8 * l + 1, 32:32 + 4 * own] = r.in_bias[l:l + 1].astype(F32)
    r.small[...] = r.small32[...].astype(BF16)


VM = pltpu.VMEM


class ForwardRefs:
    def __init__(self, *refs):
        (self.plen, self.qlen, self.units, self.x, self.qkv_w, self.attn_w, self.in_w, self.down_w, self.gains, self.biases, self.in_bias,
         self.t24, self.t96, self.m24, self.m96,
         self.gat, self.sgat, self.wq_o, self.wo_o, self.wd_o, self.sp, self.act, self.pooled, self.xb1_o, self.qkv_o,
         self.lse_o, self.ctx_o, self.n1_o, self.r1_o, self.midb_o, self.gp_o, self.hid_o, self.n2_o, self.r2_o,
         self.pk, self.wq, self.wo, self.wi, self.wd, self.sgv, self.ib, self.bq, self.xf, self.xb, self.qkv, self.lse,
         self.ctx, self.o, self.mid, self.midb, self.hid, self.gp, self.n1, self.r1, self.n2, self.r2, self.sz, self.rz,
         self.sb, self.rb, self.ssz, self.srz, self.ssb, self.srb, self.ps, self.pr, self.local, self.save,
         self.shard, self.small, self.small32, self.kb, self.qb, self.pw, self.keep,
         self.qkv_v, self.attn_v, self.in_v, self.down_v, self.t24_v, self.t96_v, self.m24_v, self.m96_v, self.given) = refs


class SmallGather(Gather):
    def slot(self, i, t, x, c, z, y):
        return self.out.at[x, c, z, y]


def forward_kernel(nz, plan, s_len, width, ff, with_comm, *refs):
    r = ForwardRefs(*refs)
    place = Place(nz)
    p = place
    chunks = [(l, ch) for l in range(LAYERS) for ch in range(CHUNKS)]
    fetched = {}
    for k, (src, dst) in enumerate(((r.qkv_w, r.qkv_v), (r.attn_w, r.attn_v), (r.in_w, r.in_v), (r.down_w, r.down_v), (r.x.at[0], r.xb),
                                    (r.t24, r.t24_v), (r.t96, r.t96_v), (r.m24, r.m24_v), (r.m96, r.m96_v))):
        fetched[k] = pltpu.make_async_copy(src, dst, r.given.at[k])
        fetched[k].start()

    def given(*ks):
        for k in ks:
            if k in fetched:
                fetched.pop(k).wait()

    owned = {}

    def pack(i):
        l, ch = i
        given(*((0, 1), (2,), (3,))[ch])
        pack_block(r, l, ch)
        owned[i] = pltpu.make_async_copy(r.shard.at[l, ch], r.gat.at[l, ch, p.x, p.c, p.z, p.y], r.local.at[3 + l * CHUNKS + ch])
        owned[i].start()

    pack_small(r)
    owns = pltpu.make_async_copy(r.small, r.sgat.at[p.x, p.c, p.z, p.y], r.local.at[1])
    owns.start()
    if with_comm:
        pack(chunks[0])
    r.kb[...] = dead_bias(r.kb.shape, 0, r.plen[0])
    r.qb[...] = dead_bias(r.qb.shape, 1, r.qlen[0])
    r.pw[...] = pool_weights(r.pw.shape, r.plen[0], r.qlen[0])
    for e in range(2):
        lane = lax.broadcasted_iota(jnp.int32, (1, width), 1)
        r.keep[e:e + 1, :] = jnp.where(lane < HEAD * r.units[0, e], 1.0, 0.0).astype(F32)
    entry_barrier(place)
    g = Gather(place, r.shard, r.gat, r.sz, r.rz, r.sb, r.rb, r.ps, r.pr)
    sg = SmallGather(place, r.small, r.sgat, r.ssz, r.srz, r.ssb, r.srb)
    owns.wait()
    pend = {}
    saves = (r.wq_o, r.wo_o, r.wd_o, r.xb1_o, r.qkv_o, r.lse_o, r.ctx_o, r.n1_o, r.r1_o, r.midb_o, r.gp_o, r.hid_o, r.n2_o, r.r2_o)

    def number(out):
        return [k for k, ref in enumerate(saves) if ref is out][0]

    def save(out, ref, l):
        k = number(out)
        cp = pltpu.make_async_copy(ref, out if out is r.xb1_o else out.at[l], r.save.at[k])
        cp.start()
        pend[k] = cp

    def settle(*outs):
        for out in outs:
            cp = pend.pop(number(out), None)
            if cp is not None:
                cp.wait()

    def load(l, ch):
        src = r.gat.at[l, ch]
        dst = r.wi if ch == 1 else r.pk
        return [pltpu.make_async_copy(src, dst, r.local.at[2])]

    def row(k, l):
        return r.sp[8 * l + k:8 * l + k + 1, :]

    def tile(name, l, j):
        if name == "load":
            for cp in load(l, j):
                cp.start()
            if l == 0 and j == 0:
                cp = pltpu.make_async_copy(r.sgat, r.sgv, r.local.at[1])
                cp.start()
        elif name in ("relay", "take"):
            for cp in load(l, j):
                cp.wait()
            if j == 0:
                if l == 0:
                    pltpu.make_async_copy(r.sgat, r.sgv, r.local.at[1]).wait()
                    given(4, 5, 6, 7, 8)
                    spread_small(r.sgv.reshape(8 * nz, 16, 128), r.t24_v, r.t96_v, r.m24_v, r.m96_v, r.sp, r.ib, width)
                    r.xf[...] = r.xb[...].astype(F32)
                settle(r.wq_o, r.wo_o)
                relay_first(r.pk.reshape(8 * nz, ROWS, width), r.wq, r.wo, width)
                save(r.wq_o, r.wq, l)
                save(r.wo_o, r.wo, l)
                r.bq[:, 0:width] = row(2, l)
                r.bq[:, width:2 * width] = jnp.zeros((1, width), F32)
                r.bq[:, 2 * width:] = row(3, l)
            elif j == 2:
                settle(r.wd_o)
                relay_down(r.pk.reshape(8 * nz, ROWS, width), r.wd, width)
                save(r.wd_o, r.wd, l)
        elif name == "qkv":
            if j == 0:
                settle(r.qkv_o)
            project_qkv(r.xb, r.wq, r.bq, r.qkv, j, width)
            if j == 2:
                save(r.qkv_o, r.qkv, l)
                settle(r.lse_o, r.ctx_o)
        elif name == "attend":
            attend_pair(r.qkv, r.kb, r.ctx, r.lse, j, width)
        elif name == "query":
            attend_query(r.qkv, r.qb, r.ctx, HEADS, width)
            save(r.lse_o, r.lse, l)
            save(r.ctx_o, r.ctx, l)
        elif name == "out":
            for q in range(3):
                project_cols(r.ctx, r.wo, r.o, q, 256)
        elif name == "norm" and j == 0:
            settle(r.n1_o, r.r1_o, r.midb_o)
            norm_rows(r.xf, r.o, row(4, l), row(0, l), row(5, l), r.n1, r.r1, r.mid, r.midb)
            save(r.n1_o, r.n1, l)
            save(r.r1_o, r.r1, l)
            save(r.midb_o, r.midb, l)
            settle(r.gp_o, r.hid_o)
        elif name == "in":
            feed_in(r.midb, r.wi.reshape(ff, width), r.ib.at[8 * l:8 * l + 1], r.hid, r.gp, j, ff // 8)
            if j == 7:
                save(r.gp_o, r.gp, l)
                save(r.hid_o, r.hid, l)
        elif name == "down":
            project_cols(r.hid, r.wd, r.o, j, 256)
        elif name == "norm" and j == 1:
            settle(r.n2_o, r.r2_o)
            last = l == LAYERS - 1
            norm_rows(r.mid, r.o, row(6, l), row(1, l), row(7, l), r.n2, r.r2, r.xf, r.act if last else r.xb)
            save(r.n2_o, r.n2, l)
            save(r.r2_o, r.r2, l)
            if not last:
                save(r.xb1_o, r.xb, l)
            pool_rows(r.xf, r.pw, r.keep, r.pooled, l)

    packed = set()
    for kind, a, b, c in plan:
        if kind == 0:
            a = "AB" if a == 0 else "CD"
            if with_comm:
                i = chunks[c]
                if b == 0 and i not in packed:
                    packed.add(i)
                    if c > 0:
                        pack(i)
                if b > 0 and i in owned and (a == "CD" or b == 3):
                    owned.pop(i).wait()
                g.step(a, b, i)
                if c == 0 and a == "AB":
                    sg.plain_step(b, i)
        elif kind == 2:
            if with_comm:
                g.finish(chunks[c])
        else:
            tile(FORWARD_NAMES[a], b, c)
    given(*range(9))
    settle(*saves)
    if with_comm:
        sg.finish(chunks[0], types=(0,))


def forward_call(plan, nz, args, cid=0, with_comm=True):
    s_len, width = args[3].shape[1:]
    ff = 4 * width
    dev = 8 * nz
    n = LAYERS * CHUNKS
    any_, vm, sm = (pl.BlockSpec(memory_space=m) for m in (pl.ANY, pltpu.VMEM, pltpu.SMEM))
    sds = jax.ShapeDtypeStruct
    L = LAYERS
    outs = [
        (sds((L, CHUNKS, 2, 2, nz, 2, ROWS, width), BF16), any_), (sds((2, 2, nz, 2, 16, 128), BF16), any_),
        (sds((L, 3 * width, width), BF16), any_), (sds((L, width, width), BF16), any_), (sds((L, width, ff), BF16), any_),
        (sds((16, width), F32), vm), (sds((s_len, width), BF16), vm), (sds((2, 2, width), F32), vm),
        (sds((s_len, width), BF16), any_), (sds((L, s_len, 3 * width), BF16), any_), (sds((L, HEADS, 1, LP), F32), any_),
        (sds((L, s_len, width), BF16), any_), (sds((L, s_len, width), F32), any_), (sds((L, s_len, 128), F32), any_),
        (sds((L, s_len, width), BF16), any_), (sds((L, s_len, ff), BF16), any_), (sds((L, s_len, ff), BF16), any_),
        (sds((L, s_len, width), F32), any_), (sds((L, s_len, 128), F32), any_),
    ]
    dma = pltpu.SemaphoreType.DMA
    scratch = [
        VM((2, 2, nz, 2, ROWS, width), BF16), VM((3 * width, width), BF16), VM((width, width), BF16), VM((2, 2, nz, 2, ROWS, width), BF16), VM((width, ff), BF16),
        VM((2, 2, nz, 2, 16, 128), BF16), VM((16, ff), F32), VM((1, 3 * width), F32),
        VM((s_len, width), F32), VM((s_len, width), BF16), VM((s_len, 3 * width), BF16), VM((HEADS, 1, LP), F32),
        VM((s_len, width), BF16), VM((s_len, width), F32), VM((s_len, width), F32), VM((s_len, width), BF16),
        VM((s_len, ff), BF16), VM((s_len, ff), BF16),
        VM((s_len, width), F32), VM((s_len, 128), F32), VM((s_len, width), F32), VM((s_len, 128), F32),
        dma((n, 4, 2, nz - 1)), dma((n, 4, 2, nz - 1)), dma((n, 4, 3)), dma((n, 4, 3)),
        dma((1, 1, 2, nz - 1)), dma((1, 1, 2, nz - 1)), dma((1, 1, 3)), dma((1, 1, 3)),
        dma((n, 4, 2, nz)), dma((n, 4, 2, nz)), dma((3 + n,)), dma((14,)),
        VM((L, CHUNKS, ROWS, width), BF16), VM((16, 128), BF16), VM((16, 128), F32),
        VM((LP, 1), F32), VM((1, s_len - LP), F32), VM((s_len, 1), F32), VM((2, width), F32),
        VM(args[4].shape, BF16), VM(args[5].shape, BF16), VM(args[6].shape, BF16), VM(args[7].shape, BF16),
        VM(args[11].shape, BF16), VM(args[12].shape, BF16), VM(args[13].shape, F32), VM(args[14].shape, F32), dma((9,)),
    ]
    return pl.pallas_call(
        functools.partial(forward_kernel, nz, plan, s_len, width, ff, with_comm),
        out_shape=[o[0] for o in outs],
        in_specs=[sm] * 3 + [any_] * 5 + [vm] * 3 + [any_] * 4,
        out_specs=[o[1] for o in outs],
        scratch_shapes=scratch,
        compiler_params=pltpu.CompilerParams(collective_id=cid, has_side_effects=True, vmem_limit_bytes=60 << 20),
        name="gather_forward",
    )(*args)


BACK_CHUNKS = tuple((l, ch) for l in (1, 0) for ch in (2, 1, 0))


def fold8(v):
    return jnp.sum(v.reshape(v.shape[0] // 8, 8, v.shape[1]), 0)


def col_total(v):
    return jnp.sum(v, 0, keepdims=True)


def norm_back(sources, n_ref, r_ref, gain, d_ref, db_ref, step=32):
    width = n_ref.shape[1]

    def body(i, carry):
        s0, s1, s2 = carry
        rows = pl.ds(pl.multiple_of(i * step, step), step)
        g = sources[0][rows, :]
        for other in sources[1:]:
            g = g + other[rows, :]
        n = n_ref[rows, :]
        e = g * gain
        d = r_ref[rows, 0:1] * (e - jnp.mean(e, -1, keepdims=True) - n * jnp.mean(e * n, -1, keepdims=True))
        db = d.astype(BF16)
        d_ref[rows, :] = d
        db_ref[rows, :] = db
        return s0 + fold8(g * n), s1 + fold8(g), s2 + fold8(db.astype(F32))
    zero = jnp.zeros((8, width), F32)
    out = lax.fori_loop(0, n_ref.shape[0] // step, body, (zero, zero, zero), unroll=True)
    return [col_total(v) for v in out]


def attend_pair_back(qkv, key_bias, lse, dctx, dqkv, i, width):
    a = 128 * i
    scale = jnp.asarray(0.125, BF16)
    q2 = qkv[0:LP, a:a + 128] * scale
    k2 = qkv[0:LP, width + a:width + a + 128]
    v2 = qkv[0:LP, 2 * width + a:2 * width + a + 128]
    c2 = dctx[0:LP, a:a + 128]
    k2t = k2.T
    dqs, dks, dvs = [], [], []
    for half in (0, 1):
        mine = lane_is(q2.shape, half)
        qm = jnp.where(mine, q2, jnp.zeros_like(q2))
        cm = jnp.where(mine, c2, jnp.zeros_like(c2))
        p = jnp.exp(nt(k2, qm) + key_bias[...] - lse[2 * i + half])
        dp = nt(v2, cm)
        dvs.append(nn(p.astype(BF16), c2))
        t = p * dp
        ds = (t - p * jnp.sum(t, 0, keepdims=True)).astype(BF16)
        dks.append(nn(ds, q2))
        dqs.append(nn(k2t[HEAD * half:HEAD * half + HEAD], ds))
    first = lane_is(q2.shape, 0)
    dqkv[0:LP, a:a + 128] = (jnp.concatenate(dqs, 0).T * 0.125).astype(BF16)
    dqkv[0:LP, width + a:width + a + 128] = jnp.where(first, dks[0], dks[1]).astype(BF16)
    dqkv[0:LP, 2 * width + a:2 * width + a + 128] = jnp.where(first, dvs[0], dvs[1]).astype(BF16)


def attend_query_back(qkv, query_bias, dctx, dqkv, heads, width):
    rows = qkv.shape[0] - LP
    mine, p, qx = query_probs(qkv, query_bias, heads, width)
    k, v = qkv[LP:, width:2 * width], qkv[LP:, 2 * width:3 * width]
    cx = jnp.where(mine, dctx[LP:, :][None].astype(F32), 0.0).astype(BF16).reshape(heads * rows, width)
    dp = nt(cx, v)
    ds = (p * (dp - jnp.sum(p * dp, -1, keepdims=True)))
    dsb = ds.astype(BF16)
    dq = jnp.sum(jnp.where(mine, nn(dsb, k).reshape(heads, rows, width), 0.0), 0) * 0.125
    dqkv[LP:, 0:width] = dq.astype(BF16)
    dqkv[LP:, width:2 * width] = nn(ds.T.astype(BF16), qx).astype(BF16)
    dqkv[LP:, 2 * width:] = nn(p.T.astype(BF16), cx).astype(BF16)


class Scatter:
    def __init__(self, place, G, LC, LA, LB, L2, LZ, sends, recvs, zs, zr, fs, fr, cred, total):
        self.p, self.fs, self.fr = place, fs, fr
        self.G, self.LC, self.LA, self.LB, self.L2, self.LZ = G, LC, LA, LB, L2, LZ
        self.sends, self.recvs, self.zs, self.zr, self.cred, self.total = sends, recvs, zs, zr, cred, total
        self.waited, self.begun = set(), set()

    def copy(self, src, dst, s, r, dev):
        return pltpu.make_async_remote_copy(
            src_ref=src, dst_ref=dst, send_sem=s, recv_sem=r, device_id=dev, device_id_type=MESH)

    def credit(self, i, k):
        if i < 2 or (i, k) in self.waited:
            return
        self.waited.add((i, k))
        if k < 3:
            pl.semaphore_wait(self.cred.at[k], 1)
        else:
            @pl.when(self.p.has_z(k - 3, 1))
            def _():
                pl.semaphore_wait(self.cred.at[k], 1)

    def give_credits(self):
        p = self.p
        for k, dev in ((1, p.over_x()), (2, p.over_y())):
            pl.semaphore_signal(self.cred.at[k], inc=1, device_id=dev, device_id_type=MESH)
        for way in (0, 1):
            @pl.when(p.has_z(1 - way, 1))
            def _():
                pl.semaphore_signal(self.cred.at[3 + way], inc=1, device_id=p.along_z(1 - way), device_id_type=MESH)

    def rows(self, t):
        return pl.ds(*PIECES[t])

    def landing(self, t):
        lo, n = PIECES[t]
        return pl.ds(0 if t < 2 else 16, n)

    def core_copy(self, i, grp):
        s, p = i % 2, self.p
        rows = pl.ds(0, 32) if grp == "AB" else pl.ds(32, 64)
        k = 0 if grp == "AB" else 1
        return self.copy(self.G.at[i % 3, :, 1 - p.c, :, :, rows], self.LC.at[s, :, :, :, rows],
                         self.sends.at[i % 3, k], self.recvs.at[s, k], p.over_c())

    def first_copy(self, i, t):
        s, p = i % 2, self.p
        al = slice(None)
        if t in (0, 2):
            return self.copy(self.G.at[i % 3, :, p.c, :, 1 - p.y, self.rows(t)], self.LA.at[s, :, :, self.landing(t)],
                             self.sends.at[i % 3, 2 + t], self.recvs.at[s, 2 + t], p.over_y())
        return self.copy(self.G.at[i % 3, 1 - p.x, p.c, :, :, self.rows(t)], self.LB.at[s, :, :, self.landing(t)],
                         self.sends.at[i % 3, 2 + t], self.recvs.at[s, 2 + t], p.over_x())

    def second_copy(self, i, t):
        s, p = i % 2, self.p
        sem = (self.sends.at[i % 3, 6 + t], self.recvs.at[s, 6 + t])
        if t == 0:
            return self.copy(self.G.at[i % 3, 1 - p.x, p.c, :, p.y, self.rows(t)], self.L2.at[s, :, self.rows(t)], *sem, p.over_x())
        if t == 1:
            return self.copy(self.G.at[i % 3, p.x, p.c, :, 1 - p.y, self.rows(t)], self.L2.at[s, :, self.rows(t)], *sem, p.over_y())
        if t == 2:
            return self.copy(self.G.at[i % 3, 1 - p.x, p.c, p.z, p.y, self.rows(t)], self.L2.at[s, 0, self.rows(t)], *sem, p.over_x())
        return self.copy(self.G.at[i % 3, p.x, p.c, p.z, 1 - p.y, self.rows(t)], self.L2.at[s, 0, self.rows(t)], *sem, p.over_y())

    def plane(self, i, t, z):
        p = self.p
        if t == 2:
            return self.G.at[i % 3, :, p.c, z, p.y, self.rows(t)]
        if t == 3:
            return self.G.at[i % 3, p.x, p.c, z, :, self.rows(t)]
        return self.G.at[i % 3, p.x, p.c, z, p.y, self.rows(t)]

    def zland(self, s, t, way, k):
        if t == 4:
            return self.LZ.at[s, way, k, 0, self.rows(t)]
        return self.LZ.at[s, way, k, :, self.rows(t)]

    def zcopy(self, i, t, way, k, zt):
        s = i % 2
        return self.copy(self.plane(i, t, zt), self.zland(s, t, way, k),
                         self.zs.at[i % 3, SLOT_OF[t], way, k], self.zr.at[s, SLOT_OF[t], way, k], self.p.along_z(way))

    def ztarget(self, way, k):
        m = self.p.nz - 1 - k
        return self.p.z + m if way == 0 else self.p.z - m

    def zsend_ok(self, way, k):
        return self.p.has_z(way, self.p.nz - 1 - k)

    def zstep(self, i, t, k):
        p, s = self.p, i % 2
        for way in (0, 1):
            if k >= 1:
                ok = p.has_z(1 - way, 1)
                if k < p.nz - 1:
                    ok = jnp.logical_and(ok, p.has_z(way, p.nz - 1 - k))
                zt = self.ztarget(way, k)

                @pl.when(ok)
                def _():
                    self.zcopy(i, t, way, k - 1, zt).wait_recv()
                    ref, add = self.plane(i, t, zt), self.zland(s, t, way, k - 1)
                    ref[...] = ref[...] + add[...]
            if k <= p.nz - 2:
                self.credit(i, 3 + way)
                zt2 = self.ztarget(way, k)

                @pl.when(self.zsend_ok(way, k))
                def _():
                    self.zcopy(i, t, way, k, zt2).start()

    def step(self, grp, st, i):
        p, s = self.p, i % 2
        types = (0, 1) if grp == "AB" else (2, 3)
        if st == 0:
            self.credit(i, 0)
            self.core_copy(i, grp).start()
            return
        if st == 1:
            self.core_copy(i, grp).wait_recv()
            lo, n = (0, 32) if grp == "AB" else (32, 64)
            rows = pl.ds(lo, n)

            def add(z, _):
                for x in (0, 1):
                    for y in (0, 1):
                        self.G[i % 3, x, p.c, z, y, rows] = self.G[i % 3, x, p.c, z, y, rows] + self.LC[s, x, z, y, rows]
                return 0
            lax.fori_loop(0, p.nz, add, 0)
            self.begun.add((i, grp))
            if (i, "AB") in self.begun and (i, "CD") in self.begun and i + 2 < len(BACK_CHUNKS):
                pl.semaphore_signal(self.cred.at[0], inc=1, device_id=p.over_c(), device_id_type=MESH)
            self.credit(i, 1)
            self.credit(i, 2)
            if grp == "AB":
                for t in types:
                    self.first_copy(i, t).start()
            else:
                for k in range(p.nz - 1, -1, -1):
                    for t in types:
                        self.by_distance(k, lambda q: self.part(i, t, q).start())
            return
        if grp == "AB":
            if st == 2:
                for t in types:
                    rows, land = self.rows(t), self.landing(t)
                    self.first_copy(i, t).wait_recv()

                    def add(z, _):
                        for o in (0, 1):
                            if t == 0:
                                self.G[i % 3, o, p.c, z, p.y, rows] = self.G[i % 3, o, p.c, z, p.y, rows] + self.LA[s, o, z, land]
                            else:
                                self.G[i % 3, p.x, p.c, z, o, rows] = self.G[i % 3, p.x, p.c, z, o, rows] + self.LB[s, z, o, land]
                        return 0
                    lax.fori_loop(0, p.nz, add, 0)
                    self.second_copy(i, t).start()
                return
            if st == 3:
                for t in types:
                    self.second_copy(i, t).wait_recv()
                rows = self.rows(4)

                def add2(z, _):
                    self.G[i % 3, p.x, p.c, z, p.y, rows] = self.G[i % 3, p.x, p.c, z, p.y, rows] + self.L2[s, z, rows]
                    return 0
                lax.fori_loop(0, p.nz, add2, 0)
            self.zstep(i, 4, st - 3)
            if st == 6:
                rows = self.rows(4)
                self.total[s, rows, :] = self.G[i % 3, p.x, p.c, p.z, p.y, rows].astype(F32)
            return
        for t in types:
            rows = self.rows(t)
            if st <= 5:
                self.by_distance(p.nz - 1 - (st - 2), lambda q: self.take_first(i, t, q))
                self.zstep(i, t, st - 2)
            if st == 5:
                self.second_copy(i, t).start()
            if st == 6:
                self.second_copy(i, t).wait_recv()
                self.total[s, rows, :] = self.G[i % 3, p.x, p.c, p.z, p.y, rows].astype(F32) + self.L2[s, 0, rows].astype(F32)

    def part(self, i, t, q):
        s, p = i % 2, self.p
        rows, land = self.rows(t), self.landing(t)
        sem = (self.fs.at[i % 3, t - 2, q], self.fr.at[s, t - 2, q])
        if t == 2:
            return self.copy(self.G.at[i % 3, :, p.c, q, 1 - p.y, rows], self.LA.at[s, :, q, land], *sem, p.over_y())
        return self.copy(self.G.at[i % 3, 1 - p.x, p.c, q, :, rows], self.LB.at[s, q, :, land], *sem, p.over_x())

    def take_first(self, i, t, q):
        s, p = i % 2, self.p
        rows, land = self.rows(t), self.landing(t)
        self.part(i, t, q).wait_recv()
        for o in (0, 1):
            if t == 2:
                self.G[i % 3, o, p.c, q, p.y, rows] = self.G[i % 3, o, p.c, q, p.y, rows] + self.LA[s, o, q, land]
            else:
                self.G[i % 3, p.x, p.c, q, o, rows] = self.G[i % 3, p.x, p.c, q, o, rows] + self.LB[s, q, o, land]

    def by_distance(self, k, run):
        p = self.p
        if k == 0:
            run(p.z)
            return
        for way in (0, 1):
            @pl.when(p.has_z(way, k))
            def _():
                run(p.z + k if way == 0 else p.z - k)

    def finish(self, i):
        for grp in ("AB", "CD"):
            self.core_copy(i, grp).wait_send()
        for t in range(4):
            if t < 2:
                self.first_copy(i, t).wait_send()
            else:
                for q in range(self.p.nz):
                    self.part(i, t, q).wait_send()
            self.second_copy(i, t).wait_send()
        for t in (4, 2, 3):
            for way in (0, 1):
                for k in range(self.p.nz - 1):
                    @pl.when(self.zsend_ok(way, k))
                    def _():
                        self.zcopy(i, t, way, k, self.ztarget(way, k)).wait_send()


class SmallSum:
    def __init__(self, place, acc, land, ss, rs):
        self.p, self.acc, self.land, self.ss, self.rs = place, acc, land, ss, rs

    def partner(self, k):
        p = self.p
        if k < 3:
            return (p.over_c, p.over_y, p.over_x)[k]()
        d = 1 << (k - 3)
        return p.device(z=p.z + d - 2 * d * lax.rem(p.z // d, 2))

    def copy(self, l, k):
        return pltpu.make_async_remote_copy(
            src_ref=self.acc.at[l, k], dst_ref=self.land.at[l, k], send_sem=self.ss.at[l, k], recv_sem=self.rs.at[l, k],
            device_id=self.partner(k), device_id_type=MESH)

    def step(self, l, k):
        if k > 0:
            self.copy(l, k - 1).wait_recv()
            self.acc[l, k] = self.acc[l, k - 1] + self.land[l, k - 1]
        if k < 5:
            self.copy(l, k).start()

    def finish(self, l):
        for k in range(5):
            self.copy(l, k).wait_send()


def backward_barrier(place, far):
    bar = pltpu.get_barrier_semaphore()
    for dev in (place.over_x(), place.over_y(), place.over_c(), far):
        pl.semaphore_signal(bar, inc=1, device_id=dev, device_id_type=MESH)
    for way in (0, 1):
        @pl.when(place.has_z(way, 1))
        def _():
            pl.semaphore_signal(bar, inc=1, device_id=place.along_z(way), device_id_type=MESH)
    pl.semaphore_wait(bar, 4 + place.has_z(0, 1).astype(jnp.int32) + place.has_z(1, 1).astype(jnp.int32))


class Refs:
    def __init__(self, *refs):
        (self.plen, self.qlen, self.sp, self.og, self.wq_h, self.wo_h, self.wd_h, self.wi_h, self.xb0_h, self.xb1_h, self.qkv_h, self.lse_h,
         self.ctx_h, self.n1_h, self.r1_h, self.midb_h, self.gp_h, self.hid_h, self.n2_h, self.r2_h,
         self.dx_h, self.owned, self.smalls,
         self.G, self.LC, self.LA, self.LB, self.L2, self.LZ, self.total, self.sacc, self.sland,
         self.wd, self.wi, self.gp, self.wo, self.wq, self.g, self.da, self.db, self.n, self.r, self.low, self.lowt,
         self.x1, self.ctx, self.u1, self.dqkv, self.gattn, self.lse,
         self.kb, self.qb, self.sends, self.recvs, self.zs, self.zr, self.fs, self.fr, self.cred, self.ss, self.rs, self.sem) = refs


FETCHES = ("n2", "r2", "n1", "r1", "og", "hid", "qkv", "midb", "xb", "ctx", "wo", "wq", "lse", "out",
           "wd0", "wd1", "wi0", "wi1", "gp0", "gp1")


def backward_kernel(nz, plan, width, ff, with_comm, *refs):
    r = Refs(*refs)
    place = Place(nz)
    p = place
    sc = Scatter(place, r.G, r.LC, r.LA, r.LB, r.L2, r.LZ, r.sends, r.recvs, r.zs, r.zr, r.fs, r.fr, r.cred, r.total)
    ssum = SmallSum(place, r.sacc, r.sland, r.ss, r.rs)
    pend = {}

    def fetch(name, l):
        if l < 0:
            return
        src, dst = {
            "n2": lambda: (r.n2_h.at[l], r.n), "r2": lambda: (r.r2_h.at[l], r.r), "n1": lambda: (r.n1_h.at[l], r.n), "r1": lambda: (r.r1_h.at[l], r.r),
            "og": lambda: (r.og.at[0], r.low), "hid": lambda: (r.hid_h.at[l], r.u1), "qkv": lambda: (r.qkv_h.at[l], r.u1.at[:, 0:3 * width]),
            "midb": lambda: (r.midb_h.at[l], r.x1), "xb": lambda: (r.xb1_h if l == 1 else r.xb0_h.at[0], r.x1), "ctx": lambda: (r.ctx_h.at[l], r.ctx),
            "wo": lambda: (r.wo_h.at[l], r.wo), "wq": lambda: (r.wq_h.at[l], r.wq), "lse": lambda: (r.lse_h.at[l], r.lse),
        }[name]()
        cp = pltpu.make_async_copy(src, dst, r.sem.at[FETCHES.index(name)])
        cp.start()
        pend[name] = cp

    def fetch_tile(l, j):
        if l < 0:
            return
        s = j % 2
        cols = slice(j * width, (j + 1) * width)
        for name, src, dst in (("wd", r.wd_h.at[l, :, cols], r.wd.at[s]), ("wi", r.wi_h.at[l, 1, j // 2, j % 2], r.wi.at[s]), ("gp", r.gp_h.at[l, :, cols], r.gp.at[s])):
            key = name + str(s)
            cp = pltpu.make_async_copy(src, dst, r.sem.at[FETCHES.index(key)])
            cp.start()
            pend[key] = cp

    def need(*names):
        for name in names:
            pend.pop(name).wait()

    r.kb[...] = dead_bias((LP, 1), 0, r.plen[0])
    r.qb[...] = dead_bias(r.qb.shape, 1, r.qlen[0])
    last = LAYERS - 1
    fetch("og", last); fetch("n2", last); fetch("r2", last); fetch("hid", last)
    fetch_tile(last, 0); fetch_tile(last, 1)
    fetch("midb", last); fetch("ctx", last); fetch("wo", last); fetch("wq", last)
    if with_comm:
        backward_barrier(place, ssum.partner(4))

    def gain(k, l):
        return r.sp[8 * l + k:8 * l + k + 1, :]

    def keep(l, k, v):
        r.sacc[l, 0, k:k + 1, :] = v

    def tile(name, l, j):
        if name == "norm" and j == 1:
            if l == last:
                need("og")
                r.g[...] = r.low[...].astype(F32)
            need("n2", "r2")
            gn, gs, ds = norm_back([r.g], r.n, r.r, gain(1, l), r.da, r.low)
            keep(l, 1, gn); keep(l, 7, gs); keep(l, 6, ds)
            r.lowt[...] = r.low[...].T
            fetch("n1", l); fetch("r1", l)
            need("hid")
        elif name == "gdown":
            a, b = j // 2, j % 2
            s = BACK_CHUNKS.index((l, 2)) % 3
            h = width // 2
            res = nn(r.lowt[a * h:(a + 1) * h, :], r.u1[:, 2 * b * width:2 * (b + 1) * width])
            res = res.reshape(4 * nz, h // (4 * nz), 2 * width)
            res = jnp.concatenate([res[:, :, :width], res[:, :, width:]], 1).astype(BF16)
            n = ROWS // 2
            r.G[s, a, :, :, :, b * n:(b + 1) * n, :] = res.reshape(2, nz, 2, n, width)
            if j == 3:
                fetch("qkv", l)
        elif name == "ff":
            s = BACK_CHUNKS.index((l, 1)) % 3
            k = j % 2
            if j == 0:
                need("midb")
            need("wd" + str(k), "gp" + str(k))
            dpre = (nn(r.low[...], r.wd[k]) * r.gp[k].astype(F32)).astype(BF16)
            keep(l, 8 + j, col_total(dpre.astype(F32)))
            r.G[s, j // 2, j % 2] = nn(dpre.T, r.x1[...]).astype(BF16).reshape(nz, 2, ROWS, width)
            need("wi" + str(k))
            wi = r.wi[k].reshape(width, width)
            if j == 0:
                r.db[...] = nn(dpre, wi)
            else:
                r.db[...] = r.db[...] + nn(dpre, wi)
            if j + 2 < 4:
                fetch_tile(l, j + 2)
            else:
                fetch_tile(l - 1, j - 2)
            if j == 3:
                fetch("xb", l)
        elif name == "norm" and j == 0:
            need("n1", "r1")
            gn, gs, ds = norm_back([r.da, r.db], r.n, r.r, gain(0, l), r.da, r.low)
            keep(l, 0, gn); keep(l, 5, gs); keep(l, 4, ds)
            r.lowt[...] = r.low[...].T
            fetch("n2", l - 1); fetch("r2", l - 1)
        elif name == "gattn":
            need("ctx")
            r.gattn[...] = nn(r.lowt[...], r.ctx[...]).astype(BF16)
        elif name == "dctx":
            need("wo")
            r.ctx[...] = nn(r.low[...], r.wo[...]).astype(BF16)
            fetch("wo", l - 1)
            need("qkv")
            fetch("lse", l)
            need("lse")
        elif name == "attend":
            attend_pair_back(r.u1, r.kb, r.lse, r.ctx, r.dqkv, j, width)
        elif name == "query":
            attend_query_back(r.u1, r.qb, r.ctx, r.dqkv, HEADS, width)
            fetch("hid", l - 1); fetch("ctx", l - 1)
            keep(l, 2, col_total(r.dqkv[:, 0:width].astype(F32)))
            keep(l, 3, col_total(r.dqkv[:, 2 * width:].astype(F32)))
            need("xb")
        elif name == "gqkv":
            s = BACK_CHUNKS.index((l, 0)) % 3
            n = 3 * width // 2
            res = nn(r.dqkv[:, j * n:(j + 1) * n].T, r.x1[...]).reshape(4 * nz, n // (4 * nz), width)
            m = width // 2
            att = r.gattn[j * m:(j + 1) * m, :].astype(F32).reshape(4 * nz, m // (4 * nz), width)
            r.G[s, j] = jnp.concatenate([res, att], 1).astype(BF16).reshape(2, nz, 2, ROWS, width)
            if j == 1:
                fetch("midb", l - 1)
        elif name == "dx":
            need("wq")
            r.g[...] = r.da[...] + nn(r.dqkv[...], r.wq[...])
            fetch("wq", l - 1)
            if l == 0:
                r.low[...] = r.g[...].astype(BF16)
                cp = pltpu.make_async_copy(r.low, r.dx_h, r.sem.at[FETCHES.index("out")])
                cp.start()
                pend["out"] = cp
        elif name == "small":
            r.sacc[l, 0, 12:16, :] = jnp.zeros((4, width), F32)

    def finish(i):
        sc.finish(i)
        if i + 2 < len(BACK_CHUNKS):
            sc.give_credits()
        l, ch = BACK_CHUNKS[i]
        r.owned[l, ch] = r.total[i % 2]

    for kind, a, b, c in plan:
        if kind == 1:
            tile(BACKWARD_NAMES[a], b, c)
        elif with_comm:
            if kind == 0:
                sc.step("AB" if a == 0 else "CD", b, c)
            elif kind == 2:
                finish(c)
            elif kind == 3:
                ssum.step(b, c)
    if with_comm:
        for l in range(LAYERS):
            ssum.finish(l)
            r.smalls[l] = r.sacc[l, 5]
    need(*list(pend))


def backward_call(plan, nz, args, cid=1, with_comm=True):
    s_len, width = args[3].shape[1:]
    ff = 4 * width
    dev = 8 * nz
    any_, vm, sm = (pl.BlockSpec(memory_space=m) for m in (pl.ANY, pltpu.VMEM, pltpu.SMEM))
    sds = jax.ShapeDtypeStruct
    L = LAYERS
    outs = [(sds((s_len, width), BF16), any_), (sds((L, CHUNKS, ROWS, width), F32), vm), (sds((L, 16, width), F32), vm)]
    dma = pltpu.SemaphoreType.DMA
    scratch = [
        VM((3, 2, 2, nz, 2, ROWS, width), BF16), VM((2, 2, nz, 2, ROWS, width), BF16),
        VM((2, 2, nz, ROWS // 2, width), BF16), VM((2, nz, 2, ROWS // 2, width), BF16), VM((2, nz, ROWS, width), BF16),
        VM((2, 2, nz - 1, 2, ROWS, width), BF16), VM((2, ROWS, width), F32),
        VM((L, 6, 16, width), F32), VM((L, 5, 16, width), F32),
        VM((2, width, width), BF16), VM((2, nz, 2, ROWS, width), BF16), VM((2, s_len, width), BF16), VM((width, width), BF16), VM((3 * width, width), BF16),
        VM((s_len, width), F32), VM((s_len, width), F32), VM((s_len, width), F32), VM((s_len, width), F32), VM((s_len, 128), F32),
        VM((s_len, width), BF16), VM((width, s_len), BF16), VM((s_len, width), BF16), VM((s_len, width), BF16), VM((s_len, ff), BF16),
        VM((s_len, 3 * width), BF16), VM((width, width), BF16), VM((HEADS, 1, LP), F32),
        VM((LP, 1), F32), VM((1, s_len - LP), F32),
        dma((3, 10)), dma((2, 10)), dma((3, 4, 2, nz - 1)), dma((2, 4, 2, nz - 1)), dma((3, 2, nz)), dma((2, 2, nz)), pltpu.SemaphoreType.REGULAR((5,)),
        dma((L, 5)), dma((L, 5)), dma((len(FETCHES),)),
    ]
    return pl.pallas_call(
        functools.partial(backward_kernel, nz, plan, width, ff, with_comm),
        out_shape=[o[0] for o in outs],
        in_specs=[sm, sm, vm] + [any_] * 17,
        out_specs=[o[1] for o in outs],
        scratch_shapes=scratch,
        compiler_params=pltpu.CompilerParams(collective_id=cid if with_comm else None, has_side_effects=True, vmem_limit_bytes=64 << 20),
        name="backward_scatter",
    )(*args)


def hand_out_kernel(dev, act, pooled, dx, owned, smalls, act_o, pooled_o, dx_o, gq, ga, gi, gd, gains, biases, in_bias):
    me = lax.axis_index("dp") * (dev // 4) + lax.axis_index("fsdp")
    width = act.shape[1]
    own = width // dev
    act_o[0] = act[...]
    pooled_o[0] = pooled[...]
    dx_o[0] = dx[...]
    for l in range(LAYERS):
        gq[l] = owned[l, 0, 0:3 * own, :]
        ga[l] = owned[l, 0, 3 * own:, :]
        gi[l] = owned[l, 1]
        for q in range(4):
            gd[l, :, q * width:(q + 1) * width] = owned[l, 2, q * own:(q + 1) * own, :]
        turned = pltpu.roll(smalls[l, 0:8, :], lax.rem(width - own * me, width), 1)
        gains[l] = turned[0:2, 0:own]
        biases[l] = turned[2:8, 0:own]
        per = dev // 4
        row = smalls[l, pl.ds(8 + me // per, 1), :]
        turned = pltpu.roll(row, lax.rem(width - 4 * own * lax.rem(me, per), width), 1)
        in_bias[l:l + 1, :] = turned[:, 0:4 * own]


def hand_out(dev, act, pooled, dx, owned, smalls):
    s_len, width = act.shape
    own = width // dev
    sds = jax.ShapeDtypeStruct
    L = LAYERS
    outs = [sds((1, s_len, width), BF16), sds((1, 2, 2, width), F32), sds((1, s_len, width), BF16),
            sds((L, 3 * own, width), F32), sds((L, own, width), F32), sds((L, 4 * own, width), F32), sds((L, own, 4 * width), F32),
            sds((L, 2, own), F32), sds((L, 6, own), F32), sds((L, 4 * own), F32)]
    vm = pl.BlockSpec(memory_space=pltpu.VMEM)
    return pl.pallas_call(functools.partial(hand_out_kernel, dev), out_shape=outs, in_specs=[vm] * 5, out_specs=[vm] * len(outs),
                          compiler_params=pltpu.CompilerParams(vmem_limit_bytes=32 << 20), name="hand_out")(act, pooled, dx, owned, smalls)

F32, BF16 = jnp.float32, jnp.bfloat16
def spread_tables(dev, width):
    n = np.arange(width)
    per = width // dev
    t24 = np.zeros((128, width), np.float32); t24[n % per, n] = 1
    t96 = np.zeros((128, width), np.float32); t96[32 + n % (4 * per), n] = 1
    m24 = (n[None] // per == np.arange(dev)[:, None]).astype(np.float32)
    m96 = (n[None] // (4 * per) == np.arange(dev // 4)[:, None]).astype(np.float32)
    return jnp.asarray(t24, BF16), jnp.asarray(t96, BF16), jnp.asarray(m24), jnp.asarray(m96)


FORWARD_NAMES = ("load", "relay", "take", "qkv", "attend", "query", "out", "norm", "in", "down")
BACKWARD_NAMES = ("norm", "gdown", "ff", "gattn", "dctx", "attend", "query", "gqkv", "dx", "small")
FORWARD_PLAN = (
    (0, 0, 0, 0), (0, 0, 0, 2), (0, 1, 0, 0), (0, 1, 0, 3), (0, 0, 0, 1), (0, 0, 1, 0), (0, 1, 0, 5), (0, 1, 1, 0),
    (0, 1, 0, 1), (0, 0, 2, 0), (0, 0, 3, 0), (0, 1, 2, 0), (0, 0, 4, 0), (0, 0, 1, 2), (0, 0, 1, 1), (0, 1, 3, 0),
    (0, 0, 0, 3), (0, 0, 2, 1), (0, 1, 1, 1), (0, 1, 4, 0), (0, 0, 5, 0), (0, 0, 0, 4), (0, 0, 0, 5), (0, 0, 2, 2),
    (0, 0, 3, 1), (0, 1, 5, 0), (0, 1, 0, 2), (0, 1, 2, 1), (0, 0, 1, 3), (0, 0, 3, 2), (0, 0, 6, 0), (0, 0, 4, 1),
    (0, 1, 6, 0), (1, 0, 0, 0), (1, 1, 0, 0), (0, 1, 1, 2), (1, 3, 0, 0), (1, 3, 0, 1), (0, 1, 3, 1), (1, 3, 0, 2),
    (1, 4, 0, 0), (0, 1, 0, 4), (1, 4, 0, 1), (1, 4, 0, 2), (1, 4, 0, 3), (0, 1, 4, 1), (0, 0, 5, 1), (0, 0, 2, 3),
    (1, 4, 0, 4), (1, 4, 0, 5), (0, 0, 4, 2), (0, 1, 2, 2), (2, 0, 0, 0), (0, 1, 5, 1), (0, 0, 1, 4), (0, 1, 1, 3),
    (1, 5, 0, 0), (1, 6, 0, 0), (0, 0, 6, 1), (1, 7, 0, 0), (0, 1, 3, 2), (0, 1, 6, 1), (0, 0, 1, 5), (0, 0, 3, 3),
    (1, 0, 0, 1), (1, 2, 0, 1), (1, 8, 0, 0), (0, 1, 2, 3), (1, 8, 0, 1), (0, 0, 2, 5), (0, 1, 4, 2), (1, 8, 0, 2),
    (0, 0, 4, 3), (0, 0, 5, 2), (1, 8, 0, 3), (0, 1, 3, 3), (0, 0, 2, 4), (2, 0, 0, 1), (1, 8, 0, 4), (0, 0, 3, 5),
    (0, 1, 5, 2), (1, 8, 0, 5), (0, 1, 4, 3), (0, 1, 1, 4), (1, 8, 0, 6), (0, 0, 6, 2), (0, 0, 5, 3), (0, 1, 6, 2),
    (0, 0, 3, 4), (1, 8, 0, 7), (1, 0, 0, 2), (0, 1, 1, 5), (1, 1, 0, 2), (1, 9, 0, 0), (0, 1, 2, 4), (1, 9, 0, 1),
    (0, 1, 5, 3), (1, 9, 0, 2), (1, 7, 0, 1), (0, 0, 4, 4), (0, 0, 6, 3), (0, 0, 4, 5), (0, 1, 3, 4), (0, 1, 6, 3),
    (1, 0, 1, 0), (1, 1, 1, 0), (1, 3, 1, 0), (0, 1, 2, 5), (1, 3, 1, 1), (0, 0, 5, 4), (1, 3, 1, 2), (2, 0, 0, 3),
    (1, 4, 1, 0), (1, 4, 1, 1), (0, 1, 4, 4), (1, 4, 1, 2), (1, 4, 1, 3), (1, 4, 1, 4), (1, 4, 1, 5), (0, 0, 5, 5),
    (0, 1, 3, 5), (0, 1, 5, 4), (1, 5, 1, 0), (1, 6, 1, 0), (1, 7, 1, 0), (0, 1, 4, 5), (0, 0, 6, 4), (0, 0, 6, 5),
    (0, 1, 6, 4), (1, 0, 1, 1), (1, 2, 1, 1), (1, 8, 1, 0), (1, 8, 1, 1), (0, 1, 5, 5), (1, 8, 1, 2), (2, 0, 0, 2),
    (1, 8, 1, 3), (0, 1, 6, 5), (1, 8, 1, 4), (2, 0, 0, 5), (2, 0, 0, 4), (1, 8, 1, 5), (1, 8, 1, 6), (1, 8, 1, 7),
    (1, 0, 1, 2), (1, 1, 1, 2), (1, 9, 1, 0), (1, 9, 1, 1), (1, 9, 1, 2), (1, 7, 1, 1),
)
BACKWARD_PLAN = (
    (1, 0, 1, 1), (1, 1, 1, 0), (1, 1, 1, 1), (1, 1, 1, 2), (1, 1, 1, 3), (0, 0, 0, 0), (0, 1, 0, 0), (1, 2, 1, 0),
    (0, 0, 1, 0), (1, 2, 1, 1), (0, 1, 1, 0), (1, 2, 1, 2), (1, 2, 1, 3), (0, 1, 2, 0), (0, 0, 2, 0), (0, 1, 0, 1),
    (0, 0, 0, 1), (1, 0, 1, 0), (1, 3, 1, 0), (1, 4, 1, 0), (0, 1, 1, 1), (0, 1, 3, 0), (1, 5, 1, 0), (1, 5, 1, 1),
    (0, 0, 1, 1), (0, 0, 3, 0), (1, 5, 1, 2), (0, 1, 4, 0), (1, 5, 1, 3), (1, 5, 1, 4), (0, 0, 4, 0), (1, 5, 1, 5),
    (0, 1, 2, 1), (1, 6, 1, 0), (0, 1, 5, 0), (0, 0, 5, 0), (1, 7, 1, 0), (1, 7, 1, 1), (0, 0, 2, 1), (0, 1, 3, 1),
    (0, 1, 0, 2), (1, 8, 1, 0), (0, 1, 6, 0), (0, 0, 6, 0), (2, 0, 0, 0), (0, 0, 3, 1), (0, 1, 4, 1), (0, 1, 1, 2),
    (1, 9, 1, 0), (1, 0, 0, 1), (0, 0, 0, 2), (0, 0, 4, 1), (1, 1, 0, 0), (1, 1, 0, 1), (1, 1, 0, 2), (0, 0, 5, 1),
    (3, 0, 1, 0), (0, 1, 2, 2), (1, 1, 0, 3), (0, 1, 0, 3), (0, 1, 5, 1), (0, 0, 1, 2), (0, 0, 0, 3), (3, 0, 1, 1),
    (0, 0, 6, 1), (0, 1, 3, 2), (0, 1, 6, 1), (2, 0, 0, 1), (1, 2, 0, 0), (0, 0, 2, 2), (0, 1, 1, 3), (0, 0, 1, 3),
    (0, 1, 4, 2), (1, 2, 0, 1), (0, 0, 3, 2), (1, 2, 0, 2), (0, 0, 4, 2), (0, 1, 2, 3), (1, 2, 0, 3), (0, 0, 5, 2),
    (3, 0, 1, 2), (1, 0, 0, 0), (0, 1, 3, 3), (0, 1, 5, 2), (1, 3, 0, 0), (1, 4, 0, 0), (0, 1, 0, 4), (1, 5, 0, 0),
    (0, 0, 6, 2), (0, 1, 6, 2), (0, 0, 2, 3), (2, 0, 0, 2), (1, 5, 0, 1), (0, 1, 1, 4), (0, 1, 4, 3), (0, 0, 0, 4),
    (1, 5, 0, 2), (1, 5, 0, 3), (0, 0, 3, 3), (0, 1, 2, 4), (0, 0, 4, 3), (0, 0, 1, 4), (1, 5, 0, 4), (1, 5, 0, 5),
    (0, 1, 3, 4), (0, 1, 5, 3), (0, 0, 5, 3), (1, 6, 0, 0), (1, 7, 0, 0), (1, 7, 0, 1), (0, 1, 0, 5), (0, 0, 2, 4),
    (3, 0, 1, 3), (0, 1, 6, 3), (0, 0, 0, 5), (0, 0, 6, 3), (2, 0, 0, 3), (0, 1, 4, 4), (0, 1, 1, 5), (0, 0, 1, 5),
    (0, 0, 3, 4), (0, 0, 4, 4), (1, 8, 0, 0), (0, 1, 2, 5), (0, 1, 3, 5), (1, 9, 0, 0), (3, 0, 0, 0), (0, 1, 4, 5),
    (3, 0, 0, 1), (0, 0, 5, 4), (0, 0, 2, 5), (3, 0, 0, 2), (0, 1, 5, 4), (0, 0, 3, 5), (0, 0, 4, 5), (3, 0, 0, 3),
    (3, 0, 1, 4), (0, 1, 5, 5), (0, 0, 5, 5), (3, 0, 0, 4), (0, 1, 6, 5), (0, 0, 6, 4), (0, 1, 6, 4), (2, 0, 0, 4),
    (0, 0, 6, 5), (3, 0, 1, 5), (2, 0, 0, 5), (3, 0, 0, 5),
)


def fast_body(nz, hidden_in, out_grad, passage_len, query_len, prefix_units, qkv_weight, attn_weight, in_weight, down_weight,
              norm_gains, bias_rows, in_bias):
    model_width = hidden_in.shape[2]
    dev_total = 8 * nz
    (gat, sgat, wq, wo, wd, sp, act, pooled, xb1, qkv, lse, ctx, n1, r1, midb, gp, hid, n2, r2) = forward_call(
        FORWARD_PLAN, nz, [passage_len, query_len, prefix_units, hidden_in, qkv_weight, attn_weight, in_weight, down_weight,
                           norm_gains, bias_rows, in_bias, *spread_tables(dev_total, model_width)])
    dx, owned, smalls = backward_call(
        BACKWARD_PLAN, nz, [passage_len, query_len, sp, out_grad, wq, wo, wd, gat, hidden_in, xb1, qkv, lse, ctx, n1, r1, midb, gp, hid, n2, r2])
    return tuple(hand_out(dev_total, act, pooled, dx, owned, smalls))


def solution(mesh):
    dp, fsdp = mesh.shape["dp"], mesh.shape["fsdp"]
    fast = dp == 4 and fsdp == 8
    return jax.shard_map(
        partial(fast_body, fsdp // 2) if fast else body,
        mesh=mesh,
        in_specs=(
            P(AX, None, None),
            P(AX, None, None),
            P(AX),
            P(AX),
            P(AX, None),
            P(None, AX, None),
            P(None, AX, None),
            P(None, AX, None),
            P(None, AX, None),
            P(None, None, AX),
            P(None, None, AX),
            P(None, AX),
        ),
        out_specs=(
            P(AX, None, None),
            P(AX, None, None, None),
            P(AX, None, None),
            P(None, AX, None),
            P(None, AX, None),
            P(None, AX, None),
            P(None, AX, None),
            P(None, None, AX),
            P(None, None, AX),
            P(None, AX),
        ),
        check_vma=False,
    )
```
